512 devices in a mesh: row: 32 (over y, x, core), col: 16 (over z).
Axes of the slice: x: 4, y: 4, z: 16, core: 2. Of those that a mesh axis runs over, the one named last changes fastest.
Arguments:
- feats: bfloat16 [1024, 32768], P('col', 'row'), may hold values from -6 to 6
- w_self: bfloat16 [1024, 1024], P('col'), may hold values from -0.1875 to 0.1875
- w_neigh: bfloat16 [1024, 1024], P('col'), may hold values from -0.375 to 0.375
- cotangent: bfloat16 [1024, 32768], P('col', 'row'), may hold values from -6 to 6
- loc_nbr: int32 [32768, 8], P('row'), may hold values from 0 to 1023
- send_rows: int32 [32, 32, 128], P('row'), may hold values from 0 to 1023
- recv_node: int32 [32, 32, 128], P('row'), may hold values from -1 to 1023, as said below
- hub_rows: int32 [512], P('row'), may hold values from 0 to 1023
- hub_nbr: int32 [32768, 2], P('row'), may hold values from 0 to 511
Outputs:
- hidden_out: bfloat16 [1024, 32768], P('col', 'row')
- grad_feats: bfloat16 [1024, 32768], P('col', 'row')
- grad_self: float32 [1024, 1024], P('col')
- grad_neigh: float32 [1024, 1024], P('col')
The draws below stay inside these ranges and needn't reach their ends.
Inputs may be any that keep to these rules, and one draw needn't show every extreme that they name: `recv_node`: for receiver block d and sender block s, the first c slots hold rows of block d and the rest hold -1, with 1 <= c <= 128; in every draw one receiver block gets all 128 slots from every sender block.
All inputs are finite; a program needn't handle non-finite values.
Results may differ from the reference program's by a relative error of at most 0.0075.
Values may be sent and summed in bfloat16 or wider, within the bound.
No kernel may reach another device: no remote copies, remote signals or barrier semaphores. Data moves between devices by JAX's collectives and lax.ppermute only.
A program may use at most 64 MiB of HBM per device.

```python
import math
import jax
import jax.numpy as jnp
import numpy as np

F = 1024
NODE_DEV = 1024
SEND = 128
HUB_DEV = 16
K_LOC = 8
K_HUB = 2
NODES = 32768
HUBS = 512
N_ROW = 32


def draw_recv_node(key, part):
    key = jax.random.fold_in(key, 11)
    key_first, key_second, key_hot, key_node = jax.random.split(key, 4)
    first = jax.random.randint(key_first, (N_ROW, N_ROW), 0, SEND + 1)
    second = jax.random.randint(key_second, (N_ROW, N_ROW), 0, SEND + 1)
    counts = 1 + first * second // (SEND + 1)
    hot_block = jax.random.randint(key_hot, (), 0, N_ROW)
    receiver = jnp.arange(N_ROW)[:, None] + jnp.zeros((N_ROW, N_ROW), jnp.int32)
    counts = jnp.where(receiver == hot_block, SEND, counts)
    chosen = jax.random.randint(key_node, (N_ROW, N_ROW, SEND), 0, NODE_DEV)
    position = jnp.arange(SEND)[None, None, :]
    return jnp.where(position < counts[:, :, None], chosen, -1).astype(jnp.int32)


def plant(values, stream_key, smallest, largest):
    spot = [jax.random.randint(jax.random.fold_in(stream_key, axis), (), 0, length) for axis, length in enumerate(values.shape)]
    longest = values.shape.index(max(values.shape))
    beside = spot[:longest] + [(spot[longest] + 1) % values.shape[longest]] + spot[longest + 1:]
    return values.at[tuple(spot)].set(smallest).at[tuple(beside)].set(largest)


def steps_of(key, extent, cuts, smallest, top_value):
    factor_of = 1.0
    for dim, parts in cuts:
        steps = jax.random.uniform(jax.random.fold_in(jax.random.fold_in(key, 6), dim), (parts,), jnp.float32, smallest / len(cuts), top_value / len(cuts))
        factor_of = factor_of * jnp.repeat(jnp.exp(steps), extent[dim] // parts).reshape((-1,) + (1,) * (len(extent) - 1 - dim))
    return factor_of


def rank_table(number_of, lean):
    portions = [(1 << 20) // math.isqrt(standing ** lean) + 1 for standing in range(1, number_of + 1)]
    scale = 1 + sum(portions) // (1 << 30)
    return np.cumsum(np.array([max(1, weight // scale) for weight in portions]))


def ranked(stream_key, shape, amount, lean):
    table = rank_table(amount, lean)
    pick = jax.random.randint(jax.random.fold_in(stream_key, 1), shape, 0, int(table[amount - 1]))
    grade = jnp.searchsorted(jnp.asarray(table, jnp.int32), pick, side="right")
    return jax.random.permutation(jax.random.fold_in(stream_key, 2), amount)[grade].astype(jnp.int32)


def scatter_about(own_key, extent, width, bound, shards=(), held_as=jnp.bfloat16):
    entries = jax.random.normal(own_key, extent, jnp.float32) * width
    if len(shards) > 0:
        entries = steps_of(own_key, extent, shards, -0.22, 0.18) * entries
    return jnp.clip(entries, min=-bound, max=bound).astype(held_as)


def setup_inputs(seed: int = 0) -> dict:
    splits = jax.random.split(jax.random.key(seed), 10)
    return {
        "feats": scatter_about(splits[0], (F, NODES), 1.0, 6.0, ((0, 16), (1, 32))),
        "w_self": scatter_about(splits[1], (F, F), F ** -0.5, 0.1875, ((0, 16),)),
        "w_neigh": scatter_about(splits[2], (F, F), (F // 4) ** -0.5, 0.375, ((0, 16),)),
        "cotangent": scatter_about(splits[3], (F, NODES), 1.0, 6.0, ((0, 16), (1, 32))),
        "loc_nbr": plant(jax.random.randint(splits[4], (NODES, K_LOC), 0, NODE_DEV), jax.random.fold_in(splits[4], 1), 0, NODE_DEV - 1).astype(jnp.int32),
        "send_rows": plant(jax.random.randint(splits[5], (N_ROW, N_ROW, SEND), 0, NODE_DEV), jax.random.fold_in(splits[5], 1), 0, NODE_DEV - 1).astype(jnp.int32),
        "recv_node": draw_recv_node(jax.random.fold_in(splits[9], 71), 0),
        "hub_rows": plant(jax.random.randint(splits[7], (HUBS,), 0, NODE_DEV), jax.random.fold_in(splits[7], 1), 0, NODE_DEV - 1).astype(jnp.int32),
        "hub_nbr": plant(ranked(splits[8], (NODES, K_HUB), HUBS, 2), jax.random.fold_in(splits[8], 3), 0, HUBS - 1).astype(jnp.int32),
    }


def silu_slope(preact):
    sigmoid_part = jax.nn.sigmoid(preact)
    return sigmoid_part * (1.0 + preact * (1.0 - sigmoid_part))


def reference(feats, w_self, w_neigh, cotangent, loc_nbr, send_rows, recv_node, hub_rows, hub_nbr):
    node_rows = feats.T
    node_slopes = cotangent.T
    node_total = node_rows.shape[0]
    block_base = (jnp.arange(node_total, dtype=jnp.int32) // NODE_DEV) * NODE_DEV
    local_global = loc_nbr + block_base[:, None]
    hub_nodes = (jnp.arange(HUBS, dtype=jnp.int32) // HUB_DEV) * NODE_DEV + hub_rows
    hub_global = hub_nodes[hub_nbr]
    owners = jnp.arange(N_ROW, dtype=jnp.int32)
    source = (owners[:, None, None] * NODE_DEV + send_rows).reshape(-1)
    arriving = jnp.transpose(recv_node, (1, 0, 2))
    live_slots = arriving >= 0
    target = jnp.where(live_slots, owners[None, :, None] * NODE_DEV + arriving, node_total).reshape(-1)
    live_flat = live_slots.reshape(-1).astype(jnp.float32)

    local_sum = jnp.zeros(node_rows.shape, jnp.float32)
    for neighbour in range(K_LOC):
        local_sum = local_sum + node_rows[local_global[:, neighbour]].astype(jnp.float32)
    hub_sum = jnp.zeros(node_rows.shape, jnp.float32)
    for neighbour in range(K_HUB):
        hub_sum = hub_sum + node_rows[hub_global[:, neighbour]].astype(jnp.float32)
    remote_sum = jax.ops.segment_sum(node_rows[source].astype(jnp.float32), target, node_total + 1)[:node_total]
    arrivals = jax.ops.segment_sum(live_flat, target, node_total + 1)[:node_total]
    degree = (K_LOC + K_HUB) + arrivals
    agg = ((local_sum + hub_sum + remote_sum) / degree[:, None]).astype(jnp.bfloat16)

    preact = jnp.dot(node_rows, w_self, preferred_element_type=jnp.float32)
    preact = preact + jnp.dot(agg, w_neigh, preferred_element_type=jnp.float32)
    hidden_out = jax.nn.silu(preact).astype(jnp.bfloat16)

    slopes = (node_slopes.astype(jnp.float32) * silu_slope(preact)).astype(jnp.bfloat16)
    grad_self = jnp.dot(node_rows.T, slopes, preferred_element_type=jnp.float32)
    grad_neigh = jnp.dot(agg.T, slopes, preferred_element_type=jnp.float32)
    direct = jnp.dot(slopes, w_self.T, preferred_element_type=jnp.float32)
    back_agg = jnp.dot(slopes, w_neigh.T, preferred_element_type=jnp.float32)
    share_back = (back_agg / degree[:, None]).astype(jnp.bfloat16)
    share_wide = share_back.astype(jnp.float32)

    gathered_back = jnp.zeros(node_rows.shape, jnp.float32)
    for neighbour in range(K_LOC):
        gathered_back = gathered_back + jax.ops.segment_sum(share_wide, local_global[:, neighbour], node_total)
    for neighbour in range(K_HUB):
        gathered_back = gathered_back + jax.ops.segment_sum(share_wide, hub_global[:, neighbour], node_total)
    share_padded = jnp.concatenate([share_wide, jnp.zeros((1, share_wide.shape[1]), jnp.float32)], axis=0)
    gathered_back = gathered_back + jax.ops.segment_sum(share_padded[target], source, node_total)
    grad_feats = (direct + gathered_back).astype(jnp.bfloat16)
    return (hidden_out.T, grad_feats.T, grad_self, grad_neigh)
```

```python
import jax
import jax.numpy as jnp
from jax import lax
from jax.experimental import pallas as pl
from jax.experimental.pallas import tpu as pltpu
from jax.sharding import PartitionSpec as P

NODES = 1024
FEATS = 64
PEERS = 32
SLOTS = 128
HUBS_OWN = 16
HUBS = 512
ROWS = 80
BF16 = jnp.bfloat16
F32 = jnp.float32
NT = (((1,), (1,)), ((), ()))
NN = (((1,), (0,)), ((), ()))
MIB = 1 << 20


def params():
    return pltpu.CompilerParams(vmem_limit_bytes=48 * MIB)


def cost(flops, moved):
    return pl.CostEstimate(flops=flops, bytes_accessed=moved, transcendentals=0)


def whole(shape):
    return pl.BlockSpec(shape, lambda *_: (0,) * len(shape))


def one_hot(mask):
    return jnp.where(mask, 1.0, 0.0).astype(BF16)


def matmul(a, b, dims):
    return lax.dot_general(a, b, dims, preferred_element_type=F32)


def gather_kernel(x_ref, send_ref, hub_ref, out_ref):
    x = x_ref[...]
    node = lax.broadcasted_iota(jnp.int32, (NODES, 2 * SLOTS), 0)
    hub_node = lax.broadcasted_iota(jnp.int32, (NODES, SLOTS), 0)
    hub_feats = matmul(x, one_hot(hub_node == hub_ref[...]), NN)
    hub_rows = hub_feats.T[:HUBS_OWN, :]
    hub_block = jnp.concatenate([hub_rows, jnp.zeros_like(hub_rows)], axis=1).astype(BF16)
    for pair in range(PEERS // 2):
        picked = matmul(x, one_hot(node == send_ref[pair : pair + 1, :]), NN).astype(BF16)
        out_ref[2 * pair, :FEATS, :] = picked[:, :SLOTS]
        out_ref[2 * pair + 1, :FEATS, :] = picked[:, SLOTS:]
        out_ref[2 * pair, FEATS:, :] = hub_block
        out_ref[2 * pair + 1, FEATS:, :] = hub_block


def gather_slots(feats, send_pairs, hub_lanes):
    return pl.pallas_call(
        gather_kernel,
        out_shape=jax.ShapeDtypeStruct((PEERS, ROWS, SLOTS), BF16),
        compiler_params=params(),
        cost_estimate=cost(2 * 256 * 4096 * 1024, 1 << 20),
        name="gather_slots",
    )(feats, send_pairs, hub_lanes)


BUILD = 128


def build_kernel(loc_ref, recv_ref, hub_ref, local_ref, slot_ref, hubs_ref, degree_ref):
    first = pl.program_id(0) * BUILD
    node = lax.broadcasted_iota(jnp.int32, (BUILD, 2 * SLOTS), 0) + first
    for pair in range(PEERS // 2):
        slot_ref[:, 2 * SLOTS * pair : 2 * SLOTS * (pair + 1)] = one_hot(
            node == recv_ref[pair : pair + 1, :]
        )
    lane = lax.broadcasted_iota(jnp.int32, (BUILD, NODES), 1)
    counts = jnp.zeros((BUILD, NODES), F32)
    for k in range(loc_ref.shape[1]):
        counts = counts + jnp.where(lane == loc_ref[:, k : k + 1], 1.0, 0.0)
    local_ref[...] = counts.astype(BF16)
    hub_lane = lax.broadcasted_iota(jnp.int32, (BUILD, HUBS), 1)
    hub_counts = jnp.zeros((BUILD, HUBS), F32)
    for k in range(hub_ref.shape[1]):
        hub_counts = hub_counts + jnp.where(hub_lane == hub_ref[:, k : k + 1], 1.0, 0.0)
    hubs_ref[...] = hub_counts.astype(BF16)
    arrivals = matmul(jnp.ones((8, PEERS * SLOTS), BF16), slot_ref[...], NT)
    degree_ref[...] = arrivals + float(loc_ref.shape[1] + hub_ref.shape[1])


def build_counts(loc_nbr, recv_pairs, hub_nbr):
    return pl.pallas_call(
        build_kernel,
        grid=(NODES // BUILD,),
        in_specs=[
            pl.BlockSpec((BUILD, loc_nbr.shape[1]), lambda i: (i, 0)),
            whole((PEERS // 2, 2 * SLOTS)),
            pl.BlockSpec((BUILD, hub_nbr.shape[1]), lambda i: (i, 0)),
        ],
        out_specs=[
            pl.BlockSpec((BUILD, NODES), lambda i: (i, 0)),
            pl.BlockSpec((BUILD, PEERS * SLOTS), lambda i: (i, 0)),
            pl.BlockSpec((BUILD, HUBS), lambda i: (i, 0)),
            pl.BlockSpec((8, BUILD), lambda i: (0, i)),
        ],
        out_shape=[
            jax.ShapeDtypeStruct((NODES, NODES), BF16),
            jax.ShapeDtypeStruct((NODES, PEERS * SLOTS), BF16),
            jax.ShapeDtypeStruct((NODES, HUBS), BF16),
            jax.ShapeDtypeStruct((8, NODES), F32),
        ],
        compiler_params=params(),
        cost_estimate=cost(1 << 30, 24 << 20),
        name="build_counts",
    )(loc_nbr, recv_pairs, hub_nbr)


AGG = 256


def aggregate_kernel(x_ref, inc_ref, local_ref, slot_ref, hubs_ref, degree_ref, out_ref, slots, table):
    @pl.when(pl.program_id(0) == 0)
    def _():
        for peer in range(PEERS):
            slots[:, SLOTS * peer : SLOTS * (peer + 1)] = inc_ref[peer, :FEATS, :]
        rows = inc_ref[:, FEATS:, :].astype(F32).reshape(HUBS, SLOTS)
        table[...] = rows.T[:FEATS, :].astype(BF16)

    total = (
        matmul(x_ref[...], local_ref[...], NT)
        + matmul(slots[...], slot_ref[...], NT)
        + matmul(table[...], hubs_ref[...], NT)
    )
    out_ref[...] = (total / degree_ref[0:1, :]).astype(BF16)


def aggregate(feats, incoming, local, slot, hubs, degree):
    return pl.pallas_call(
        aggregate_kernel,
        grid=(NODES // AGG,),
        in_specs=[
            whole((FEATS, NODES)),
            whole((PEERS, ROWS, SLOTS)),
            pl.BlockSpec((AGG, NODES), lambda i: (i, 0)),
            pl.BlockSpec((AGG, PEERS * SLOTS), lambda i: (i, 0)),
            pl.BlockSpec((AGG, HUBS), lambda i: (i, 0)),
            pl.BlockSpec((8, AGG), lambda i: (0, i)),
        ],
        out_specs=pl.BlockSpec((FEATS, AGG), lambda i: (0, i)),
        out_shape=jax.ShapeDtypeStruct((FEATS, NODES), BF16),
        scratch_shapes=[pltpu.VMEM((FEATS, PEERS * SLOTS), BF16), pltpu.VMEM((FEATS, HUBS), BF16)],
        compiler_params=params(),
        cost_estimate=cost(2 * 256 * 5632 * 1024, 12 << 20),
        name="aggregate",
    )(feats, incoming, local, slot, hubs, degree)


def return_kernel(share_ref, slot_ref, hubs_ref, out_ref):
    share = share_ref[...]
    values = matmul(share, slot_ref[...], NN).astype(BF16)
    for peer in range(8):
        out_ref[peer, :FEATS, :] = values[:, SLOTS * peer : SLOTS * (peer + 1)]
    terms = matmul(share, hubs_ref[...], NN).T
    high = terms.astype(BF16)
    low = (terms - high.astype(F32)).astype(BF16)
    both = jnp.concatenate([high.astype(F32), low.astype(F32)], axis=1)
    out_ref[:, FEATS:, :] = both.reshape(8, HUBS_OWN, SLOTS).astype(BF16)


def return_slots(share, slot, hubs):
    return pl.pallas_call(
        return_kernel,
        grid=(PEERS // 8,),
        in_specs=[
            whole((FEATS, NODES)),
            pl.BlockSpec((NODES, 8 * SLOTS), lambda i: (0, i)),
            pl.BlockSpec((NODES, 8 * HUBS_OWN), lambda i: (0, i)),
        ],
        out_specs=pl.BlockSpec((8, ROWS, SLOTS), lambda i: (i, 0, 0)),
        out_shape=jax.ShapeDtypeStruct((PEERS, ROWS, SLOTS), BF16),
        compiler_params=params(),
        cost_estimate=cost(2 * 256 * 4608 * 1024, 10 << 20),
        name="return_slots",
    )(share, slot, hubs)


SPREAD = 256


def spread_kernel(back_ref, send_ref, hub_ref, base_ref, out_ref, slots, hub_total):
    @pl.when(pl.program_id(0) == 0)
    def _():
        for peer in range(PEERS):
            slots[:, SLOTS * peer : SLOTS * (peer + 1)] = back_ref[peer, :FEATS, :]
        sums = jnp.sum(back_ref[:, FEATS:, :].astype(F32), axis=0)
        total = sums[:, :FEATS] + sums[:, FEATS:]
        high = total.astype(BF16).astype(F32)
        stacked = jnp.concatenate(
            [high, total - high, jnp.zeros((SLOTS - 2 * HUBS_OWN, FEATS), F32)], axis=0
        )
        hub_total[...] = stacked.T.astype(BF16)

    first = pl.program_id(0) * SPREAD
    node = lax.broadcasted_iota(jnp.int32, (SPREAD, 2 * SLOTS), 0) + first
    grad = base_ref[...]
    for pair in range(PEERS // 2):
        grad = grad + matmul(
            slots[:, 2 * SLOTS * pair : 2 * SLOTS * (pair + 1)],
            one_hot(node == send_ref[pair : pair + 1, :]),
            NT,
        )
    hub_node = lax.broadcasted_iota(jnp.int32, (SPREAD, SLOTS), 0) + first
    grad = grad + matmul(hub_total[...], one_hot(hub_node == hub_ref[...]), NT)
    out_ref[...] = grad.astype(BF16)


def spread_grads(returned, send_pairs, hub_lanes, base):
    return pl.pallas_call(
        spread_kernel,
        grid=(NODES // SPREAD,),
        in_specs=[
            whole((PEERS, ROWS, SLOTS)),
            whole((PEERS // 2, 2 * SLOTS)),
            whole((1, SLOTS)),
            pl.BlockSpec((FEATS, SPREAD), lambda i: (0, i)),
        ],
        out_specs=pl.BlockSpec((FEATS, SPREAD), lambda i: (0, i)),
        out_shape=jax.ShapeDtypeStruct((FEATS, NODES), BF16),
        scratch_shapes=[pltpu.VMEM((FEATS, PEERS * SLOTS), BF16), pltpu.VMEM((FEATS, SLOTS), BF16)],
        compiler_params=params(),
        cost_estimate=cost(2 * 256 * 4224 * 1024, 2 << 20),
        name="spread_grads",
    )(returned, send_pairs, hub_lanes, base)


def silu_slope(preact):
    sigmoid_part = jax.nn.sigmoid(preact)
    return sigmoid_part * (1.0 + preact * (1.0 - sigmoid_part))


def per_device(feats, w_self, w_neigh, cotangent, loc_nbr, send_rows, recv_node, hub_rows, hub_nbr):
    send_pairs = send_rows.reshape(PEERS // 2, 2 * SLOTS)
    recv_pairs = recv_node.reshape(PEERS // 2, 2 * SLOTS)
    hub_lanes = jnp.concatenate(
        [hub_rows, hub_rows, jnp.full((SLOTS - 2 * HUBS_OWN,), -1, jnp.int32)]
    )[None, :]
    outgoing = gather_slots(feats, send_pairs, hub_lanes)
    incoming = lax.all_to_all(outgoing, "row", 0, 0, tiled=True)
    local, slot, hubs, degree = build_counts(loc_nbr, recv_pairs, hub_nbr)
    agg = aggregate(feats, incoming, local, slot, hubs, degree)
    joined = jnp.concatenate([feats, agg], axis=0)
    weights = jnp.concatenate([w_self, w_neigh], axis=0)
    partial_product = lax.dot_general(
        weights, joined, (((0,), (0,)), ((), ())), preferred_element_type=F32
    )
    preact = lax.psum_scatter(partial_product, "col", scatter_dimension=0, tiled=True)
    hidden_out = jax.nn.silu(preact).astype(BF16)
    slopes = (cotangent.astype(F32) * silu_slope(preact)).astype(BF16)
    block_rows = lax.all_gather(slopes, "col", axis=0, tiled=True)
    back_sum = matmul(weights, block_rows, NN)
    share = (back_sum[FEATS:] / degree[0:1, :]).astype(BF16)
    returned = lax.all_to_all(return_slots(share, slot, hubs), "row", 0, 0, tiled=True)
    weight_part = matmul(joined, block_rows, NT)
    pieces = weight_part.reshape(16, 8, 2, 512).transpose(0, 2, 1, 3).reshape(PEERS, 8, 512)
    pieces = lax.all_to_all(pieces, "row", 0, 0, tiled=True)
    piece = jnp.sum(pieces, axis=0, keepdims=True)
    pieces = lax.all_to_all(jnp.broadcast_to(piece, pieces.shape), "row", 0, 0, tiled=True)
    weight_total = pieces.reshape(16, 2, 8, 512).transpose(0, 2, 1, 3).reshape(2 * FEATS, 1024)
    base = back_sum[:FEATS] + matmul(share, local, NN)
    grad_feats = spread_grads(returned, send_pairs, hub_lanes, base)
    return (hidden_out, grad_feats, weight_total[:FEATS], weight_total[FEATS:])


def solution(mesh):
    return jax.shard_map(
        per_device,
        mesh=mesh,
        in_specs=(
            P("col", "row"),
            P("col", None),
            P("col", None),
            P("col", "row"),
            P("row", None),
            P("row", None, None),
            P("row", None, None),
            P("row"),
            P("row", None),
        ),
        out_specs=(P("col", "row"), P("col", "row"), P("col", None), P("col", None)),
        check_vma=False,
    )
```

```python
import jax
import jax.numpy as jnp
from jax import lax
from jax.experimental import pallas as pl
from jax.experimental.pallas import tpu as pltpu
from jax.sharding import PartitionSpec as P

NODES = 1024
FEATS = 64
PEERS = 32
SLOTS = 128
HUBS_OWN = 16
HUBS = 512
ROWS = 80
LAYERS = 16
OWN = 64
OUTS = 1024
BF16 = jnp.bfloat16
F32 = jnp.float32
NT = (((1,), (1,)), ((), ()))
NN = (((1,), (0,)), ((), ()))
MIB = 1 << 20


def params():
    return pltpu.CompilerParams(vmem_limit_bytes=48 * MIB)


def cost(flops, moved):
    return pl.CostEstimate(flops=flops, bytes_accessed=moved, transcendentals=0)


def whole(shape):
    return pl.BlockSpec(shape, lambda *_: (0,) * len(shape))


def one_hot(mask):
    return jnp.where(mask, 1.0, 0.0).astype(BF16)


def matmul(a, b, dims):
    return lax.dot_general(a, b, dims, preferred_element_type=F32)


def pair_lanes(ref, pair):
    return jnp.concatenate([ref[2 * pair : 2 * pair + 1, :], ref[2 * pair + 1 : 2 * pair + 2, :]], axis=1)


def gather_kernel(x_ref, send_ref, hub_ref, out_ref):
    x = x_ref[...]
    node = lax.broadcasted_iota(jnp.int32, (NODES, 2 * SLOTS), 0)
    hub_node = lax.broadcasted_iota(jnp.int32, (NODES, HUBS_OWN), 0)
    hub_feats = matmul(x, one_hot(hub_node == hub_ref[...]), NN)
    hub_rows = hub_feats.T
    hub_block = jnp.concatenate([hub_rows, jnp.zeros_like(hub_rows)], axis=1).astype(BF16)
    for pair in range(PEERS // 2):
        picked = matmul(x, one_hot(node == pair_lanes(send_ref, pair)), NN).astype(BF16)
        out_ref[2 * pair, :FEATS, :] = picked[:, :SLOTS]
        out_ref[2 * pair + 1, :FEATS, :] = picked[:, SLOTS:]
        out_ref[2 * pair, FEATS:, :] = hub_block
        out_ref[2 * pair + 1, FEATS:, :] = hub_block


def gather_slots(feats, send_lanes, hub_own):
    return pl.pallas_call(
        gather_kernel,
        out_shape=jax.ShapeDtypeStruct((PEERS, ROWS, SLOTS), BF16),
        compiler_params=params(),
        cost_estimate=cost(2 * 256 * 4096 * 1024, 1 << 20),
        name="gather_slots",
    )(feats, send_lanes, hub_own)


BUILD = 128


def build_kernel(loc_ref, recv_ref, hub_ref, local_ref, slot_ref, hubs_ref, degree_ref):
    first = pl.program_id(0) * BUILD
    node = lax.broadcasted_iota(jnp.int32, (BUILD, 2 * SLOTS), 0) + first
    for pair in range(PEERS // 2):
        slot_ref[:, 2 * SLOTS * pair : 2 * SLOTS * (pair + 1)] = one_hot(
            node == pair_lanes(recv_ref, pair)
        )
    lane = lax.broadcasted_iota(jnp.int32, (BUILD, NODES), 1)
    counts = jnp.zeros((BUILD, NODES), F32)
    for k in range(loc_ref.shape[1]):
        counts = counts + jnp.where(lane == loc_ref[:, k : k + 1], 1.0, 0.0)
    local_ref[...] = counts.astype(BF16)
    hub_lane = lax.broadcasted_iota(jnp.int32, (BUILD, HUBS), 1)
    hub_counts = jnp.zeros((BUILD, HUBS), F32)
    for k in range(hub_ref.shape[1]):
        hub_counts = hub_counts + jnp.where(hub_lane == hub_ref[:, k : k + 1], 1.0, 0.0)
    hubs_ref[...] = hub_counts.astype(BF16)
    arrivals = matmul(jnp.ones((8, PEERS * SLOTS), BF16), slot_ref[...], NT)
    degree_ref[...] = arrivals + float(loc_ref.shape[1] + hub_ref.shape[1])


def build_counts(loc_nbr, recv_lanes, hub_nbr):
    return pl.pallas_call(
        build_kernel,
        grid=(NODES // BUILD,),
        in_specs=[
            pl.BlockSpec((BUILD, loc_nbr.shape[1]), lambda i: (i, 0)),
            whole((PEERS, SLOTS)),
            pl.BlockSpec((BUILD, hub_nbr.shape[1]), lambda i: (i, 0)),
        ],
        out_specs=[
            pl.BlockSpec((BUILD, NODES), lambda i: (i, 0)),
            pl.BlockSpec((BUILD, PEERS * SLOTS), lambda i: (i, 0)),
            pl.BlockSpec((BUILD, HUBS), lambda i: (i, 0)),
            pl.BlockSpec((8, BUILD), lambda i: (0, i)),
        ],
        out_shape=[
            jax.ShapeDtypeStruct((NODES, NODES), BF16),
            jax.ShapeDtypeStruct((NODES, PEERS * SLOTS), BF16),
            jax.ShapeDtypeStruct((NODES, HUBS), BF16),
            jax.ShapeDtypeStruct((8, NODES), F32),
        ],
        compiler_params=params(),
        cost_estimate=cost(1 << 30, 24 << 20),
        name="build_counts",
    )(loc_nbr, recv_lanes, hub_nbr)


AGG = 256


def fold_halves(block):
    return jnp.concatenate([block[: OWN // 2, :], block[OWN // 2 :, :]], axis=1)


def aggregate_kernel(
    x_ref, inc_ref, local_ref, slot_ref, hubs_ref, degree_ref, x_tile_ref, cot_ref, out_ref, slots, table
):
    @pl.when(pl.program_id(0) == 0)
    def _():
        for peer in range(PEERS):
            slots[:, SLOTS * peer : SLOTS * (peer + 1)] = inc_ref[peer, :FEATS, :]
        rows = inc_ref[:, FEATS:, :].astype(F32).reshape(HUBS, SLOTS)
        table[...] = rows.T[:FEATS, :].astype(BF16)

    total = (
        matmul(x_ref[...], local_ref[...], NT)
        + matmul(slots[...], slot_ref[...], NT)
        + matmul(table[...], hubs_ref[...], NT)
    )
    mean = (total / degree_ref[0:1, :]).T
    nodes = jnp.concatenate([x_tile_ref[...].astype(F32).T, mean], axis=1).astype(BF16)
    slopes = cot_ref[...].astype(F32).T
    for layer in range(AGG // OWN):
        out_ref[layer, :OWN, :] = nodes[OWN * layer : OWN * (layer + 1), :]
        out_ref[layer, OWN:, :] = fold_halves(slopes[OWN * layer : OWN * (layer + 1), :]).astype(BF16)


def aggregate(feats, incoming, local, slot, hubs, degree, cotangent):
    return pl.pallas_call(
        aggregate_kernel,
        grid=(NODES // AGG,),
        in_specs=[
            whole((FEATS, NODES)),
            whole((PEERS, ROWS, SLOTS)),
            pl.BlockSpec((AGG, NODES), lambda i: (i, 0)),
            pl.BlockSpec((AGG, PEERS * SLOTS), lambda i: (i, 0)),
            pl.BlockSpec((AGG, HUBS), lambda i: (i, 0)),
            pl.BlockSpec((8, AGG), lambda i: (0, i)),
            pl.BlockSpec((FEATS, AGG), lambda i: (0, i)),
            pl.BlockSpec((FEATS, AGG), lambda i: (0, i)),
        ],
        out_specs=pl.BlockSpec((AGG // OWN, 96, SLOTS), lambda i: (i, 0, 0)),
        out_shape=jax.ShapeDtypeStruct((LAYERS, 96, SLOTS), BF16),
        scratch_shapes=[pltpu.VMEM((FEATS, PEERS * SLOTS), BF16), pltpu.VMEM((FEATS, HUBS), BF16)],
        compiler_params=params(),
        cost_estimate=cost(2 * 256 * 5632 * 1024, 12 << 20),
        name="aggregate",
    )(feats, incoming, local, slot, hubs, degree, feats, cotangent)


PIECE = 16
TILE = 256


def regroup_kernel(inc_ref, out_ref):
    group = lax.broadcasted_iota(jnp.int32, (OWN, SLOTS), 1) // PIECE
    for half in range(2):
        blocks = [inc_ref[8 * half + i, :OWN, :].astype(F32) for i in range(8)]
        for slice_of in range(8):
            tile = jnp.zeros((OWN, SLOTS), F32)
            for i in range(8):
                moved = blocks[i]
                if i != slice_of:
                    moved = pltpu.roll(moved, (PIECE * (i - slice_of)) % SLOTS, 1)
                tile = jnp.where(group == i, moved, tile)
            tile = tile.astype(BF16)
            for outs in range(4):
                out_ref[4 * slice_of + outs, :, SLOTS * half : SLOTS * (half + 1)] = tile


def regroup(node_block):
    return pl.pallas_call(
        regroup_kernel,
        out_shape=jax.ShapeDtypeStruct((PEERS, OWN, TILE), BF16),
        compiler_params=params(),
        cost_estimate=cost(1 << 24, 2 << 20),
        name="regroup",
    )(node_block)


def forward_kernel(inc_ref, weights_ref, slopes_ref, hidden_ref, flat_ref):
    joined = jnp.concatenate([inc_ref[layer, :OWN, :] for layer in range(LAYERS)], axis=1)
    preact = matmul(joined, weights_ref[...], NN)
    sigmoid_part = jax.nn.sigmoid(preact)
    hidden = preact * sigmoid_part
    slope = sigmoid_part * (1.0 + preact * (1.0 - sigmoid_part))
    half = OWN // 2
    for pair in range(LAYERS // 2):
        even = inc_ref[2 * pair, OWN:, :].astype(F32)
        odd = inc_ref[2 * pair + 1, OWN:, :].astype(F32)
        top = jnp.concatenate([even[:, :FEATS], odd[:, :FEATS]], axis=1)
        bottom = jnp.concatenate([even[:, FEATS:], odd[:, FEATS:]], axis=1)
        lanes = slice(SLOTS * pair, SLOTS * (pair + 1))
        slopes = (jnp.concatenate([top, bottom], axis=0) * slope[:, lanes]).astype(BF16)
        flat_ref[:, lanes] = slopes
        for slice_of in range(8):
            column = SLOTS * (pair % 2)
            slopes_ref[4 * slice_of + pair // 2, :, column : column + SLOTS] = slopes
        tile = hidden[:, lanes]
        hidden_ref[2 * pair] = fold_halves(tile[:, :FEATS]).astype(BF16)
        hidden_ref[2 * pair + 1] = fold_halves(tile[:, FEATS:]).astype(BF16)


def forward(node_block, weights):
    return pl.pallas_call(
        forward_kernel,
        out_shape=[
            jax.ShapeDtypeStruct((PEERS, OWN, TILE), BF16),
            jax.ShapeDtypeStruct((LAYERS, OWN // 2, SLOTS), BF16),
            jax.ShapeDtypeStruct((OWN, OUTS), BF16),
        ],
        compiler_params=params(),
        cost_estimate=cost(2 * 256 * 2048 * 1024, 6 << 20),
        name="forward",
    )(node_block, weights)


def backward_kernel(slopes_ref, weights_ref, degree_ref, out_ref):
    back = matmul(slopes_ref[...], weights_ref[...], NT)
    direct = lax.broadcasted_iota(jnp.int32, (OWN, SLOTS), 1) < FEATS
    divisor = jnp.where(direct, 1.0, degree_ref[...])
    for layer in range(LAYERS):
        out_ref[layer] = (back[:, SLOTS * layer : SLOTS * (layer + 1)] / divisor).astype(BF16)


def backward(slopes, weights, own_degree):
    return pl.pallas_call(
        backward_kernel,
        out_shape=jax.ShapeDtypeStruct((LAYERS, OWN, SLOTS), BF16),
        compiler_params=params(),
        cost_estimate=cost(2 * 256 * 2048 * 1024, 6 << 20),
        name="backward",
    )(slopes, weights, own_degree)


def weight_kernel(joined_ref, slopes_ref, back_ref, hidden_ref, out_ref):
    part = matmul(joined_ref[...], slopes_ref[...], NN).astype(BF16)
    for layer in range(LAYERS):
        out_ref[layer, :OWN, :] = back_ref[layer]
        out_ref[layer, OWN:96, :] = hidden_ref[layer]
        out_ref[layer, 96:112, :] = part[PIECE * layer : PIECE * (layer + 1), :SLOTS]
        out_ref[layer, 112:, :] = part[PIECE * layer : PIECE * (layer + 1), SLOTS:]


def weight_parts(joined_cols, slopes_rows, back, hidden):
    return pl.pallas_call(
        weight_kernel,
        out_shape=jax.ShapeDtypeStruct((LAYERS, SLOTS, SLOTS), BF16),
        compiler_params=params(),
        cost_estimate=cost(2 * 256 * 2048 * 256, 3 << 20),
        name="weight_parts",
    )(joined_cols, slopes_rows, back, hidden)


RETURN_ROWS = 112


def return_kernel(back_ref, slot_ref, hubs_ref, out_ref, share, sums):
    @pl.when(pl.program_id(0) == 0)
    def _():
        rows = back_ref[:, :OWN, :].astype(F32).reshape(NODES, SLOTS)
        share[...] = rows.T[FEATS:, :].astype(BF16)
        sums[...] = jnp.sum(back_ref[:, 96:, :].astype(F32), axis=0).astype(BF16)

    values = matmul(share[...], slot_ref[...], NN).astype(BF16)
    for peer in range(8):
        out_ref[peer, :FEATS, :] = values[:, SLOTS * peer : SLOTS * (peer + 1)]
        out_ref[peer, ROWS:, :] = sums[...]
    terms = matmul(share[...], hubs_ref[...], NN).T
    high = terms.astype(BF16).astype(F32)
    both = jnp.concatenate([high, terms - high], axis=1)
    out_ref[:, FEATS:ROWS, :] = both.reshape(8, HUBS_OWN, SLOTS).astype(BF16)


def return_slots(back_block, slot, hubs):
    return pl.pallas_call(
        return_kernel,
        grid=(PEERS // 8,),
        in_specs=[
            whole((LAYERS, SLOTS, SLOTS)),
            pl.BlockSpec((NODES, 8 * SLOTS), lambda i: (0, i)),
            pl.BlockSpec((NODES, 8 * HUBS_OWN), lambda i: (0, i)),
        ],
        out_specs=pl.BlockSpec((8, RETURN_ROWS, SLOTS), lambda i: (i, 0, 0)),
        out_shape=jax.ShapeDtypeStruct((PEERS, RETURN_ROWS, SLOTS), BF16),
        scratch_shapes=[pltpu.VMEM((FEATS, NODES), BF16), pltpu.VMEM((32, SLOTS), BF16)],
        compiler_params=params(),
        cost_estimate=cost(2 * 256 * 4608 * 1024, 10 << 20),
        name="return_slots",
    )(back_block, slot, hubs)


def local_kernel(back_ref, local_ref, base_ref, hidden_ref):
    columns = back_ref[:, :OWN, :].astype(F32).reshape(NODES, SLOTS).T
    share = columns[FEATS:, :].astype(BF16)
    base_ref[...] = columns[:FEATS, :] + matmul(share, local_ref[...], NN)
    folded = back_ref[:, OWN:96, :].astype(F32)
    rows = jnp.concatenate([folded[:, :, :FEATS], folded[:, :, FEATS:]], axis=1)
    hidden_ref[...] = rows.reshape(NODES, FEATS).T.astype(BF16)


def local_grads(back_block, local):
    return pl.pallas_call(
        local_kernel,
        out_shape=[
            jax.ShapeDtypeStruct((FEATS, NODES), F32),
            jax.ShapeDtypeStruct((FEATS, NODES), BF16),
        ],
        compiler_params=params(),
        cost_estimate=cost(2 * 256 * 1024 * 1024, 3 << 20),
        name="local_grads",
    )(back_block, local)


SPREAD = 256


def spread_kernel(back_ref, send_ref, hub_ref, base_ref, out_ref, self_ref, neigh_ref, slots, hub_total):
    @pl.when(pl.program_id(0) == 0)
    def _():
        for peer in range(PEERS):
            slots[:, SLOTS * peer : SLOTS * (peer + 1)] = back_ref[peer, :FEATS, :]
            grads = back_ref[peer, ROWS:, :].astype(F32)
            slice_of, outs = peer // 4, peer % 4
            weight_ref = self_ref if slice_of < 4 else neigh_ref
            row = PIECE * (slice_of % 4)
            weight_ref[row : row + PIECE, TILE * outs : TILE * outs + SLOTS] = grads[:PIECE, :]
            weight_ref[row : row + PIECE, TILE * outs + SLOTS : TILE * (outs + 1)] = grads[PIECE:, :]
        sums = jnp.sum(back_ref[:, FEATS:ROWS, :].astype(F32), axis=0)
        total = sums[:, :FEATS] + sums[:, FEATS:]
        high = total.astype(BF16).astype(F32)
        stacked = jnp.concatenate(
            [high, total - high, jnp.zeros((SLOTS - 2 * HUBS_OWN, FEATS), F32)], axis=0
        )
        hub_total[...] = stacked.T.astype(BF16)

    first = pl.program_id(0) * SPREAD
    node = lax.broadcasted_iota(jnp.int32, (SPREAD, 2 * SLOTS), 0) + first
    grad = base_ref[...]
    for pair in range(PEERS // 2):
        grad = grad + matmul(
            slots[:, 2 * SLOTS * pair : 2 * SLOTS * (pair + 1)],
            one_hot(node == pair_lanes(send_ref, pair)),
            NT,
        )
    hub_node = lax.broadcasted_iota(jnp.int32, (SPREAD, SLOTS), 0) + first
    grad = grad + matmul(hub_total[...], one_hot(hub_node == hub_ref[...]), NT)
    out_ref[...] = grad.astype(BF16)


def spread_grads(returned, send_lanes, hub_lanes, base):
    return pl.pallas_call(
        spread_kernel,
        grid=(NODES // SPREAD,),
        in_specs=[
            whole((PEERS, RETURN_ROWS, SLOTS)),
            whole((PEERS, SLOTS)),
            whole((1, SLOTS)),
            pl.BlockSpec((FEATS, SPREAD), lambda i: (0, i)),
        ],
        out_specs=[
            pl.BlockSpec((FEATS, SPREAD), lambda i: (0, i)),
            whole((FEATS, OUTS)),
            whole((FEATS, OUTS)),
        ],
        out_shape=[
            jax.ShapeDtypeStruct((FEATS, NODES), BF16),
            jax.ShapeDtypeStruct((FEATS, OUTS), F32),
            jax.ShapeDtypeStruct((FEATS, OUTS), F32),
        ],
        scratch_shapes=[pltpu.VMEM((FEATS, PEERS * SLOTS), BF16), pltpu.VMEM((FEATS, SLOTS), BF16)],
        compiler_params=params(),
        cost_estimate=cost(2 * 256 * 4224 * 1024, 2 << 20),
        name="spread_grads",
    )(returned, send_lanes, hub_lanes, base)


def exchange(blocks, axis):
    return lax.all_to_all(blocks, axis, 0, 0, tiled=True)


def per_device(feats, w_self, w_neigh, cotangent, loc_nbr, send_rows, recv_node, hub_rows, hub_nbr):
    send_lanes = send_rows.reshape(PEERS, SLOTS)
    recv_lanes = recv_node.reshape(PEERS, SLOTS)
    hub_lanes = jnp.concatenate(
        [hub_rows, hub_rows, jnp.full((SLOTS - 2 * HUBS_OWN,), -1, jnp.int32)]
    )[None, :]
    weights = lax.all_gather(jnp.concatenate([w_self, w_neigh], axis=0), "col", axis=0, tiled=True)
    incoming = exchange(gather_slots(feats, send_lanes, hub_rows[None, :]), "row")
    local, slot, hubs, degree = build_counts(loc_nbr, recv_lanes, hub_nbr)
    node_block = exchange(
        aggregate(feats, incoming, local, slot, hubs, degree, cotangent), "col"
    )
    own_degree = lax.dynamic_slice_in_dim(degree[0], OWN * lax.axis_index("col"), OWN)[:, None]
    joined_cols = exchange(regroup(node_block), "row").reshape(PEERS * OWN, TILE).T
    slopes_out, hidden, slopes = forward(node_block, weights)
    slopes_rows = exchange(slopes_out, "row").reshape(PEERS * OWN, TILE)
    back = backward(slopes, weights, own_degree)
    back_block = exchange(weight_parts(joined_cols, slopes_rows, back, hidden), "col")
    returned = exchange(return_slots(back_block, slot, hubs), "row")
    base, hidden_out = local_grads(back_block, local)
    grad_feats, grad_self, grad_neigh = spread_grads(returned, send_lanes, hub_lanes, base)
    return (hidden_out, grad_feats, grad_self, grad_neigh)


def solution(mesh):
    return jax.shard_map(
        per_device,
        mesh=mesh,
        in_specs=(
            P("col", "row"),
            P("col", None),
            P("col", None),
            P("col", "row"),
            P("row", None),
            P("row", None, None),
            P("row", None, None),
            P("row"),
            P("row", None),
        ),
        out_specs=(P("col", "row"), P("col", "row"), P("col", None), P("col", None)),
        check_vma=False,
    )
```

```python
import jax
import jax.numpy as jnp
from jax import lax
from jax.experimental import pallas as pl
from jax.experimental.pallas import tpu as pltpu
from jax.sharding import PartitionSpec as P

NODES = 1024
FEATS = 64
PEERS = 32
SLOTS = 128
HUBS_OWN = 16
HUBS = 512
ROWS = 80
LAYERS = 16
OWN = 64
OUTS = 1024
BF16 = jnp.bfloat16
F32 = jnp.float32
NT = (((1,), (1,)), ((), ()))
NN = (((1,), (0,)), ((), ()))
MIB = 1 << 20


def params(mib):
    return pltpu.CompilerParams(vmem_limit_bytes=mib * MIB)


def cost(flops, moved):
    return pl.CostEstimate(flops=flops, bytes_accessed=moved, transcendentals=0)


def whole(shape):
    return pl.BlockSpec(shape, lambda *_: (0,) * len(shape))


def one_hot(mask):
    return jnp.where(mask, 1.0, 0.0).astype(BF16)


def matmul(a, b, dims):
    return lax.dot_general(a, b, dims, preferred_element_type=F32)


def pair_lanes(ref, pair):
    return jnp.concatenate([ref[2 * pair : 2 * pair + 1, :], ref[2 * pair + 1 : 2 * pair + 2, :]], axis=1)


def gather_kernel(x_ref, send_ref, hub_ref, out_ref):
    x = x_ref[...]
    node = lax.broadcasted_iota(jnp.int32, (NODES, 2 * SLOTS), 0)
    hub_node = lax.broadcasted_iota(jnp.int32, (NODES, HUBS_OWN), 0)
    hub_feats = matmul(x, one_hot(hub_node == hub_ref[...]), NN)
    hub_rows = hub_feats.T
    hub_block = jnp.concatenate([hub_rows, jnp.zeros_like(hub_rows)], axis=1).astype(BF16)
    for pair in range(PEERS // 2):
        picked = matmul(x, one_hot(node == pair_lanes(send_ref, pair)), NN).astype(BF16)
        out_ref[2 * pair, :FEATS, :] = picked[:, :SLOTS]
        out_ref[2 * pair + 1, :FEATS, :] = picked[:, SLOTS:]
        out_ref[2 * pair, FEATS:, :] = hub_block
        out_ref[2 * pair + 1, FEATS:, :] = hub_block


def gather_slots(feats, send_lanes, hub_own):
    return pl.pallas_call(
        gather_kernel,
        out_shape=jax.ShapeDtypeStruct((PEERS, ROWS, SLOTS), BF16),
        compiler_params=params(8),
        cost_estimate=cost(2 * 256 * 4096 * 1024, 1 << 20),
        name="gather_slots",
    )(feats, send_lanes, hub_own)


BUILD = 128


def build_kernel(loc_ref, hub_ref, local_ref, hubs_ref):
    lane = lax.broadcasted_iota(jnp.int32, (BUILD, NODES), 1)
    counts = jnp.zeros((BUILD, NODES), F32)
    for k in range(loc_ref.shape[1]):
        counts = counts + jnp.where(lane == loc_ref[:, k : k + 1], 1.0, 0.0)
    local_ref[...] = counts.astype(BF16)
    hub_lane = lax.broadcasted_iota(jnp.int32, (BUILD, HUBS), 1)
    hub_counts = jnp.zeros((BUILD, HUBS), F32)
    for k in range(hub_ref.shape[1]):
        hub_counts = hub_counts + jnp.where(hub_lane == hub_ref[:, k : k + 1], 1.0, 0.0)
    hubs_ref[...] = hub_counts.astype(BF16)


def build_counts(loc_nbr, hub_nbr):
    return pl.pallas_call(
        build_kernel,
        grid=(NODES // BUILD,),
        in_specs=[
            pl.BlockSpec((BUILD, loc_nbr.shape[1]), lambda i: (i, 0)),
            pl.BlockSpec((BUILD, hub_nbr.shape[1]), lambda i: (i, 0)),
        ],
        out_specs=[
            pl.BlockSpec((BUILD, NODES), lambda i: (i, 0)),
            pl.BlockSpec((BUILD, HUBS), lambda i: (i, 0)),
        ],
        out_shape=[
            jax.ShapeDtypeStruct((NODES, NODES), BF16),
            jax.ShapeDtypeStruct((NODES, HUBS), BF16),
        ],
        compiler_params=params(8),
        cost_estimate=cost(1 << 30, 12 << 20),
        name="build_counts",
    )(loc_nbr, hub_nbr)


AGG = 256


def fold_halves(block):
    return jnp.concatenate([block[: OWN // 2, :], block[OWN // 2 :, :]], axis=1)


NEIGHBOURS = 10.0


def aggregate_kernel(
    x_ref, inc_ref, recv_ref, local_ref, hubs_ref, cot_ref, out_ref, degree_ref, slots, table
):
    for peer in range(PEERS):
        slots[:FEATS, SLOTS * peer : SLOTS * (peer + 1)] = inc_ref[peer, :FEATS, :]
    slots[FEATS:, :] = jnp.ones((16, PEERS * SLOTS), BF16)
    rows = inc_ref[:, FEATS:, :].astype(F32).reshape(HUBS, SLOTS)
    table[...] = rows.T[:FEATS, :].astype(BF16)
    for tile in range(NODES // AGG):
        lanes = slice(AGG * tile, AGG * (tile + 1))
        node = lax.broadcasted_iota(jnp.int32, (AGG, 2 * SLOTS), 0) + AGG * tile
        remote = jnp.zeros((ROWS, AGG), F32)
        for pair in range(PEERS // 2):
            remote = remote + matmul(
                slots[:, 2 * SLOTS * pair : 2 * SLOTS * (pair + 1)],
                one_hot(node == pair_lanes(recv_ref, pair)),
                NT,
            )
        total = (
            remote[:FEATS, :]
            + matmul(x_ref[...], local_ref[lanes, :], NT)
            + matmul(table[...], hubs_ref[lanes, :], NT)
        )
        degree = remote[FEATS : FEATS + 8, :] + NEIGHBOURS
        degree_ref[:, lanes] = degree
        mean = (total / degree[0:1, :]).T
        nodes = jnp.concatenate([x_ref[:, lanes].astype(F32).T, mean], axis=1).astype(BF16)
        slopes = cot_ref[:, lanes].astype(F32).T
        for part in range(AGG // OWN):
            layer = AGG // OWN * tile + part
            out_ref[layer, :OWN, :] = nodes[OWN * part : OWN * (part + 1), :]
            out_ref[layer, OWN:, :] = fold_halves(slopes[OWN * part : OWN * (part + 1), :]).astype(BF16)


def aggregate(feats, incoming, recv_lanes, local, hubs, cotangent):
    return pl.pallas_call(
        aggregate_kernel,
        out_shape=[
            jax.ShapeDtypeStruct((LAYERS, 96, SLOTS), BF16),
            jax.ShapeDtypeStruct((8, NODES), F32),
        ],
        scratch_shapes=[pltpu.VMEM((ROWS, PEERS * SLOTS), BF16), pltpu.VMEM((FEATS, HUBS), BF16)],
        compiler_params=params(16),
        cost_estimate=cost(2 * 256 * 5632 * 1024, 5 << 20),
        name="aggregate",
    )(feats, incoming, recv_lanes, local, hubs, cotangent)


PIECE = 16
TILE = 256


def regroup_kernel(inc_ref, out_ref):
    group = lax.broadcasted_iota(jnp.int32, (OWN, SLOTS), 1) // PIECE
    for half in range(2):
        blocks = [inc_ref[8 * half + i, :OWN, :].astype(F32) for i in range(8)]
        for slice_of in range(8):
            tile = jnp.zeros((OWN, SLOTS), F32)
            for i in range(8):
                moved = blocks[i]
                if i != slice_of:
                    moved = pltpu.roll(moved, (PIECE * (i - slice_of)) % SLOTS, 1)
                tile = jnp.where(group == i, moved, tile)
            tile = tile.astype(BF16)
            for outs in range(4):
                out_ref[4 * slice_of + outs, :, SLOTS * half : SLOTS * (half + 1)] = tile


def regroup(node_block):
    return pl.pallas_call(
        regroup_kernel,
        out_shape=jax.ShapeDtypeStruct((PEERS, OWN, TILE), BF16),
        compiler_params=params(6),
        cost_estimate=cost(1 << 24, 2 << 20),
        name="regroup",
    )(node_block)


HALF = OUTS // 2


def forward_kernel(inc_ref, own_ref, other_ref, slopes_ref, hidden_ref, flat_ref, halves):
    core = lax.axis_index("row") % 2
    joined = jnp.concatenate([inc_ref[layer, :OWN, :] for layer in range(LAYERS)], axis=1)
    halves[core] = matmul(joined, own_ref[...], NN)
    halves[1 - core] = matmul(joined, other_ref[...], NN)
    for pair in range(LAYERS // 2):
        side, start = pair // 4, SLOTS * (pair % 4)
        preact = halves[side, :, start : start + SLOTS]
        sigmoid_part = jax.nn.sigmoid(preact)
        hidden = preact * sigmoid_part
        slope = sigmoid_part * (1.0 + preact * (1.0 - sigmoid_part))
        even = inc_ref[2 * pair, OWN:, :].astype(F32)
        odd = inc_ref[2 * pair + 1, OWN:, :].astype(F32)
        top = jnp.concatenate([even[:, :FEATS], odd[:, :FEATS]], axis=1)
        bottom = jnp.concatenate([even[:, FEATS:], odd[:, FEATS:]], axis=1)
        slopes = (jnp.concatenate([top, bottom], axis=0) * slope).astype(BF16)
        flat_ref[side, :, start : start + SLOTS] = slopes
        for slice_of in range(8):
            column = SLOTS * (pair % 2)
            slopes_ref[4 * slice_of + pair // 2, :, column : column + SLOTS] = slopes
        hidden_ref[2 * pair] = fold_halves(hidden[:, :FEATS]).astype(BF16)
        hidden_ref[2 * pair + 1] = fold_halves(hidden[:, FEATS:]).astype(BF16)


def forward(node_block, own, other):
    return pl.pallas_call(
        forward_kernel,
        out_shape=[
            jax.ShapeDtypeStruct((PEERS, OWN, TILE), BF16),
            jax.ShapeDtypeStruct((LAYERS, OWN // 2, SLOTS), BF16),
            jax.ShapeDtypeStruct((2, OWN, HALF), BF16),
        ],
        scratch_shapes=[pltpu.VMEM((2, OWN, HALF), F32)],
        compiler_params=params(12),
        cost_estimate=cost(2 * 256 * 2048 * 1024, 6 << 20),
        name="forward",
    )(node_block, own, other)


def backward_kernel(slopes_ref, own_ref, other_ref, degree_ref, out_ref):
    core = lax.axis_index("row") % 2
    back = matmul(slopes_ref[core], own_ref[...], NT) + matmul(
        slopes_ref[1 - core], other_ref[...], NT
    )
    direct = lax.broadcasted_iota(jnp.int32, (OWN, SLOTS), 1) < FEATS
    divisor = jnp.where(direct, 1.0, degree_ref[...])
    for layer in range(LAYERS):
        out_ref[layer] = (back[:, SLOTS * layer : SLOTS * (layer + 1)] / divisor).astype(BF16)


def backward(slopes, own, other, own_degree):
    return pl.pallas_call(
        backward_kernel,
        out_shape=jax.ShapeDtypeStruct((LAYERS, OWN, SLOTS), BF16),
        compiler_params=params(12),
        cost_estimate=cost(2 * 256 * 2048 * 1024, 6 << 20),
        name="backward",
    )(slopes, own, other, own_degree)


def weight_kernel(joined_ref, slopes_ref, back_ref, hidden_ref, out_ref):
    part = matmul(joined_ref[...], slopes_ref[...], NN).astype(BF16)
    for layer in range(LAYERS):
        out_ref[layer, :OWN, :] = back_ref[layer]
        out_ref[layer, OWN:96, :] = hidden_ref[layer]
        out_ref[layer, 96:112, :] = part[PIECE * layer : PIECE * (layer + 1), :SLOTS]
        out_ref[layer, 112:, :] = part[PIECE * layer : PIECE * (layer + 1), SLOTS:]


def weight_parts(joined_cols, slopes_rows, back, hidden):
    return pl.pallas_call(
        weight_kernel,
        out_shape=jax.ShapeDtypeStruct((LAYERS, SLOTS, SLOTS), BF16),
        compiler_params=params(8),
        cost_estimate=cost(2 * 256 * 2048 * 256, 3 << 20),
        name="weight_parts",
    )(joined_cols, slopes_rows, back, hidden)


RETURN_ROWS = 112


def return_kernel(back_ref, recv_ref, hubs_ref, out_ref):
    rows = back_ref[:, :OWN, :].astype(F32).reshape(NODES, SLOTS)
    share = rows.T[FEATS:, :].astype(BF16)
    sums = jnp.sum(back_ref[:, 96:, :].astype(F32), axis=0).astype(BF16)
    terms = matmul(share, hubs_ref[...], NN).T
    high = terms.astype(BF16).astype(F32)
    both = jnp.concatenate([high, terms - high], axis=1)
    out_ref[:, FEATS:ROWS, :] = both.reshape(PEERS, HUBS_OWN, SLOTS).astype(BF16)
    node = lax.broadcasted_iota(jnp.int32, (NODES, 2 * SLOTS), 0)
    for pair in range(PEERS // 2):
        values = matmul(share, one_hot(node == pair_lanes(recv_ref, pair)), NN).astype(BF16)
        out_ref[2 * pair, :FEATS, :] = values[:, :SLOTS]
        out_ref[2 * pair + 1, :FEATS, :] = values[:, SLOTS:]
        out_ref[2 * pair, ROWS:, :] = sums
        out_ref[2 * pair + 1, ROWS:, :] = sums


def return_slots(back_block, recv_lanes, hubs):
    return pl.pallas_call(
        return_kernel,
        out_shape=jax.ShapeDtypeStruct((PEERS, RETURN_ROWS, SLOTS), BF16),
        compiler_params=params(12),
        cost_estimate=cost(2 * 256 * 4608 * 1024, 3 << 20),
        name="return_slots",
    )(back_block, recv_lanes, hubs)


def local_kernel(back_ref, local_ref, base_ref, hidden_ref):
    columns = back_ref[:, :OWN, :].astype(F32).reshape(NODES, SLOTS).T
    share = columns[FEATS:, :].astype(BF16)
    base_ref[...] = columns[:FEATS, :] + matmul(share, local_ref[...], NN)
    folded = back_ref[:, OWN:96, :].astype(F32)
    rows = jnp.concatenate([folded[:, :, :FEATS], folded[:, :, FEATS:]], axis=1)
    hidden_ref[...] = rows.reshape(NODES, FEATS).T.astype(BF16)


def local_grads(back_block, local):
    return pl.pallas_call(
        local_kernel,
        out_shape=[
            jax.ShapeDtypeStruct((FEATS, NODES), F32),
            jax.ShapeDtypeStruct((FEATS, NODES), BF16),
        ],
        compiler_params=params(8),
        cost_estimate=cost(2 * 256 * 1024 * 1024, 3 << 20),
        name="local_grads",
    )(back_block, local)


SPREAD = 256


def spread_kernel(back_ref, send_ref, hub_ref, base_ref, out_ref, self_ref, neigh_ref, slots, hub_total):
    @pl.when(pl.program_id(0) == 0)
    def _():
        for peer in range(PEERS):
            slots[:, SLOTS * peer : SLOTS * (peer + 1)] = back_ref[peer, :FEATS, :]
            grads = back_ref[peer, ROWS:, :].astype(F32)
            slice_of, outs = peer // 4, peer % 4
            weight_ref = self_ref if slice_of < 4 else neigh_ref
            row = PIECE * (slice_of % 4)
            weight_ref[row : row + PIECE, TILE * outs : TILE * outs + SLOTS] = grads[:PIECE, :]
            weight_ref[row : row + PIECE, TILE * outs + SLOTS : TILE * (outs + 1)] = grads[PIECE:, :]
        sums = jnp.sum(back_ref[:, FEATS:ROWS, :].astype(F32), axis=0)
        total = sums[:, :FEATS] + sums[:, FEATS:]
        high = total.astype(BF16).astype(F32)
        hub_total[0] = high.T.astype(BF16)
        hub_total[1] = (total - high).T.astype(BF16)

    first = pl.program_id(0) * SPREAD
    node = lax.broadcasted_iota(jnp.int32, (SPREAD, 2 * SLOTS), 0) + first
    grad = base_ref[...]
    for pair in range(PEERS // 2):
        grad = grad + matmul(
            slots[:, 2 * SLOTS * pair : 2 * SLOTS * (pair + 1)],
            one_hot(node == pair_lanes(send_ref, pair)),
            NT,
        )
    hub_node = lax.broadcasted_iota(jnp.int32, (SPREAD, HUBS_OWN), 0) + first
    hub_hot = one_hot(hub_node == hub_ref[...])
    grad = grad + matmul(hub_total[0], hub_hot, NT) + matmul(hub_total[1], hub_hot, NT)
    out_ref[...] = grad.astype(BF16)


def spread_grads(returned, send_lanes, hub_own, base):
    return pl.pallas_call(
        spread_kernel,
        grid=(NODES // SPREAD,),
        in_specs=[
            whole((PEERS, RETURN_ROWS, SLOTS)),
            whole((PEERS, SLOTS)),
            whole((1, HUBS_OWN)),
            pl.BlockSpec((FEATS, SPREAD), lambda i: (0, i)),
        ],
        out_specs=[
            pl.BlockSpec((FEATS, SPREAD), lambda i: (0, i)),
            whole((FEATS, OUTS)),
            whole((FEATS, OUTS)),
        ],
        out_shape=[
            jax.ShapeDtypeStruct((FEATS, NODES), BF16),
            jax.ShapeDtypeStruct((FEATS, OUTS), F32),
            jax.ShapeDtypeStruct((FEATS, OUTS), F32),
        ],
        scratch_shapes=[pltpu.VMEM((FEATS, PEERS * SLOTS), BF16), pltpu.VMEM((2, FEATS, HUBS_OWN), BF16)],
        compiler_params=params(8),
        cost_estimate=cost(2 * 256 * 4224 * 1024, 2 << 20),
        name="spread_grads",
    )(returned, send_lanes, hub_own, base)


def exchange(blocks, axis):
    return lax.all_to_all(blocks, axis, 0, 0, tiled=True)


def per_device(feats, w_self, w_neigh, cotangent, loc_nbr, send_rows, recv_node, hub_rows, hub_nbr):
    send_lanes = send_rows.reshape(PEERS, SLOTS)
    recv_lanes = recv_node.reshape(PEERS, SLOTS)
    hub_own = hub_rows[None, :]
    core = lax.axis_index("row") % 2
    own_half = lax.dynamic_slice_in_dim(
        jnp.concatenate([w_self, w_neigh], axis=0), HALF * core, HALF, 1
    )
    own = lax.all_gather(own_half, "col", axis=0, tiled=True)
    other = lax.ppermute(own, "row", [(i, i ^ 1) for i in range(PEERS)])
    incoming = exchange(gather_slots(feats, send_lanes, hub_own), "row")
    local, hubs = build_counts(loc_nbr, hub_nbr)
    outgoing, degree = aggregate(feats, incoming, recv_lanes, local, hubs, cotangent)
    node_block = exchange(outgoing, "col")
    own_degree = lax.dynamic_slice_in_dim(degree[0], OWN * lax.axis_index("col"), OWN)[:, None]
    joined_cols = exchange(regroup(node_block), "row").reshape(PEERS * OWN, TILE).T
    slopes_out, hidden, slopes = forward(node_block, own, other)
    slopes_rows = exchange(slopes_out, "row").reshape(PEERS * OWN, TILE)
    back = backward(slopes, own, other, own_degree)
    back_block = exchange(weight_parts(joined_cols, slopes_rows, back, hidden), "col")
    returned = exchange(return_slots(back_block, recv_lanes, hubs), "row")
    base, hidden_out = local_grads(back_block, local)
    grad_feats, grad_self, grad_neigh = spread_grads(returned, send_lanes, hub_own, base)
    return (hidden_out, grad_feats, grad_self, grad_neigh)


def solution(mesh):
    return jax.shard_map(
        per_device,
        mesh=mesh,
        in_specs=(
            P("col", "row"),
            P("col", None),
            P("col", None),
            P("col", "row"),
            P("row", None),
            P("row", None, None),
            P("row", None, None),
            P("row"),
            P("row", None),
        ),
        out_specs=(P("col", "row"), P("col", "row"), P("col", None), P("col", None)),
        check_vma=False,
    )
```

```python
import jax
import jax.numpy as jnp
from jax import lax
from jax.experimental import pallas as pl
from jax.experimental.pallas import tpu as pltpu
from jax.sharding import PartitionSpec as P

NODES = 1024
FEATS = 64
PEERS = 32
SLOTS = 128
HUBS_OWN = 16
HUBS = 512
ROWS = 80
LAYERS = 16
OWN = 64
OUTS = 1024
BF16 = jnp.bfloat16
F32 = jnp.float32
NT = (((1,), (1,)), ((), ()))
NN = (((1,), (0,)), ((), ()))
MIB = 1 << 20


def params(mib):
    return pltpu.CompilerParams(vmem_limit_bytes=mib * MIB)


def cost(flops, moved):
    return pl.CostEstimate(flops=flops, bytes_accessed=moved, transcendentals=0)


def whole(shape):
    return pl.BlockSpec(shape, lambda *_: (0,) * len(shape))


HBM = pl.BlockSpec(memory_space=pltpu.HBM)
VMEM = pl.BlockSpec(memory_space=pltpu.VMEM)


def copies(sems, *pairs):
    started = []
    for i, (source, target) in enumerate(pairs):
        copy = pltpu.make_async_copy(source, target, sems.at[i])
        copy.start()
        started.append(copy)
    return started


def one_hot(mask):
    return jnp.where(mask, 1.0, 0.0).astype(BF16)


def matmul(a, b, dims):
    return lax.dot_general(a, b, dims, preferred_element_type=F32)


def pair_lanes(ref, pair):
    return jnp.concatenate([ref[2 * pair : 2 * pair + 1, :], ref[2 * pair + 1 : 2 * pair + 2, :]], axis=1)


def gather_kernel(x_hbm, send_hbm, hub_hbm, out_ref, x_ref, send_ref, hub_ref, sems):
    for copy in copies(sems, (x_hbm, x_ref), (send_hbm, send_ref), (hub_hbm, hub_ref)):
        copy.wait()
    x = x_ref[...]
    node = lax.broadcasted_iota(jnp.int32, (NODES, 2 * SLOTS), 0)
    hub_node = lax.broadcasted_iota(jnp.int32, (NODES, HUBS_OWN), 0)
    hub_feats = matmul(x, one_hot(hub_node == hub_ref[...]), NN)
    hub_rows = hub_feats.T
    hub_block = jnp.concatenate([hub_rows, jnp.zeros_like(hub_rows)], axis=1).astype(BF16)
    for pair in range(PEERS // 2):
        picked = matmul(x, one_hot(node == pair_lanes(send_ref, pair)), NN).astype(BF16)
        out_ref[2 * pair, :FEATS, :] = picked[:, :SLOTS]
        out_ref[2 * pair + 1, :FEATS, :] = picked[:, SLOTS:]
        out_ref[2 * pair, FEATS:, :] = hub_block
        out_ref[2 * pair + 1, FEATS:, :] = hub_block


def gather_slots(feats, send_lanes, hub_own):
    return pl.pallas_call(
        gather_kernel,
        in_specs=[HBM, HBM, HBM],
        out_shape=jax.ShapeDtypeStruct((PEERS, ROWS, SLOTS), BF16),
        scratch_shapes=[
            pltpu.VMEM((FEATS, NODES), BF16),
            pltpu.VMEM((PEERS, SLOTS), jnp.int32),
            pltpu.VMEM((1, HUBS_OWN), jnp.int32),
            pltpu.SemaphoreType.DMA((3,)),
        ],
        compiler_params=params(60),
        cost_estimate=cost(2 * 256 * 4096 * 1024, 1 << 20),
        name="gather_slots",
    )(feats, send_lanes, hub_own)


BUILD = 128


def build_kernel(loc_ref, hub_ref, local_ref, hubs_ref):
    lane = lax.broadcasted_iota(jnp.int32, (BUILD, NODES), 1)
    counts = jnp.zeros((BUILD, NODES), F32)
    for k in range(loc_ref.shape[1]):
        counts = counts + jnp.where(lane == loc_ref[:, k : k + 1], 1.0, 0.0)
    local_ref[...] = counts.astype(BF16)
    hub_lane = lax.broadcasted_iota(jnp.int32, (BUILD, HUBS), 1)
    hub_counts = jnp.zeros((BUILD, HUBS), F32)
    for k in range(hub_ref.shape[1]):
        hub_counts = hub_counts + jnp.where(hub_lane == hub_ref[:, k : k + 1], 1.0, 0.0)
    hubs_ref[...] = hub_counts.astype(BF16)


def build_counts(loc_nbr, hub_nbr):
    return pl.pallas_call(
        build_kernel,
        grid=(NODES // BUILD,),
        in_specs=[
            pl.BlockSpec((BUILD, loc_nbr.shape[1]), lambda i: (i, 0)),
            pl.BlockSpec((BUILD, hub_nbr.shape[1]), lambda i: (i, 0)),
        ],
        out_specs=[
            pl.BlockSpec((BUILD, NODES), lambda i: (i, 0)),
            pl.BlockSpec((BUILD, HUBS), lambda i: (i, 0)),
        ],
        out_shape=[
            jax.ShapeDtypeStruct((NODES, NODES), BF16),
            jax.ShapeDtypeStruct((NODES, HUBS), BF16),
        ],
        compiler_params=params(60),
        cost_estimate=cost(1 << 30, 12 << 20),
        name="build_counts",
    )(loc_nbr, hub_nbr)


AGG = 256


def fold_halves(block):
    return jnp.concatenate([block[: OWN // 2, :], block[OWN // 2 :, :]], axis=1)


NEIGHBOURS = 10.0


def aggregate_kernel(
    x_hbm, inc_ref, recv_hbm, local_hbm, hubs_hbm, cot_hbm, out_ref, degree_ref,
    slots, table, recv_ref, x_ref, local_ref, hubs_ref, cot_ref, sems,
):
    staged = copies(
        sems,
        (recv_hbm, recv_ref),
        (x_hbm, x_ref),
        (local_hbm, local_ref),
        (hubs_hbm, hubs_ref),
        (cot_hbm, cot_ref),
    )
    for peer in range(PEERS):
        slots[:FEATS, SLOTS * peer : SLOTS * (peer + 1)] = inc_ref[peer, :FEATS, :]
    slots[FEATS:, :] = jnp.ones((16, PEERS * SLOTS), BF16)
    rows = inc_ref[:, FEATS:, :].astype(F32).reshape(HUBS, SLOTS)
    table[...] = rows.T[:FEATS, :].astype(BF16)
    staged[0].wait()
    for tile in range(NODES // AGG):
        lanes = slice(AGG * tile, AGG * (tile + 1))
        node = lax.broadcasted_iota(jnp.int32, (AGG, 2 * SLOTS), 0) + AGG * tile
        remote = jnp.zeros((ROWS, AGG), F32)
        for pair in range(PEERS // 2):
            remote = remote + matmul(
                slots[:, 2 * SLOTS * pair : 2 * SLOTS * (pair + 1)],
                one_hot(node == pair_lanes(recv_ref, pair)),
                NT,
            )
        if tile == 0:
            for copy in staged[1:]:
                copy.wait()
        total = (
            remote[:FEATS, :]
            + matmul(x_ref[...], local_ref[lanes, :], NT)
            + matmul(table[...], hubs_ref[lanes, :], NT)
        )
        degree = remote[FEATS : FEATS + 8, :] + NEIGHBOURS
        degree_ref[:, lanes] = degree
        mean = (total / degree[0:1, :]).T
        nodes = jnp.concatenate([x_ref[:, lanes].astype(F32).T, mean], axis=1).astype(BF16)
        slopes = cot_ref[:, lanes].astype(F32).T
        for part in range(AGG // OWN):
            layer = AGG // OWN * tile + part
            out_ref[layer, :OWN, :] = nodes[OWN * part : OWN * (part + 1), :]
            out_ref[layer, OWN:, :] = fold_halves(slopes[OWN * part : OWN * (part + 1), :]).astype(BF16)


def aggregate(feats, incoming, recv_lanes, local, hubs, cotangent):
    return pl.pallas_call(
        aggregate_kernel,
        out_shape=[
            jax.ShapeDtypeStruct((LAYERS, 96, SLOTS), BF16),
            jax.ShapeDtypeStruct((8, NODES), F32),
        ],
        in_specs=[HBM, VMEM, HBM, HBM, HBM, HBM],
        scratch_shapes=[
            pltpu.VMEM((ROWS, PEERS * SLOTS), BF16),
            pltpu.VMEM((FEATS, HUBS), BF16),
            pltpu.VMEM((PEERS, SLOTS), jnp.int32),
            pltpu.VMEM((FEATS, NODES), BF16),
            pltpu.VMEM((NODES, NODES), BF16),
            pltpu.VMEM((NODES, HUBS), BF16),
            pltpu.VMEM((FEATS, NODES), BF16),
            pltpu.SemaphoreType.DMA((5,)),
        ],
        compiler_params=params(16),
        cost_estimate=cost(2 * 256 * 5632 * 1024, 5 << 20),
        name="aggregate",
    )(feats, incoming, recv_lanes, local, hubs, cotangent)


PIECE = 16
TILE = 256


def regroup_kernel(inc_ref, out_ref):
    group = lax.broadcasted_iota(jnp.int32, (OWN, SLOTS), 1) // PIECE
    for half in range(2):
        blocks = [inc_ref[8 * half + i, :OWN, :].astype(F32) for i in range(8)]
        for slice_of in range(8):
            tile = jnp.zeros((OWN, SLOTS), F32)
            for i in range(8):
                moved = blocks[i]
                if i != slice_of:
                    moved = pltpu.roll(moved, (PIECE * (i - slice_of)) % SLOTS, 1)
                tile = jnp.where(group == i, moved, tile)
            tile = tile.astype(BF16)
            for outs in range(4):
                out_ref[4 * slice_of + outs, :, SLOTS * half : SLOTS * (half + 1)] = tile


def regroup(node_block):
    return pl.pallas_call(
        regroup_kernel,
        out_shape=jax.ShapeDtypeStruct((PEERS, OWN, TILE), BF16),
        compiler_params=params(16),
        cost_estimate=cost(1 << 24, 2 << 20),
        name="regroup",
    )(node_block)


HALF = OUTS // 2
CHIPS = PEERS // 2


def forward_kernel(
    own_hbm, other_hbm, weights_hbm, slopes_hbm, flat_hbm, hidden_hbm,
    own_block, other_block, weights, blocks, cots, out_tile, flat, hidden, in_sems, out_sems,
):
    core = lax.axis_index("row") % 2
    staged = copies(
        in_sems, (own_hbm, own_block), (other_hbm, other_block), (weights_hbm, weights)
    )
    staged[0].wait()
    staged[1].wait()
    for layer in range(LAYERS):
        lanes = slice(SLOTS * layer, SLOTS * (layer + 1))
        blocks[core, :, lanes] = own_block[layer, :OWN, :]
        blocks[1 - core, :, lanes] = other_block[layer, :OWN, :]
    for layer in range(LAYERS // 2):
        cots[core, layer] = own_block[8 * core + layer, OWN:, :]
        cots[1 - core, layer] = other_block[8 * core + layer, OWN:, :]
    staged[2].wait()
    preacts = matmul(blocks[...].reshape(2 * OWN, 2 * OUTS), weights[...], NN)
    for block in range(2):
        for pair in range(4):
            lanes = slice(SLOTS * pair, SLOTS * (pair + 1))
            preact = preacts[OWN * block : OWN * (block + 1), lanes]
            sigmoid_part = jax.nn.sigmoid(preact)
            silu = preact * sigmoid_part
            slope = sigmoid_part * (1.0 + preact * (1.0 - sigmoid_part))
            even = cots[block, 2 * pair].astype(F32)
            odd = cots[block, 2 * pair + 1].astype(F32)
            top = jnp.concatenate([even[:, :FEATS], odd[:, :FEATS]], axis=1)
            bottom = jnp.concatenate([even[:, FEATS:], odd[:, FEATS:]], axis=1)
            slopes = (jnp.concatenate([top, bottom], axis=0) * slope).astype(BF16)
            column = SLOTS * (pair % 2)
            out_tile[pair // 2, OWN * block : OWN * (block + 1), column : column + SLOTS] = slopes
            flat[OWN * block : OWN * (block + 1), lanes] = slopes
            hidden[block, 2 * pair] = fold_halves(silu[:, :FEATS]).astype(BF16)
            hidden[block, 2 * pair + 1] = fold_halves(silu[:, FEATS:]).astype(BF16)
    sent = copies(
        out_sems,
        *[(out_tile.at[chip % 2], slopes_hbm.at[chip]) for chip in range(CHIPS)],
        (flat, flat_hbm),
        (hidden, hidden_hbm),
    )
    for copy in sent:
        copy.wait()


def forward(own_block, other_block, weights):
    return pl.pallas_call(
        forward_kernel,
        in_specs=[HBM, HBM, HBM],
        out_specs=[HBM, HBM, HBM],
        out_shape=[
            jax.ShapeDtypeStruct((CHIPS, 2 * OWN, TILE), BF16),
            jax.ShapeDtypeStruct((2 * OWN, HALF), BF16),
            jax.ShapeDtypeStruct((2, LAYERS // 2, OWN // 2, SLOTS), BF16),
        ],
        scratch_shapes=[
            pltpu.VMEM((LAYERS, 96, SLOTS), BF16),
            pltpu.VMEM((LAYERS, 96, SLOTS), BF16),
            pltpu.VMEM((2 * OUTS, HALF), BF16),
            pltpu.VMEM((2, OWN, 2 * OUTS), BF16),
            pltpu.VMEM((2, LAYERS // 2, OWN // 2, SLOTS), BF16),
            pltpu.VMEM((2, 2 * OWN, TILE), BF16),
            pltpu.VMEM((2 * OWN, HALF), BF16),
            pltpu.VMEM((2, LAYERS // 2, OWN // 2, SLOTS), BF16),
            pltpu.SemaphoreType.DMA((3,)),
            pltpu.SemaphoreType.DMA((CHIPS + 2,)),
        ],
        compiler_params=params(60),
        cost_estimate=cost(2 * 256 * 2048 * 512, 4 << 20),
        name="forward",
    )(own_block, other_block, weights)


def backward_kernel(slopes_ref, hidden_ref, weights_ref, keep_ref, send_ref, keep_hidden, send_hidden, parts):
    core = lax.axis_index("row") % 2
    back = matmul(slopes_ref[...], weights_ref[...], NT)
    parts[0] = back[:OWN, :]
    parts[1] = back[OWN:, :]
    keep_ref[...] = parts[core]
    send_ref[...] = parts[1 - core]
    keep_hidden[...] = hidden_ref[core]
    send_hidden[...] = hidden_ref[1 - core]


def backward(slopes, hidden, weights):
    part = jax.ShapeDtypeStruct((OWN, 2 * OUTS), F32)
    block = jax.ShapeDtypeStruct((LAYERS // 2, OWN // 2, SLOTS), BF16)
    return pl.pallas_call(
        backward_kernel,
        out_shape=[part, part, block, block],
        scratch_shapes=[pltpu.VMEM((2, OWN, 2 * OUTS), F32)],
        compiler_params=params(60),
        cost_estimate=cost(2 * 256 * 2048 * 512, 4 << 20),
        name="backward",
    )(slopes, hidden, weights)


def combine_kernel(mine_ref, theirs_ref, my_hidden, their_hidden, degree_ref, out_ref):
    core = lax.axis_index("row") % 2
    direct = lax.broadcasted_iota(jnp.int32, (OWN, SLOTS), 1) < FEATS
    divisor = jnp.where(direct, 1.0, degree_ref[...])
    for layer in range(LAYERS):
        lanes = slice(SLOTS * layer, SLOTS * (layer + 1))
        back = mine_ref[:, lanes] + theirs_ref[:, lanes]
        out_ref[layer, :OWN, :] = (back / divisor).astype(BF16)
    for layer in range(LAYERS // 2):
        out_ref[8 * core + layer, OWN:, :] = my_hidden[layer]
        out_ref[8 * (1 - core) + layer, OWN:, :] = their_hidden[layer]


def combine(mine, theirs, my_hidden, their_hidden, own_degree):
    return pl.pallas_call(
        combine_kernel,
        out_shape=jax.ShapeDtypeStruct((LAYERS, 96, SLOTS), BF16),
        compiler_params=params(60),
        cost_estimate=cost(1 << 20, 2 << 20),
        name="combine",
    )(mine, theirs, my_hidden, their_hidden, own_degree)


STEPS = 4


def weight_kernel(joined_hbm, slopes_ref, back_hbm, out_ref, joined, back, sems):
    depth = PEERS * OWN // STEPS
    staged = copies(
        sems,
        *[
            (joined_hbm.at[:, depth * i : depth * (i + 1)], joined.at[:, depth * i : depth * (i + 1)])
            for i in range(STEPS)
        ],
        (back_hbm, back),
    )
    part = jnp.zeros((TILE, TILE), F32)
    for i in range(STEPS):
        staged[i].wait()
        rows = slice(depth * i, depth * (i + 1))
        part = part + matmul(joined[:, rows], slopes_ref[rows, :], NN)
    part = part.astype(BF16)
    for layer in range(LAYERS):
        out_ref[layer, 96:112, :] = part[PIECE * layer : PIECE * (layer + 1), :SLOTS]
        out_ref[layer, 112:, :] = part[PIECE * layer : PIECE * (layer + 1), SLOTS:]
    staged[STEPS].wait()
    out_ref[:, :96, :] = back[...]


def weight_parts(joined_cols, slopes_rows, back):
    return pl.pallas_call(
        weight_kernel,
        in_specs=[HBM, VMEM, HBM],
        out_shape=jax.ShapeDtypeStruct((LAYERS, SLOTS, SLOTS), BF16),
        scratch_shapes=[
            pltpu.VMEM((TILE, PEERS * OWN), BF16),
            pltpu.VMEM((LAYERS, 96, SLOTS), BF16),
            pltpu.SemaphoreType.DMA((STEPS + 1,)),
        ],
        compiler_params=params(16),
        cost_estimate=cost(2 * 256 * 2048 * 256, 3 << 20),
        name="weight_parts",
    )(joined_cols, slopes_rows, back)


RETURN_ROWS = 112


def return_kernel(back_ref, recv_hbm, hubs_hbm, out_hbm, recv_ref, hubs_ref, out_ref, in_sems, out_sems):
    staged = copies(in_sems, (recv_hbm, recv_ref), (hubs_hbm, hubs_ref))
    rows = back_ref[:, :OWN, :].astype(F32).reshape(NODES, SLOTS)
    share = rows.T[FEATS:, :].astype(BF16)
    sums = jnp.sum(back_ref[:, 96:, :].astype(F32), axis=0).astype(BF16)
    node = lax.broadcasted_iota(jnp.int32, (NODES, 2 * SLOTS), 0)
    staged[0].wait()
    sent = []
    for pair in range(PEERS // 2):
        values = matmul(share, one_hot(node == pair_lanes(recv_ref, pair)), NN).astype(BF16)
        for side in range(2):
            peer = 2 * pair + side
            out_ref[peer, :FEATS, :] = values[:, SLOTS * side : SLOTS * (side + 1)]
            out_ref[peer, ROWS:, :] = sums
        if pair == 0:
            staged[1].wait()
            terms = matmul(share, hubs_ref[...], NN).T
            high = terms.astype(BF16).astype(F32)
            both = jnp.concatenate([high, terms - high], axis=1)
            out_ref[:, FEATS:ROWS, :] = both.reshape(PEERS, HUBS_OWN, SLOTS).astype(BF16)
        if pair % 4 == 3:
            part = pl.ds(2 * pair - 6, 8)
            copy = pltpu.make_async_copy(out_ref.at[part], out_hbm.at[part], out_sems.at[pair // 4])
            copy.start()
            sent.append(copy)
    for copy in sent:
        copy.wait()


def return_slots(back_block, recv_lanes, hubs):
    return pl.pallas_call(
        return_kernel,
        in_specs=[VMEM, HBM, HBM],
        out_specs=HBM,
        out_shape=jax.ShapeDtypeStruct((PEERS, RETURN_ROWS, SLOTS), BF16),
        scratch_shapes=[
            pltpu.VMEM((PEERS, SLOTS), jnp.int32),
            pltpu.VMEM((NODES, HUBS), BF16),
            pltpu.VMEM((PEERS, RETURN_ROWS, SLOTS), BF16),
            pltpu.SemaphoreType.DMA((2,)),
            pltpu.SemaphoreType.DMA((4,)),
        ],
        compiler_params=params(60),
        cost_estimate=cost(2 * 256 * 4608 * 1024, 3 << 20),
        name="return_slots",
    )(back_block, recv_lanes, hubs)


def local_kernel(back_ref, local_ref, base_ref, hidden_ref):
    columns = back_ref[:, :OWN, :].astype(F32).reshape(NODES, SLOTS).T
    share = columns[FEATS:, :].astype(BF16)
    base_ref[...] = columns[:FEATS, :] + matmul(share, local_ref[...], NN)
    folded = back_ref[:, OWN:96, :].astype(F32)
    rows = jnp.concatenate([folded[:, :, :FEATS], folded[:, :, FEATS:]], axis=1)
    hidden_ref[...] = rows.reshape(NODES, FEATS).T.astype(BF16)


def local_grads(back_block, local):
    return pl.pallas_call(
        local_kernel,
        out_shape=[
            jax.ShapeDtypeStruct((FEATS, NODES), F32),
            jax.ShapeDtypeStruct((FEATS, NODES), BF16),
        ],
        compiler_params=params(60),
        cost_estimate=cost(2 * 256 * 1024 * 1024, 3 << 20),
        name="local_grads",
    )(back_block, local)


SPREAD = 256


def spread_kernel(
    back_ref, send_hbm, hub_hbm, base_hbm, out_ref, self_hbm, neigh_hbm,
    send_ref, hub_ref, base_ref, grads_ref, slots, in_sems, out_sems,
):
    staged = copies(in_sems, (send_hbm, send_ref), (hub_hbm, hub_ref), (base_hbm, base_ref))
    for peer in range(PEERS):
        slots[:, SLOTS * peer : SLOTS * (peer + 1)] = back_ref[peer, :FEATS, :]
        grads = back_ref[peer, ROWS:, :].astype(F32)
        slice_of, outs = peer // 4, 2 * (peer % 2) + peer // 2 % 2
        rows = slice(PIECE * slice_of, PIECE * (slice_of + 1))
        grads_ref[rows, TILE * outs : TILE * outs + SLOTS] = grads[:PIECE, :]
        grads_ref[rows, TILE * outs + SLOTS : TILE * (outs + 1)] = grads[PIECE:, :]
    sent = copies(
        out_sems, (grads_ref.at[:FEATS], self_hbm), (grads_ref.at[FEATS:], neigh_hbm)
    )
    sums = jnp.sum(back_ref[:, FEATS:ROWS, :].astype(F32), axis=0)
    total = sums[:, :FEATS] + sums[:, FEATS:]
    high = total.astype(BF16).astype(F32)
    hub_high = high.T.astype(BF16)
    hub_low = (total - high).T.astype(BF16)
    for copy in staged:
        copy.wait()
    for tile in range(NODES // SPREAD):
        lanes = slice(SPREAD * tile, SPREAD * (tile + 1))
        node = lax.broadcasted_iota(jnp.int32, (SPREAD, 2 * SLOTS), 0) + SPREAD * tile
        grad = base_ref[:, lanes]
        for pair in range(PEERS // 2):
            grad = grad + matmul(
                slots[:, 2 * SLOTS * pair : 2 * SLOTS * (pair + 1)],
                one_hot(node == pair_lanes(send_ref, pair)),
                NT,
            )
        hub_node = lax.broadcasted_iota(jnp.int32, (SPREAD, HUBS_OWN), 0) + SPREAD * tile
        hub_hot = one_hot(hub_node == hub_ref[...])
        grad = grad + matmul(hub_high, hub_hot, NT) + matmul(hub_low, hub_hot, NT)
        out_ref[:, lanes] = grad.astype(BF16)
    for copy in sent:
        copy.wait()


def spread_grads(returned, send_lanes, hub_own, base):
    return pl.pallas_call(
        spread_kernel,
        in_specs=[VMEM, HBM, HBM, HBM],
        out_specs=[VMEM, HBM, HBM],
        out_shape=[
            jax.ShapeDtypeStruct((FEATS, NODES), BF16),
            jax.ShapeDtypeStruct((FEATS, OUTS), F32),
            jax.ShapeDtypeStruct((FEATS, OUTS), F32),
        ],
        scratch_shapes=[
            pltpu.VMEM((PEERS, SLOTS), jnp.int32),
            pltpu.VMEM((1, HUBS_OWN), jnp.int32),
            pltpu.VMEM((FEATS, NODES), F32),
            pltpu.VMEM((2 * FEATS, OUTS), F32),
            pltpu.VMEM((FEATS, PEERS * SLOTS), BF16),
            pltpu.SemaphoreType.DMA((3,)),
            pltpu.SemaphoreType.DMA((2,)),
        ],
        compiler_params=params(16),
        cost_estimate=cost(2 * 256 * 4224 * 1024, 2 << 20),
        name="spread_grads",
    )(returned, send_lanes, hub_own, base)


SAME_CORE = [list(range(core, PEERS, 2)) for core in range(2)]


def exchange(blocks, axis, groups=None):
    return lax.all_to_all(blocks, axis, 0, 0, axis_index_groups=groups, tiled=True)


def other_core(block):
    return lax.ppermute(block, "row", [(i, i ^ 1) for i in range(PEERS)])


def per_device(feats, w_self, w_neigh, cotangent, loc_nbr, send_rows, recv_node, hub_rows, hub_nbr):
    send_lanes = send_rows.reshape(PEERS, SLOTS)
    recv_lanes = recv_node.reshape(PEERS, SLOTS)
    hub_own = hub_rows[None, :]
    half = HALF * (lax.axis_index("row") % 2)
    weights = lax.all_gather(
        lax.dynamic_slice_in_dim(jnp.concatenate([w_self, w_neigh], axis=0), half, HALF, 1),
        "col",
        axis=0,
        tiled=True,
    )
    incoming = exchange(gather_slots(feats, send_lanes, hub_own), "row")
    local, hubs = build_counts(loc_nbr, hub_nbr)
    outgoing, degree = aggregate(feats, incoming, recv_lanes, local, hubs, cotangent)
    node_block = exchange(outgoing, "col")
    own_degree = lax.dynamic_slice_in_dim(degree[0], OWN * lax.axis_index("col"), OWN)[:, None]
    joined_cols = exchange(regroup(node_block), "row").reshape(PEERS * OWN, TILE).T
    slopes_out, slopes, hidden = forward(node_block, other_core(node_block), weights)
    slopes_rows = exchange(slopes_out, "row", SAME_CORE).reshape(PEERS * OWN, TILE)
    mine, theirs, my_hidden, their_hidden = backward(slopes, hidden, weights)
    back = combine(mine, other_core(theirs), my_hidden, other_core(their_hidden), own_degree)
    back_block = exchange(weight_parts(joined_cols, slopes_rows, back), "col")
    returned = exchange(return_slots(back_block, recv_lanes, hubs), "row")
    base, hidden_out = local_grads(back_block, local)
    grad_feats, grad_self, grad_neigh = spread_grads(returned, send_lanes, hub_own, base)
    return (hidden_out, grad_feats, grad_self, grad_neigh)


def solution(mesh):
    return jax.shard_map(
        per_device,
        mesh=mesh,
        in_specs=(
            P("col", "row"),
            P("col", None),
            P("col", None),
            P("col", "row"),
            P("row", None),
            P("row", None, None),
            P("row", None, None),
            P("row"),
            P("row", None),
        ),
        out_specs=(P("col", "row"), P("col", "row"), P("col", None), P("col", None)),
        check_vma=False,
    )
```

```python
import jax
import jax.numpy as jnp
from jax import lax
from jax.experimental import pallas as pl
from jax.experimental.pallas import tpu as pltpu
from jax.sharding import PartitionSpec as P

NODES = 1024
FEATS = 64
PEERS = 32
SLOTS = 128
HUBS_OWN = 16
HUBS = 512
ROWS = 80
LAYERS = 16
OWN = 64
OUTS = 1024
BF16 = jnp.bfloat16
F32 = jnp.float32
NT = (((1,), (1,)), ((), ()))
NN = (((1,), (0,)), ((), ()))
MIB = 1 << 20


def params(mib):
    return pltpu.CompilerParams(vmem_limit_bytes=mib * MIB)


def cost(flops, moved):
    return pl.CostEstimate(flops=flops, bytes_accessed=moved, transcendentals=0)


def whole(shape):
    return pl.BlockSpec(shape, lambda *_: (0,) * len(shape))


HBM = pl.BlockSpec(memory_space=pltpu.HBM)
VMEM = pl.BlockSpec(memory_space=pltpu.VMEM)


def copies(sems, *pairs):
    started = []
    for i, (source, target) in enumerate(pairs):
        copy = pltpu.make_async_copy(source, target, sems.at[i])
        copy.start()
        started.append(copy)
    return started


def one_hot(mask):
    return jnp.where(mask, 1.0, 0.0).astype(BF16)


def matmul(a, b, dims):
    return lax.dot_general(a, b, dims, preferred_element_type=F32)


def pair_lanes(ref, pair):
    return jnp.concatenate([ref[2 * pair : 2 * pair + 1, :], ref[2 * pair + 1 : 2 * pair + 2, :]], axis=1)


def gather_kernel(x_hbm, send_hbm, hub_hbm, out_ref, x_ref, send_ref, hub_ref, sems):
    for copy in copies(sems, (x_hbm, x_ref), (send_hbm, send_ref), (hub_hbm, hub_ref)):
        copy.wait()
    x = x_ref[...]
    node = lax.broadcasted_iota(jnp.int32, (NODES, 2 * SLOTS), 0)
    hub_node = lax.broadcasted_iota(jnp.int32, (NODES, HUBS_OWN), 0)
    hub_feats = matmul(x, one_hot(hub_node == hub_ref[...]), NN)
    hub_rows = hub_feats.T
    hub_block = jnp.concatenate([hub_rows, jnp.zeros_like(hub_rows)], axis=1).astype(BF16)
    for pair in range(PEERS // 2):
        picked = matmul(x, one_hot(node == pair_lanes(send_ref, pair)), NN).astype(BF16)
        out_ref[2 * pair, :FEATS, :] = picked[:, :SLOTS]
        out_ref[2 * pair + 1, :FEATS, :] = picked[:, SLOTS:]
        out_ref[2 * pair, FEATS:, :] = hub_block
        out_ref[2 * pair + 1, FEATS:, :] = hub_block


def gather_slots(feats, send_lanes, hub_own):
    return pl.pallas_call(
        gather_kernel,
        in_specs=[HBM, HBM, HBM],
        out_shape=jax.ShapeDtypeStruct((PEERS, ROWS, SLOTS), BF16),
        scratch_shapes=[
            pltpu.VMEM((FEATS, NODES), BF16),
            pltpu.VMEM((PEERS, SLOTS), jnp.int32),
            pltpu.VMEM((1, HUBS_OWN), jnp.int32),
            pltpu.SemaphoreType.DMA((3,)),
        ],
        compiler_params=params(60),
        cost_estimate=cost(2 * 256 * 4096 * 1024, 1 << 20),
        name="gather_slots",
    )(feats, send_lanes, hub_own)


BUILD = 256


def counts_of(nbr_ref, rows):
    first = lax.broadcasted_iota(jnp.int32, (rows, nbr_ref.shape[1]), 0)
    counts = jnp.zeros(first.shape, F32)
    for k in range(nbr_ref.shape[0]):
        counts = counts + jnp.where(first == nbr_ref[k : k + 1, :], 1.0, 0.0)
    return counts.astype(BF16)


def build_kernel(x_ref, loc_ref, hub_ref, local_ref, hubs_ref, sum_ref):
    counts = counts_of(loc_ref, NODES)
    local_ref[...] = counts
    hubs_ref[...] = counts_of(hub_ref, HUBS)
    sum_ref[...] = matmul(x_ref[...], counts, NN)


def build_counts(feats, loc_lanes, hub_lanes):
    return pl.pallas_call(
        build_kernel,
        grid=(NODES // BUILD,),
        in_specs=[
            whole((FEATS, NODES)),
            pl.BlockSpec((loc_lanes.shape[0], BUILD), lambda i: (0, i)),
            pl.BlockSpec((hub_lanes.shape[0], BUILD), lambda i: (0, i)),
        ],
        out_specs=[
            pl.BlockSpec((NODES, BUILD), lambda i: (0, i)),
            pl.BlockSpec((HUBS, BUILD), lambda i: (0, i)),
            pl.BlockSpec((FEATS, BUILD), lambda i: (0, i)),
        ],
        out_shape=[
            jax.ShapeDtypeStruct((NODES, NODES), BF16),
            jax.ShapeDtypeStruct((HUBS, NODES), BF16),
            jax.ShapeDtypeStruct((FEATS, NODES), F32),
        ],
        compiler_params=params(60),
        cost_estimate=cost(1 << 30, 4 << 20),
        name="build_counts",
    )(feats, loc_lanes, hub_lanes)


AGG = 256


def fold_halves(block):
    return jnp.concatenate([block[: OWN // 2, :], block[OWN // 2 :, :]], axis=1)


NEIGHBOURS = 10.0


def aggregate_kernel(
    x_hbm, inc_ref, recv_hbm, sum_hbm, hub_hbm, cot_hbm, out_ref, degree_ref,
    slots, table, recv_ref, hub_ref, x_ref, cot_ref, sum_ref, sems,
):
    staged = copies(
        sems,
        (recv_hbm, recv_ref),
        (hub_hbm, hub_ref),
        (x_hbm, x_ref),
        (cot_hbm, cot_ref),
        (sum_hbm, sum_ref),
    )
    for peer in range(PEERS):
        slots[:FEATS, SLOTS * peer : SLOTS * (peer + 1)] = inc_ref[peer, :FEATS, :]
    slots[FEATS:, :] = jnp.ones((16, PEERS * SLOTS), BF16)
    rows = inc_ref[:, FEATS:, :].astype(F32).reshape(HUBS, SLOTS)
    table[...] = rows.T[:FEATS, :].astype(BF16)
    staged[0].wait()
    for tile in range(NODES // AGG):
        lanes = slice(AGG * tile, AGG * (tile + 1))
        node = lax.broadcasted_iota(jnp.int32, (AGG, 2 * SLOTS), 0) + AGG * tile
        remote = jnp.zeros((ROWS, AGG), F32)
        for pair in range(PEERS // 2):
            remote = remote + matmul(
                slots[:, 2 * SLOTS * pair : 2 * SLOTS * (pair + 1)],
                one_hot(node == pair_lanes(recv_ref, pair)),
                NT,
            )
        if tile == 0:
            for copy in staged[1:]:
                copy.wait()
        hubs = counts_of(hub_ref[:, lanes], HUBS)
        total = remote[:FEATS, :] + sum_ref[:, lanes] + matmul(table[...], hubs, NN)
        degree = remote[FEATS : FEATS + 8, :] + NEIGHBOURS
        degree_ref[:, lanes] = degree
        mean = (total / degree[0:1, :]).T
        nodes = jnp.concatenate([x_ref[:, lanes].astype(F32).T, mean], axis=1).astype(BF16)
        slopes = cot_ref[:, lanes].astype(F32).T
        for part in range(AGG // OWN):
            layer = AGG // OWN * tile + part
            out_ref[layer, :OWN, :] = nodes[OWN * part : OWN * (part + 1), :]
            out_ref[layer, OWN:, :] = fold_halves(slopes[OWN * part : OWN * (part + 1), :]).astype(BF16)


def aggregate(feats, incoming, recv_lanes, local_sum, hub_lanes, cotangent):
    return pl.pallas_call(
        aggregate_kernel,
        out_shape=[
            jax.ShapeDtypeStruct((LAYERS, 96, SLOTS), BF16),
            jax.ShapeDtypeStruct((8, NODES), F32),
        ],
        in_specs=[HBM, VMEM, HBM, HBM, HBM, HBM],
        scratch_shapes=[
            pltpu.VMEM((ROWS, PEERS * SLOTS), BF16),
            pltpu.VMEM((FEATS, HUBS), BF16),
            pltpu.VMEM((PEERS, SLOTS), jnp.int32),
            pltpu.VMEM((2, NODES), jnp.int32),
            pltpu.VMEM((FEATS, NODES), BF16),
            pltpu.VMEM((FEATS, NODES), BF16),
            pltpu.VMEM((FEATS, NODES), F32),
            pltpu.SemaphoreType.DMA((5,)),
        ],
        compiler_params=params(16),
        cost_estimate=cost(2 * 256 * 5632 * 1024, 3 << 20),
        name="aggregate",
    )(feats, incoming, recv_lanes, local_sum, hub_lanes, cotangent)


PIECE = 16
TILE = 256


def regroup_kernel(inc_ref, out_ref):
    group = lax.broadcasted_iota(jnp.int32, (OWN, SLOTS), 1) // PIECE
    for half in range(2):
        blocks = [inc_ref[8 * half + i, :OWN, :].astype(F32) for i in range(8)]
        for slice_of in range(8):
            tile = jnp.zeros((OWN, SLOTS), F32)
            for i in range(8):
                moved = blocks[i]
                if i != slice_of:
                    moved = pltpu.roll(moved, (PIECE * (i - slice_of)) % SLOTS, 1)
                tile = jnp.where(group == i, moved, tile)
            tile = tile.astype(BF16)
            for outs in range(4):
                out_ref[4 * slice_of + outs, :, SLOTS * half : SLOTS * (half + 1)] = tile


def regroup(node_block):
    return pl.pallas_call(
        regroup_kernel,
        out_shape=jax.ShapeDtypeStruct((PEERS, OWN, TILE), BF16),
        compiler_params=params(16),
        cost_estimate=cost(1 << 24, 2 << 20),
        name="regroup",
    )(node_block)


HALF = OUTS // 2
CHIPS = PEERS // 2


def forward_kernel(
    own_hbm, other_hbm, weights_hbm, slopes_hbm, flat_hbm, hidden_hbm,
    own_block, other_block, weights, blocks, cots, out_tile, flat, hidden, in_sems, out_sems,
):
    core = lax.axis_index("row") % 2
    staged = copies(
        in_sems, (own_hbm, own_block), (other_hbm, other_block), (weights_hbm, weights)
    )
    staged[0].wait()
    staged[1].wait()
    for layer in range(LAYERS):
        lanes = slice(SLOTS * layer, SLOTS * (layer + 1))
        blocks[core, :, lanes] = own_block[layer, :OWN, :]
        blocks[1 - core, :, lanes] = other_block[layer, :OWN, :]
    for layer in range(LAYERS // 2):
        cots[core, layer] = own_block[8 * core + layer, OWN:, :]
        cots[1 - core, layer] = other_block[8 * core + layer, OWN:, :]
    staged[2].wait()
    preacts = matmul(blocks[...].reshape(2 * OWN, 2 * OUTS), weights[...], NN)
    for block in range(2):
        for pair in range(4):
            lanes = slice(SLOTS * pair, SLOTS * (pair + 1))
            preact = preacts[OWN * block : OWN * (block + 1), lanes]
            sigmoid_part = jax.nn.sigmoid(preact)
            silu = preact * sigmoid_part
            slope = sigmoid_part * (1.0 + preact * (1.0 - sigmoid_part))
            even = cots[block, 2 * pair].astype(F32)
            odd = cots[block, 2 * pair + 1].astype(F32)
            top = jnp.concatenate([even[:, :FEATS], odd[:, :FEATS]], axis=1)
            bottom = jnp.concatenate([even[:, FEATS:], odd[:, FEATS:]], axis=1)
            slopes = (jnp.concatenate([top, bottom], axis=0) * slope).astype(BF16)
            column = SLOTS * (pair % 2)
            out_tile[pair // 2, OWN * block : OWN * (block + 1), column : column + SLOTS] = slopes
            flat[OWN * block : OWN * (block + 1), lanes] = slopes
            hidden[block, 2 * pair] = fold_halves(silu[:, :FEATS]).astype(BF16)
            hidden[block, 2 * pair + 1] = fold_halves(silu[:, FEATS:]).astype(BF16)
    sent = copies(
        out_sems,
        *[(out_tile.at[chip % 2], slopes_hbm.at[chip]) for chip in range(CHIPS)],
        (flat, flat_hbm),
        (hidden, hidden_hbm),
    )
    for copy in sent:
        copy.wait()


def forward(own_block, other_block, weights):
    return pl.pallas_call(
        forward_kernel,
        in_specs=[HBM, HBM, HBM],
        out_specs=[HBM, HBM, HBM],
        out_shape=[
            jax.ShapeDtypeStruct((CHIPS, 2 * OWN, TILE), BF16),
            jax.ShapeDtypeStruct((2 * OWN, HALF), BF16),
            jax.ShapeDtypeStruct((2, LAYERS // 2, OWN // 2, SLOTS), BF16),
        ],
        scratch_shapes=[
            pltpu.VMEM((LAYERS, 96, SLOTS), BF16),
            pltpu.VMEM((LAYERS, 96, SLOTS), BF16),
            pltpu.VMEM((2 * OUTS, HALF), BF16),
            pltpu.VMEM((2, OWN, 2 * OUTS), BF16),
            pltpu.VMEM((2, LAYERS // 2, OWN // 2, SLOTS), BF16),
            pltpu.VMEM((2, 2 * OWN, TILE), BF16),
            pltpu.VMEM((2 * OWN, HALF), BF16),
            pltpu.VMEM((2, LAYERS // 2, OWN // 2, SLOTS), BF16),
            pltpu.SemaphoreType.DMA((3,)),
            pltpu.SemaphoreType.DMA((CHIPS + 2,)),
        ],
        compiler_params=params(60),
        cost_estimate=cost(2 * 256 * 2048 * 512, 4 << 20),
        name="forward",
    )(own_block, other_block, weights)


def backward_kernel(slopes_ref, hidden_ref, weights_ref, keep_ref, send_ref, keep_hidden, send_hidden, parts):
    core = lax.axis_index("row") % 2
    back = matmul(slopes_ref[...], weights_ref[...], NT)
    parts[0] = back[:OWN, :]
    parts[1] = back[OWN:, :]
    keep_ref[...] = parts[core]
    send_ref[...] = parts[1 - core]
    keep_hidden[...] = hidden_ref[core]
    send_hidden[...] = hidden_ref[1 - core]


def backward(slopes, hidden, weights):
    part = jax.ShapeDtypeStruct((OWN, 2 * OUTS), F32)
    block = jax.ShapeDtypeStruct((LAYERS // 2, OWN // 2, SLOTS), BF16)
    return pl.pallas_call(
        backward_kernel,
        out_shape=[part, part, block, block],
        scratch_shapes=[pltpu.VMEM((2, OWN, 2 * OUTS), F32)],
        compiler_params=params(16),
        cost_estimate=cost(2 * 256 * 2048 * 512, 4 << 20),
        name="backward",
    )(slopes, hidden, weights)


def combine_kernel(mine_ref, theirs_ref, my_hidden, their_hidden, degree_ref, out_ref):
    core = lax.axis_index("row") % 2
    direct = lax.broadcasted_iota(jnp.int32, (OWN, SLOTS), 1) < FEATS
    divisor = jnp.where(direct, 1.0, degree_ref[...])
    for layer in range(LAYERS):
        lanes = slice(SLOTS * layer, SLOTS * (layer + 1))
        back = mine_ref[:, lanes] + theirs_ref[:, lanes]
        out_ref[layer, :OWN, :] = (back / divisor).astype(BF16)
    for layer in range(LAYERS // 2):
        out_ref[8 * core + layer, OWN:, :] = my_hidden[layer]
        out_ref[8 * (1 - core) + layer, OWN:, :] = their_hidden[layer]


def combine(mine, theirs, my_hidden, their_hidden, own_degree):
    return pl.pallas_call(
        combine_kernel,
        out_shape=jax.ShapeDtypeStruct((LAYERS, 96, SLOTS), BF16),
        compiler_params=params(16),
        cost_estimate=cost(1 << 20, 2 << 20),
        name="combine",
    )(mine, theirs, my_hidden, their_hidden, own_degree)


STEPS = 4


def weight_kernel(joined_hbm, slopes_ref, back_hbm, out_ref, joined, back, sems):
    depth = PEERS * OWN // STEPS
    staged = copies(
        sems,
        *[
            (joined_hbm.at[:, depth * i : depth * (i + 1)], joined.at[:, depth * i : depth * (i + 1)])
            for i in range(STEPS)
        ],
        (back_hbm, back),
    )
    part = jnp.zeros((TILE, TILE), F32)
    for i in range(STEPS):
        staged[i].wait()
        rows = slice(depth * i, depth * (i + 1))
        part = part + matmul(joined[:, rows], slopes_ref[rows, :], NN)
    part = part.astype(BF16)
    for layer in range(LAYERS):
        out_ref[layer, 96:112, :] = part[PIECE * layer : PIECE * (layer + 1), :SLOTS]
        out_ref[layer, 112:, :] = part[PIECE * layer : PIECE * (layer + 1), SLOTS:]
    staged[STEPS].wait()
    out_ref[:, :96, :] = back[...]


def weight_parts(joined_cols, slopes_rows, back):
    return pl.pallas_call(
        weight_kernel,
        in_specs=[HBM, VMEM, HBM],
        out_shape=jax.ShapeDtypeStruct((LAYERS, SLOTS, SLOTS), BF16),
        scratch_shapes=[
            pltpu.VMEM((TILE, PEERS * OWN), BF16),
            pltpu.VMEM((LAYERS, 96, SLOTS), BF16),
            pltpu.SemaphoreType.DMA((STEPS + 1,)),
        ],
        compiler_params=params(16),
        cost_estimate=cost(2 * 256 * 2048 * 256, 3 << 20),
        name="weight_parts",
    )(joined_cols, slopes_rows, back)


RETURN_ROWS = 112


def return_kernel(back_ref, recv_hbm, hubs_hbm, out_hbm, recv_ref, hubs_ref, out_ref, in_sems, out_sems):
    staged = copies(in_sems, (recv_hbm, recv_ref), (hubs_hbm, hubs_ref))
    rows = back_ref[:, :OWN, :].astype(F32).reshape(NODES, SLOTS)
    share = rows.T[FEATS:, :].astype(BF16)
    sums = jnp.sum(back_ref[:, 96:, :].astype(F32), axis=0).astype(BF16)
    node = lax.broadcasted_iota(jnp.int32, (NODES, 2 * SLOTS), 0)
    staged[0].wait()
    sent = []
    for pair in range(PEERS // 2):
        values = matmul(share, one_hot(node == pair_lanes(recv_ref, pair)), NN).astype(BF16)
        for side in range(2):
            peer = 2 * pair + side
            out_ref[peer, :FEATS, :] = values[:, SLOTS * side : SLOTS * (side + 1)]
            out_ref[peer, ROWS:, :] = sums
        if pair == 3:
            staged[1].wait()
            terms = matmul(share, hubs_ref[...], NT).T
            high = terms.astype(BF16).astype(F32)
            both = jnp.concatenate([high, terms - high], axis=1)
            out_ref[:, FEATS:ROWS, :] = both.reshape(PEERS, HUBS_OWN, SLOTS).astype(BF16)
        if pair % 4 == 3:
            part = pl.ds(2 * pair - 6, 8)
            copy = pltpu.make_async_copy(out_ref.at[part], out_hbm.at[part], out_sems.at[pair // 4])
            copy.start()
            sent.append(copy)
    for copy in sent:
        copy.wait()


def return_slots(back_block, recv_lanes, hubs):
    return pl.pallas_call(
        return_kernel,
        in_specs=[VMEM, HBM, HBM],
        out_specs=HBM,
        out_shape=jax.ShapeDtypeStruct((PEERS, RETURN_ROWS, SLOTS), BF16),
        scratch_shapes=[
            pltpu.VMEM((PEERS, SLOTS), jnp.int32),
            pltpu.VMEM((HUBS, NODES), BF16),
            pltpu.VMEM((PEERS, RETURN_ROWS, SLOTS), BF16),
            pltpu.SemaphoreType.DMA((2,)),
            pltpu.SemaphoreType.DMA((4,)),
        ],
        compiler_params=params(60),
        cost_estimate=cost(2 * 256 * 4608 * 1024, 3 << 20),
        name="return_slots",
    )(back_block, recv_lanes, hubs)


def local_kernel(back_ref, local_ref, base_ref, hidden_ref):
    columns = back_ref[:, :OWN, :].astype(F32).reshape(NODES, SLOTS).T
    share = columns[FEATS:, :].astype(BF16)
    base_ref[...] = columns[:FEATS, :] + matmul(share, local_ref[...], NT)
    folded = back_ref[:, OWN:96, :].astype(F32)
    rows = jnp.concatenate([folded[:, :, :FEATS], folded[:, :, FEATS:]], axis=1)
    hidden_ref[...] = rows.reshape(NODES, FEATS).T.astype(BF16)


def local_grads(back_block, local):
    return pl.pallas_call(
        local_kernel,
        out_shape=[
            jax.ShapeDtypeStruct((FEATS, NODES), F32),
            jax.ShapeDtypeStruct((FEATS, NODES), BF16),
        ],
        compiler_params=params(60),
        cost_estimate=cost(2 * 256 * 1024 * 1024, 3 << 20),
        name="local_grads",
    )(back_block, local)


SPREAD = 256


def spread_kernel(
    back_ref, send_hbm, hub_hbm, base_hbm, out_ref, self_hbm, neigh_hbm,
    send_ref, hub_ref, base_ref, grads_ref, slots, in_sems, out_sems,
):
    staged = copies(in_sems, (send_hbm, send_ref), (hub_hbm, hub_ref), (base_hbm, base_ref))
    for peer in range(PEERS):
        slots[:, SLOTS * peer : SLOTS * (peer + 1)] = back_ref[peer, :FEATS, :]
        grads = back_ref[peer, ROWS:, :].astype(F32)
        slice_of, outs = peer // 4, 2 * (peer % 2) + peer // 2 % 2
        rows = slice(PIECE * slice_of, PIECE * (slice_of + 1))
        grads_ref[rows, TILE * outs : TILE * outs + SLOTS] = grads[:PIECE, :]
        grads_ref[rows, TILE * outs + SLOTS : TILE * (outs + 1)] = grads[PIECE:, :]
    sent = copies(
        out_sems, (grads_ref.at[:FEATS], self_hbm), (grads_ref.at[FEATS:], neigh_hbm)
    )
    sums = jnp.sum(back_ref[:, FEATS:ROWS, :].astype(F32), axis=0)
    total = sums[:, :FEATS] + sums[:, FEATS:]
    high = total.astype(BF16).astype(F32)
    hub_high = high.T.astype(BF16)
    hub_low = (total - high).T.astype(BF16)
    for copy in staged:
        copy.wait()
    for tile in range(NODES // SPREAD):
        lanes = slice(SPREAD * tile, SPREAD * (tile + 1))
        node = lax.broadcasted_iota(jnp.int32, (SPREAD, 2 * SLOTS), 0) + SPREAD * tile
        grad = base_ref[:, lanes]
        for pair in range(PEERS // 2):
            grad = grad + matmul(
                slots[:, 2 * SLOTS * pair : 2 * SLOTS * (pair + 1)],
                one_hot(node == pair_lanes(send_ref, pair)),
                NT,
            )
        hub_node = lax.broadcasted_iota(jnp.int32, (SPREAD, HUBS_OWN), 0) + SPREAD * tile
        hub_hot = one_hot(hub_node == hub_ref[...])
        grad = grad + matmul(hub_high, hub_hot, NT) + matmul(hub_low, hub_hot, NT)
        out_ref[:, lanes] = grad.astype(BF16)
    for copy in sent:
        copy.wait()


def spread_grads(returned, send_lanes, hub_own, base):
    return pl.pallas_call(
        spread_kernel,
        in_specs=[VMEM, HBM, HBM, HBM],
        out_specs=[VMEM, HBM, HBM],
        out_shape=[
            jax.ShapeDtypeStruct((FEATS, NODES), BF16),
            jax.ShapeDtypeStruct((FEATS, OUTS), F32),
            jax.ShapeDtypeStruct((FEATS, OUTS), F32),
        ],
        scratch_shapes=[
            pltpu.VMEM((PEERS, SLOTS), jnp.int32),
            pltpu.VMEM((1, HUBS_OWN), jnp.int32),
            pltpu.VMEM((FEATS, NODES), F32),
            pltpu.VMEM((2 * FEATS, OUTS), F32),
            pltpu.VMEM((FEATS, PEERS * SLOTS), BF16),
            pltpu.SemaphoreType.DMA((3,)),
            pltpu.SemaphoreType.DMA((2,)),
        ],
        compiler_params=params(16),
        cost_estimate=cost(2 * 256 * 4224 * 1024, 2 << 20),
        name="spread_grads",
    )(returned, send_lanes, hub_own, base)


SAME_CORE = [list(range(core, PEERS, 2)) for core in range(2)]


def exchange(blocks, axis, groups=None):
    return lax.all_to_all(blocks, axis, 0, 0, axis_index_groups=groups, tiled=True)


def other_core(block):
    return lax.ppermute(block, "row", [(i, i ^ 1) for i in range(PEERS)])


def per_device(feats, w_self, w_neigh, cotangent, loc_nbr, send_rows, recv_node, hub_rows, hub_nbr):
    send_lanes = send_rows.reshape(PEERS, SLOTS)
    recv_lanes = recv_node.reshape(PEERS, SLOTS)
    hub_own = hub_rows[None, :]
    half = HALF * (lax.axis_index("row") % 2)
    weights = lax.all_gather(
        lax.dynamic_slice_in_dim(jnp.concatenate([w_self, w_neigh], axis=0), half, HALF, 1),
        "col",
        axis=0,
        tiled=True,
    )
    incoming = exchange(gather_slots(feats, send_lanes, hub_own), "row")
    hub_lanes = hub_nbr.T
    local, hubs, local_sum = build_counts(feats, loc_nbr.T, hub_lanes)
    outgoing, degree = aggregate(feats, incoming, recv_lanes, local_sum, hub_lanes, cotangent)
    node_block = exchange(outgoing, "col")
    own_degree = lax.dynamic_slice_in_dim(degree[0], OWN * lax.axis_index("col"), OWN)[:, None]
    joined_cols = exchange(regroup(node_block), "row").reshape(PEERS * OWN, TILE).T
    slopes_out, slopes, hidden = forward(node_block, other_core(node_block), weights)
    slopes_rows = exchange(slopes_out, "row", SAME_CORE).reshape(PEERS * OWN, TILE)
    mine, theirs, my_hidden, their_hidden = backward(slopes, hidden, weights)
    back = combine(mine, other_core(theirs), my_hidden, other_core(their_hidden), own_degree)
    back_block = exchange(weight_parts(joined_cols, slopes_rows, back), "col")
    returned = exchange(return_slots(back_block, recv_lanes, hubs), "row")
    base, hidden_out = local_grads(back_block, local)
    grad_feats, grad_self, grad_neigh = spread_grads(returned, send_lanes, hub_own, base)
    return (hidden_out, grad_feats, grad_self, grad_neigh)


def solution(mesh):
    return jax.shard_map(
        per_device,
        mesh=mesh,
        in_specs=(
            P("col", "row"),
            P("col", None),
            P("col", None),
            P("col", "row"),
            P("row", None),
            P("row", None, None),
            P("row", None, None),
            P("row"),
            P("row", None),
        ),
        out_specs=(P("col", "row"), P("col", "row"), P("col", None), P("col", None)),
        check_vma=False,
    )
```

```python
import jax
import jax.numpy as jnp
from jax import lax
from jax.experimental import pallas as pl
from jax.experimental.pallas import tpu as pltpu
from jax.sharding import PartitionSpec as P

NODES = 1024
FEATS = 64
PEERS = 32
SLOTS = 128
HUBS_OWN = 16
HUBS = 512
ROWS = 80
LAYERS = 16
OWN = 64
OUTS = 1024
BF16 = jnp.bfloat16
F32 = jnp.float32
NT = (((1,), (1,)), ((), ()))
NN = (((1,), (0,)), ((), ()))
MIB = 1 << 20


def params(mib):
    return pltpu.CompilerParams(vmem_limit_bytes=mib * MIB)


def cost(flops, moved):
    return pl.CostEstimate(flops=flops, bytes_accessed=moved, transcendentals=0)


def whole(shape):
    return pl.BlockSpec(shape, lambda *_: (0,) * len(shape))


HBM = pl.BlockSpec(memory_space=pltpu.HBM)
VMEM = pl.BlockSpec(memory_space=pltpu.VMEM)


def copies(sems, *pairs):
    started = []
    for i, (source, target) in enumerate(pairs):
        copy = pltpu.make_async_copy(source, target, sems.at[i])
        copy.start()
        started.append(copy)
    return started


def one_hot(mask):
    return jnp.where(mask, 1.0, 0.0).astype(BF16)


def matmul(a, b, dims):
    return lax.dot_general(a, b, dims, preferred_element_type=F32)


def pair_lanes(ref, pair):
    return jnp.concatenate([ref[2 * pair : 2 * pair + 1, :], ref[2 * pair + 1 : 2 * pair + 2, :]], axis=1)


def gather_kernel(x_hbm, send_hbm, hub_hbm, out_ref, x_ref, send_ref, hub_ref, sems):
    for copy in copies(sems, (x_hbm, x_ref), (send_hbm, send_ref), (hub_hbm, hub_ref)):
        copy.wait()
    x = x_ref[...]
    node = lax.broadcasted_iota(jnp.int32, (NODES, 2 * SLOTS), 0)
    hub_node = lax.broadcasted_iota(jnp.int32, (NODES, HUBS_OWN), 0)
    hub_feats = matmul(x, one_hot(hub_node == hub_ref[...]), NN)
    hub_rows = hub_feats.T
    hub_block = jnp.concatenate([hub_rows, jnp.zeros_like(hub_rows)], axis=1).astype(BF16)
    for pair in range(PEERS // 2):
        picked = matmul(x, one_hot(node == pair_lanes(send_ref, pair)), NN).astype(BF16)
        out_ref[2 * pair, :FEATS, :] = picked[:, :SLOTS]
        out_ref[2 * pair + 1, :FEATS, :] = picked[:, SLOTS:]
        out_ref[2 * pair, FEATS:, :] = hub_block
        out_ref[2 * pair + 1, FEATS:, :] = hub_block


def gather_slots(feats, send_lanes, hub_own):
    return pl.pallas_call(
        gather_kernel,
        in_specs=[HBM, HBM, HBM],
        out_shape=jax.ShapeDtypeStruct((PEERS, ROWS, SLOTS), BF16),
        scratch_shapes=[
            pltpu.VMEM((FEATS, NODES), BF16),
            pltpu.VMEM((PEERS, SLOTS), jnp.int32),
            pltpu.VMEM((1, HUBS_OWN), jnp.int32),
            pltpu.SemaphoreType.DMA((3,)),
        ],
        compiler_params=params(60),
        cost_estimate=cost(2 * 256 * 4096 * 1024, 1 << 20),
        name="gather_slots",
    )(feats, send_lanes, hub_own)


BUILD = 256
KEPT = 512


def counts_of(nbr_ref, rows):
    first = lax.broadcasted_iota(jnp.int32, (rows, nbr_ref.shape[1]), 0)
    counts = jnp.zeros(first.shape, F32)
    for k in range(nbr_ref.shape[0]):
        counts = counts + jnp.where(first == nbr_ref[k : k + 1, :], 1.0, 0.0)
    return counts.astype(BF16)


def build_kernel(x_ref, loc_ref, hub_ref, local_ref, hubs_ref, sum_ref):
    counts = counts_of(loc_ref, NODES)
    local_ref[...] = counts
    hubs_ref[...] = counts_of(hub_ref, HUBS)
    sum_ref[...] = matmul(x_ref[...], counts, NN)


def build_counts(feats, loc_lanes, hub_lanes):
    return pl.pallas_call(
        build_kernel,
        grid=(NODES // BUILD,),
        in_specs=[
            whole((FEATS, NODES)),
            pl.BlockSpec((loc_lanes.shape[0], BUILD), lambda i: (0, i)),
            pl.BlockSpec((hub_lanes.shape[0], BUILD), lambda i: (0, i)),
        ],
        out_specs=[
            pl.BlockSpec((NODES, BUILD), lambda i: (0, i)),
            pl.BlockSpec((HUBS, BUILD), lambda i: (0, i)),
            pl.BlockSpec((FEATS, BUILD), lambda i: (0, i)),
        ],
        out_shape=[
            jax.ShapeDtypeStruct((NODES, NODES), BF16),
            jax.ShapeDtypeStruct((HUBS, NODES), BF16),
            jax.ShapeDtypeStruct((KEPT, NODES), F32),
        ],
        compiler_params=params(60),
        cost_estimate=cost(1 << 30, 4 << 20),
        name="build_counts",
    )(feats, loc_lanes, hub_lanes)


AGG = 256


def fold_halves(block):
    return jnp.concatenate([block[: OWN // 2, :], block[OWN // 2 :, :]], axis=1)


NEIGHBOURS = 10.0


def aggregate_kernel(
    x_hbm, inc_ref, recv_hbm, sum_hbm, hub_hbm, cot_hbm, out_ref, degree_ref,
    slots, table, recv_ref, hub_ref, x_ref, cot_ref, sum_ref, sems,
):
    staged = copies(
        sems,
        (recv_hbm, recv_ref),
        (hub_hbm, hub_ref),
        (x_hbm, x_ref),
        (cot_hbm, cot_ref),
        (sum_hbm.at[:FEATS], sum_ref),
    )
    for peer in range(PEERS):
        slots[:FEATS, SLOTS * peer : SLOTS * (peer + 1)] = inc_ref[peer, :FEATS, :]
    slots[FEATS:, :] = jnp.ones((16, PEERS * SLOTS), BF16)
    rows = inc_ref[:, FEATS:, :].astype(F32).reshape(HUBS, SLOTS)
    table[...] = rows.T[:FEATS, :].astype(BF16)
    staged[0].wait()
    for tile in range(NODES // AGG):
        lanes = slice(AGG * tile, AGG * (tile + 1))
        node = lax.broadcasted_iota(jnp.int32, (AGG, 2 * SLOTS), 0) + AGG * tile
        remote = jnp.zeros((ROWS, AGG), F32)
        for pair in range(PEERS // 2):
            remote = remote + matmul(
                slots[:, 2 * SLOTS * pair : 2 * SLOTS * (pair + 1)],
                one_hot(node == pair_lanes(recv_ref, pair)),
                NT,
            )
        if tile == 0:
            for copy in staged[1:]:
                copy.wait()
        hubs = counts_of(hub_ref[:, lanes], HUBS)
        total = remote[:FEATS, :] + sum_ref[:, lanes] + matmul(table[...], hubs, NN)
        degree = remote[FEATS : FEATS + 8, :] + NEIGHBOURS
        degree_ref[:, lanes] = degree
        mean = (total / degree[0:1, :]).T
        nodes = jnp.concatenate([x_ref[:, lanes].astype(F32).T, mean], axis=1).astype(BF16)
        slopes = cot_ref[:, lanes].astype(F32).T
        for part in range(AGG // OWN):
            layer = AGG // OWN * tile + part
            out_ref[layer, :OWN, :] = nodes[OWN * part : OWN * (part + 1), :]
            out_ref[layer, OWN:, :] = fold_halves(slopes[OWN * part : OWN * (part + 1), :]).astype(BF16)


def aggregate(feats, incoming, recv_lanes, local_sum, hub_lanes, cotangent):
    return pl.pallas_call(
        aggregate_kernel,
        out_shape=[
            jax.ShapeDtypeStruct((LAYERS, 96, SLOTS), BF16),
            jax.ShapeDtypeStruct((8, NODES), F32),
        ],
        in_specs=[HBM, VMEM, HBM, HBM, HBM, HBM],
        scratch_shapes=[
            pltpu.VMEM((ROWS, PEERS * SLOTS), BF16),
            pltpu.VMEM((FEATS, HUBS), BF16),
            pltpu.VMEM((PEERS, SLOTS), jnp.int32),
            pltpu.VMEM((2, NODES), jnp.int32),
            pltpu.VMEM((FEATS, NODES), BF16),
            pltpu.VMEM((FEATS, NODES), BF16),
            pltpu.VMEM((FEATS, NODES), F32),
            pltpu.SemaphoreType.DMA((5,)),
        ],
        compiler_params=params(52),
        cost_estimate=cost(2 * 256 * 5632 * 1024, 3 << 20),
        name="aggregate",
    )(feats, incoming, recv_lanes, local_sum, hub_lanes, cotangent)


PIECE = 16
TILE = 256


def regroup_kernel(inc_ref, out_ref):
    group = lax.broadcasted_iota(jnp.int32, (OWN, SLOTS), 1) // PIECE
    for half in range(2):
        blocks = [inc_ref[8 * half + i, :OWN, :].astype(F32) for i in range(8)]
        for slice_of in range(8):
            tile = jnp.zeros((OWN, SLOTS), F32)
            for i in range(8):
                moved = blocks[i]
                if i != slice_of:
                    moved = pltpu.roll(moved, (PIECE * (i - slice_of)) % SLOTS, 1)
                tile = jnp.where(group == i, moved, tile)
            tile = tile.astype(BF16)
            for outs in range(4):
                out_ref[4 * slice_of + outs, :, SLOTS * half : SLOTS * (half + 1)] = tile


def regroup(node_block):
    return pl.pallas_call(
        regroup_kernel,
        out_shape=jax.ShapeDtypeStruct((PEERS, OWN, TILE), BF16),
        compiler_params=params(16),
        cost_estimate=cost(1 << 24, 2 << 20),
        name="regroup",
    )(node_block)


HALF = OUTS // 2
CHIPS = PEERS // 2


def prepare_kernel(own_block, other_block, joined_ref, cot_ref):
    core = lax.axis_index("row") % 2
    for layer in range(LAYERS):
        lanes = slice(SLOTS * layer, SLOTS * (layer + 1))
        joined_ref[core, :, lanes] = own_block[layer, :OWN, :]
        joined_ref[1 - core, :, lanes] = other_block[layer, :OWN, :]
    for side, block in ((core, own_block), (1 - core, other_block)):
        for pair in range(LAYERS // 4):
            even = block[8 * core + 2 * pair, OWN:, :].astype(F32)
            odd = block[8 * core + 2 * pair + 1, OWN:, :].astype(F32)
            top = jnp.concatenate([even[:, :FEATS], odd[:, :FEATS]], axis=1)
            bottom = jnp.concatenate([even[:, FEATS:], odd[:, FEATS:]], axis=1)
            cot_ref[side, :, SLOTS * pair : SLOTS * (pair + 1)] = jnp.concatenate(
                [top, bottom], axis=0
            ).astype(BF16)


def prepare(own_block, other_block):
    return pl.pallas_call(
        prepare_kernel,
        out_shape=[
            jax.ShapeDtypeStruct((2, OWN, 2 * OUTS), BF16),
            jax.ShapeDtypeStruct((2, OWN, HALF), BF16),
        ],
        compiler_params=params(16),
        cost_estimate=cost(1 << 20, 2 << 20),
        name="prepare",
    )(own_block, other_block)


def forward_kernel(
    joined_hbm, cot_hbm, weights_hbm, slopes_hbm, flat_hbm, hidden_hbm,
    joined, cots, weights, out_tile, flat, hidden, in_sems, out_sems,
):
    staged = copies(
        in_sems,
        (joined_hbm, joined),
        (weights_hbm.at[:, :TILE], weights.at[:, :TILE]),
        (cot_hbm, cots),
        (weights_hbm.at[:, TILE:], weights.at[:, TILE:]),
    )
    staged[0].wait()
    sent = []
    for side in range(2):
        staged[2 * side + 1].wait()
        columns = slice(TILE * side, TILE * (side + 1))
        preact = matmul(joined[...].reshape(2 * OWN, 2 * OUTS), weights[:, columns], NN)
        if side == 0:
            staged[2].wait()
        sigmoid_part = jax.nn.sigmoid(preact)
        silu = preact * sigmoid_part
        slope = sigmoid_part * (1.0 + preact * (1.0 - sigmoid_part))
        cot = cots[:, :, columns].reshape(2 * OWN, TILE).astype(F32)
        slopes = (cot * slope).astype(BF16)
        out_tile[side] = slopes
        for chip in range(side, CHIPS, 2):
            copy = pltpu.make_async_copy(out_tile.at[side], slopes_hbm.at[chip], out_sems.at[chip])
            copy.start()
            sent.append(copy)
        flat[:, columns] = slopes
        for block in range(2):
            for layer in range(4):
                tile = silu[OWN * block : OWN * (block + 1), FEATS * layer : FEATS * (layer + 1)]
                hidden[block, 4 * side + layer] = fold_halves(tile).astype(BF16)
    for i, (source, target) in enumerate(((flat, flat_hbm), (hidden, hidden_hbm))):
        copy = pltpu.make_async_copy(source, target, out_sems.at[CHIPS + i])
        copy.start()
        sent.append(copy)
    for copy in sent:
        copy.wait()


def forward(joined, cots, weights):
    return pl.pallas_call(
        forward_kernel,
        in_specs=[HBM, HBM, HBM],
        out_specs=[HBM, HBM, HBM],
        out_shape=[
            jax.ShapeDtypeStruct((CHIPS, 2 * OWN, TILE), BF16),
            jax.ShapeDtypeStruct((2 * OWN, HALF), BF16),
            jax.ShapeDtypeStruct((2, LAYERS // 2, OWN // 2, SLOTS), BF16),
        ],
        scratch_shapes=[
            pltpu.VMEM((2, OWN, 2 * OUTS), BF16),
            pltpu.VMEM((2, OWN, HALF), BF16),
            pltpu.VMEM((2 * OUTS, HALF), BF16),
            pltpu.VMEM((2, 2 * OWN, TILE), BF16),
            pltpu.VMEM((2 * OWN, HALF), BF16),
            pltpu.VMEM((2, LAYERS // 2, OWN // 2, SLOTS), BF16),
            pltpu.SemaphoreType.DMA((4,)),
            pltpu.SemaphoreType.DMA((CHIPS + 2,)),
        ],
        compiler_params=params(60),
        cost_estimate=cost(2 * 256 * 2048 * 512, 4 << 20),
        name="forward",
    )(joined, cots, weights)


def backward_kernel(slopes_ref, hidden_ref, weights_ref, keep_ref, send_ref, keep_hidden, send_hidden, parts):
    core = lax.axis_index("row") % 2
    back = matmul(slopes_ref[...], weights_ref[...], NT)
    parts[0] = back[:OWN, :]
    parts[1] = back[OWN:, :]
    keep_ref[...] = parts[core]
    send_ref[...] = parts[1 - core]
    keep_hidden[...] = hidden_ref[core]
    send_hidden[...] = hidden_ref[1 - core]


def backward(slopes, hidden, weights):
    part = jax.ShapeDtypeStruct((OWN, 2 * OUTS), F32)
    block = jax.ShapeDtypeStruct((LAYERS // 2, OWN // 2, SLOTS), BF16)
    return pl.pallas_call(
        backward_kernel,
        out_shape=[part, part, block, block],
        scratch_shapes=[pltpu.VMEM((2, OWN, 2 * OUTS), F32)],
        compiler_params=params(16),
        cost_estimate=cost(2 * 256 * 2048 * 512, 4 << 20),
        name="backward",
    )(slopes, hidden, weights)


def combine_kernel(mine_ref, theirs_ref, my_hidden, their_hidden, degree_ref, out_ref):
    core = lax.axis_index("row") % 2
    direct = lax.broadcasted_iota(jnp.int32, (OWN, SLOTS), 1) < FEATS
    divisor = jnp.where(direct, 1.0, degree_ref[...])
    for layer in range(LAYERS):
        lanes = slice(SLOTS * layer, SLOTS * (layer + 1))
        back = mine_ref[:, lanes] + theirs_ref[:, lanes]
        out_ref[layer, :OWN, :] = (back / divisor).astype(BF16)
    for layer in range(LAYERS // 2):
        out_ref[8 * core + layer, OWN:, :] = my_hidden[layer]
        out_ref[8 * (1 - core) + layer, OWN:, :] = their_hidden[layer]


def combine(mine, theirs, my_hidden, their_hidden, own_degree):
    return pl.pallas_call(
        combine_kernel,
        out_shape=jax.ShapeDtypeStruct((LAYERS, 96, SLOTS), BF16),
        compiler_params=params(16),
        cost_estimate=cost(1 << 20, 2 << 20),
        name="combine",
    )(mine, theirs, my_hidden, their_hidden, own_degree)


STEPS = 4


def weight_kernel(joined_hbm, slopes_ref, back_hbm, out_ref, joined, back, sems):
    depth = PEERS * OWN // STEPS
    staged = copies(
        sems,
        *[
            (joined_hbm.at[:, depth * i : depth * (i + 1)], joined.at[:, depth * i : depth * (i + 1)])
            for i in range(STEPS)
        ],
        (back_hbm, back),
    )
    part = jnp.zeros((TILE, TILE), F32)
    for i in range(STEPS):
        staged[i].wait()
        rows = slice(depth * i, depth * (i + 1))
        part = part + matmul(joined[:, rows], slopes_ref[rows, :], NN)
    part = part.astype(BF16)
    for layer in range(LAYERS):
        out_ref[layer, 96:112, :] = part[PIECE * layer : PIECE * (layer + 1), :SLOTS]
        out_ref[layer, 112:, :] = part[PIECE * layer : PIECE * (layer + 1), SLOTS:]
    staged[STEPS].wait()
    out_ref[:, :96, :] = back[...]


def weight_parts(joined_cols, slopes_rows, back):
    return pl.pallas_call(
        weight_kernel,
        in_specs=[HBM, VMEM, HBM],
        out_shape=jax.ShapeDtypeStruct((LAYERS, SLOTS, SLOTS), BF16),
        scratch_shapes=[
            pltpu.VMEM((TILE, PEERS * OWN), BF16),
            pltpu.VMEM((LAYERS, 96, SLOTS), BF16),
            pltpu.SemaphoreType.DMA((STEPS + 1,)),
        ],
        compiler_params=params(16),
        cost_estimate=cost(2 * 256 * 2048 * 256, 3 << 20),
        name="weight_parts",
    )(joined_cols, slopes_rows, back)


RETURN_ROWS = 112


def return_kernel(
    back_hbm, recv_hbm, hubs_hbm, out_hbm,
    back_ref, part_ref, recv_ref, hubs_ref, out_ref, in_sems, out_sems,
):
    staged = copies(
        in_sems,
        (recv_hbm, recv_ref),
        (hubs_hbm, hubs_ref),
        (back_hbm.at[:, :OWN, :], back_ref),
        (back_hbm.at[:, 96:, :], part_ref),
    )
    node = lax.broadcasted_iota(jnp.int32, (NODES, 2 * SLOTS), 0)
    staged[2].wait()
    share = back_ref[...].astype(F32).reshape(NODES, SLOTS).T[FEATS:, :].astype(BF16)
    staged[0].wait()
    staged[3].wait()
    sums = jnp.sum(part_ref[...].astype(F32), axis=0).astype(BF16)
    sent = []
    for pair in range(PEERS // 2):
        values = matmul(share, one_hot(node == pair_lanes(recv_ref, pair)), NN).astype(BF16)
        for side in range(2):
            peer = 2 * pair + side
            out_ref[peer, :FEATS, :] = values[:, SLOTS * side : SLOTS * (side + 1)]
            out_ref[peer, ROWS:, :] = sums
        if pair == 3:
            staged[1].wait()
            terms = matmul(share, hubs_ref[...], NT).T
            high = terms.astype(BF16).astype(F32)
            both = jnp.concatenate([high, terms - high], axis=1)
            out_ref[:, FEATS:ROWS, :] = both.reshape(PEERS, HUBS_OWN, SLOTS).astype(BF16)
        if pair % 4 == 3:
            part = pl.ds(2 * pair - 6, 8)
            copy = pltpu.make_async_copy(out_ref.at[part], out_hbm.at[part], out_sems.at[pair // 4])
            copy.start()
            sent.append(copy)
    for copy in sent:
        copy.wait()


def return_slots(back_block, recv_lanes, hubs):
    return pl.pallas_call(
        return_kernel,
        in_specs=[HBM, HBM, HBM],
        out_specs=HBM,
        out_shape=jax.ShapeDtypeStruct((PEERS, RETURN_ROWS, SLOTS), BF16),
        scratch_shapes=[
            pltpu.VMEM((LAYERS, OWN, SLOTS), BF16),
            pltpu.VMEM((LAYERS, 32, SLOTS), BF16),
            pltpu.VMEM((PEERS, SLOTS), jnp.int32),
            pltpu.VMEM((HUBS, NODES), BF16),
            pltpu.VMEM((PEERS, RETURN_ROWS, SLOTS), BF16),
            pltpu.SemaphoreType.DMA((4,)),
            pltpu.SemaphoreType.DMA((4,)),
        ],
        compiler_params=params(60),
        cost_estimate=cost(2 * 256 * 4608 * 1024, 3 << 20),
        name="return_slots",
    )(back_block, recv_lanes, hubs)


def local_kernel(back_ref, local_ref, base_hbm, hidden_ref, base_ref, sems):
    columns = back_ref[:, :OWN, :].astype(F32).reshape(NODES, SLOTS).T
    share = columns[FEATS:, :].astype(BF16)
    base_ref[...] = columns[:FEATS, :] + matmul(share, local_ref[...], NT)
    (sent,) = copies(sems, (base_ref, base_hbm.at[:FEATS]))
    folded = back_ref[:, OWN:96, :].astype(F32)
    rows = jnp.concatenate([folded[:, :, :FEATS], folded[:, :, FEATS:]], axis=1)
    hidden_ref[...] = rows.reshape(NODES, FEATS).T.astype(BF16)
    sent.wait()


def local_grads(back_block, local):
    return pl.pallas_call(
        local_kernel,
        out_specs=[HBM, VMEM],
        out_shape=[
            jax.ShapeDtypeStruct((KEPT, NODES), F32),
            jax.ShapeDtypeStruct((FEATS, NODES), BF16),
        ],
        scratch_shapes=[pltpu.VMEM((FEATS, NODES), F32), pltpu.SemaphoreType.DMA((1,))],
        compiler_params=params(60),
        cost_estimate=cost(2 * 256 * 1024 * 1024, 3 << 20),
        name="local_grads",
    )(back_block, local)


SPREAD = 256


def spread_kernel(
    back_ref, send_hbm, hub_hbm, base_hbm, out_ref, self_hbm, neigh_hbm,
    send_ref, hub_ref, base_ref, grads_ref, slots, in_sems, out_sems,
):
    staged = copies(in_sems, (send_hbm, send_ref), (hub_hbm, hub_ref), (base_hbm.at[:FEATS], base_ref))
    for peer in range(PEERS):
        slots[:, SLOTS * peer : SLOTS * (peer + 1)] = back_ref[peer, :FEATS, :]
        grads = back_ref[peer, ROWS:, :].astype(F32)
        slice_of, outs = peer // 4, 2 * (peer % 2) + peer // 2 % 2
        rows = slice(PIECE * slice_of, PIECE * (slice_of + 1))
        grads_ref[rows, TILE * outs : TILE * outs + SLOTS] = grads[:PIECE, :]
        grads_ref[rows, TILE * outs + SLOTS : TILE * (outs + 1)] = grads[PIECE:, :]
    sent = copies(
        out_sems, (grads_ref.at[:FEATS], self_hbm), (grads_ref.at[FEATS:], neigh_hbm)
    )
    sums = jnp.sum(back_ref[:, FEATS:ROWS, :].astype(F32), axis=0)
    total = sums[:, :FEATS] + sums[:, FEATS:]
    high = total.astype(BF16).astype(F32)
    hub_high = high.T.astype(BF16)
    hub_low = (total - high).T.astype(BF16)
    for copy in staged:
        copy.wait()
    for tile in range(NODES // SPREAD):
        lanes = slice(SPREAD * tile, SPREAD * (tile + 1))
        node = lax.broadcasted_iota(jnp.int32, (SPREAD, 2 * SLOTS), 0) + SPREAD * tile
        grad = base_ref[:, lanes]
        for pair in range(PEERS // 2):
            grad = grad + matmul(
                slots[:, 2 * SLOTS * pair : 2 * SLOTS * (pair + 1)],
                one_hot(node == pair_lanes(send_ref, pair)),
                NT,
            )
        hub_node = lax.broadcasted_iota(jnp.int32, (SPREAD, HUBS_OWN), 0) + SPREAD * tile
        hub_hot = one_hot(hub_node == hub_ref[...])
        grad = grad + matmul(hub_high, hub_hot, NT) + matmul(hub_low, hub_hot, NT)
        out_ref[:, lanes] = grad.astype(BF16)
    for copy in sent:
        copy.wait()


def spread_grads(returned, send_lanes, hub_own, base):
    return pl.pallas_call(
        spread_kernel,
        in_specs=[VMEM, HBM, HBM, HBM],
        out_specs=[VMEM, HBM, HBM],
        out_shape=[
            jax.ShapeDtypeStruct((FEATS, NODES), BF16),
            jax.ShapeDtypeStruct((FEATS, OUTS), F32),
            jax.ShapeDtypeStruct((FEATS, OUTS), F32),
        ],
        scratch_shapes=[
            pltpu.VMEM((PEERS, SLOTS), jnp.int32),
            pltpu.VMEM((1, HUBS_OWN), jnp.int32),
            pltpu.VMEM((FEATS, NODES), F32),
            pltpu.VMEM((2 * FEATS, OUTS), F32),
            pltpu.VMEM((FEATS, PEERS * SLOTS), BF16),
            pltpu.SemaphoreType.DMA((3,)),
            pltpu.SemaphoreType.DMA((2,)),
        ],
        compiler_params=params(52),
        cost_estimate=cost(2 * 256 * 4224 * 1024, 2 << 20),
        name="spread_grads",
    )(returned, send_lanes, hub_own, base)


SAME_CORE = [list(range(core, PEERS, 2)) for core in range(2)]


def exchange(blocks, axis, groups=None):
    return lax.all_to_all(blocks, axis, 0, 0, axis_index_groups=groups, tiled=True)


def other_core(block):
    return lax.ppermute(block, "row", [(i, i ^ 1) for i in range(PEERS)])


def per_device(feats, w_self, w_neigh, cotangent, loc_nbr, send_rows, recv_node, hub_rows, hub_nbr):
    send_lanes = send_rows.reshape(PEERS, SLOTS)
    recv_lanes = recv_node.reshape(PEERS, SLOTS)
    hub_own = hub_rows[None, :]
    half = HALF * (lax.axis_index("row") % 2)
    weights = lax.all_gather(
        lax.dynamic_slice_in_dim(jnp.concatenate([w_self, w_neigh], axis=0), half, HALF, 1),
        "col",
        axis=0,
        tiled=True,
    )
    incoming = exchange(gather_slots(feats, send_lanes, hub_own), "row")
    hub_lanes = hub_nbr.T
    local, hubs, local_sum = build_counts(feats, loc_nbr.T, hub_lanes)
    outgoing, degree = aggregate(feats, incoming, recv_lanes, local_sum, hub_lanes, cotangent)
    node_block = exchange(outgoing, "col")
    own_degree = lax.dynamic_slice_in_dim(degree[0], OWN * lax.axis_index("col"), OWN)[:, None]
    joined_cols = exchange(regroup(node_block), "row").reshape(PEERS * OWN, TILE).T
    joined, cots = prepare(node_block, other_core(node_block))
    slopes_out, slopes, hidden = forward(joined, cots, weights)
    slopes_rows = exchange(slopes_out, "row", SAME_CORE).reshape(PEERS * OWN, TILE)
    mine, theirs, my_hidden, their_hidden = backward(slopes, hidden, weights)
    back = combine(mine, other_core(theirs), my_hidden, other_core(their_hidden), own_degree)
    back_block = exchange(weight_parts(joined_cols, slopes_rows, back), "col")
    returned = exchange(return_slots(back_block, recv_lanes, hubs), "row")
    base, hidden_out = local_grads(back_block, local)
    grad_feats, grad_self, grad_neigh = spread_grads(returned, send_lanes, hub_own, base)
    return (hidden_out, grad_feats, grad_self, grad_neigh)


def solution(mesh):
    return jax.shard_map(
        per_device,
        mesh=mesh,
        in_specs=(
            P("col", "row"),
            P("col", None),
            P("col", None),
            P("col", "row"),
            P("row", None),
            P("row", None, None),
            P("row", None, None),
            P("row"),
            P("row", None),
        ),
        out_specs=(P("col", "row"), P("col", "row"), P("col", None), P("col", None)),
        check_vma=False,
    )
```

```python
import jax
import jax.numpy as jnp
from jax import lax
from jax.experimental import pallas as pl
from jax.experimental.pallas import tpu as pltpu
from jax.sharding import PartitionSpec as P

NODES = 1024
FEATS = 64
PEERS = 32
SLOTS = 128
HUBS_OWN = 16
HUBS = 512
ROWS = 80
LAYERS = 16
OWN = 64
OUTS = 1024
BF16 = jnp.bfloat16
F32 = jnp.float32
NT = (((1,), (1,)), ((), ()))
NN = (((1,), (0,)), ((), ()))
MIB = 1 << 20


def params(mib):
    return pltpu.CompilerParams(vmem_limit_bytes=mib * MIB)


def cost(flops, moved):
    return pl.CostEstimate(flops=flops, bytes_accessed=moved, transcendentals=0)


def whole(shape):
    return pl.BlockSpec(shape, lambda *_: (0,) * len(shape))


HBM = pl.BlockSpec(memory_space=pltpu.HBM)
VMEM = pl.BlockSpec(memory_space=pltpu.VMEM)


def copies(sems, *pairs):
    started = []
    for i, (source, target) in enumerate(pairs):
        copy = pltpu.make_async_copy(source, target, sems.at[i])
        copy.start()
        started.append(copy)
    return started


def one_hot(mask):
    return jnp.where(mask, 1.0, 0.0).astype(BF16)


def matmul(a, b, dims):
    return lax.dot_general(a, b, dims, preferred_element_type=F32)


def pair_lanes(ref, pair):
    return jnp.concatenate([ref[2 * pair : 2 * pair + 1, :], ref[2 * pair + 1 : 2 * pair + 2, :]], axis=1)


def gather_kernel(x_hbm, send_hbm, hub_hbm, out_ref, x_ref, send_ref, hub_ref, sems):
    for copy in copies(sems, (x_hbm, x_ref), (send_hbm, send_ref), (hub_hbm, hub_ref)):
        copy.wait()
    x = x_ref[...]
    node = lax.broadcasted_iota(jnp.int32, (NODES, 2 * SLOTS), 0)
    hub_node = lax.broadcasted_iota(jnp.int32, (NODES, HUBS_OWN), 0)
    hub_feats = matmul(x, one_hot(hub_node == hub_ref[...]), NN)
    hub_rows = hub_feats.T
    hub_block = jnp.concatenate([hub_rows, jnp.zeros_like(hub_rows)], axis=1).astype(BF16)
    for pair in range(PEERS // 2):
        picked = matmul(x, one_hot(node == pair_lanes(send_ref, pair)), NN).astype(BF16)
        out_ref[2 * pair, :FEATS, :] = picked[:, :SLOTS]
        out_ref[2 * pair + 1, :FEATS, :] = picked[:, SLOTS:]
        out_ref[2 * pair, FEATS:, :] = hub_block
        out_ref[2 * pair + 1, FEATS:, :] = hub_block


def gather_slots(feats, send_lanes, hub_own):
    return pl.pallas_call(
        gather_kernel,
        in_specs=[HBM, HBM, HBM],
        out_shape=jax.ShapeDtypeStruct((PEERS, ROWS, SLOTS), BF16),
        scratch_shapes=[
            pltpu.VMEM((FEATS, NODES), BF16),
            pltpu.VMEM((PEERS, SLOTS), jnp.int32),
            pltpu.VMEM((1, HUBS_OWN), jnp.int32),
            pltpu.SemaphoreType.DMA((3,)),
        ],
        compiler_params=params(60),
        cost_estimate=cost(2 * 256 * 4096 * 1024, 1 << 20),
        name="gather_slots",
    )(feats, send_lanes, hub_own)


BUILD = 256
KEPT = 512


def counts_of(nbr_ref, rows):
    first = lax.broadcasted_iota(jnp.int32, (rows, nbr_ref.shape[1]), 0)
    counts = jnp.zeros(first.shape, F32)
    for k in range(nbr_ref.shape[0]):
        counts = counts + jnp.where(first == nbr_ref[k : k + 1, :], 1.0, 0.0)
    return counts.astype(BF16)


def build_kernel(x_ref, loc_ref, hub_ref, local_ref, hubs_ref, sum_ref):
    counts = counts_of(loc_ref, NODES)
    local_ref[...] = counts
    hubs_ref[...] = counts_of(hub_ref, HUBS)
    sum_ref[...] = matmul(x_ref[...], counts, NN)


def build_counts(feats, loc_lanes, hub_lanes):
    return pl.pallas_call(
        build_kernel,
        grid=(NODES // BUILD,),
        in_specs=[
            whole((FEATS, NODES)),
            pl.BlockSpec((loc_lanes.shape[0], BUILD), lambda i: (0, i)),
            pl.BlockSpec((hub_lanes.shape[0], BUILD), lambda i: (0, i)),
        ],
        out_specs=[
            pl.BlockSpec((NODES, BUILD), lambda i: (0, i)),
            pl.BlockSpec((HUBS, BUILD), lambda i: (0, i)),
            pl.BlockSpec((FEATS, BUILD), lambda i: (0, i)),
        ],
        out_shape=[
            jax.ShapeDtypeStruct((NODES, NODES), BF16),
            jax.ShapeDtypeStruct((HUBS, NODES), BF16),
            jax.ShapeDtypeStruct((KEPT, NODES), F32),
        ],
        compiler_params=params(60),
        cost_estimate=cost(1 << 30, 4 << 20),
        name="build_counts",
    )(feats, loc_lanes, hub_lanes)


AGG = 256


def fold_halves(block):
    return jnp.concatenate([block[: OWN // 2, :], block[OWN // 2 :, :]], axis=1)


NEIGHBOURS = 10.0


def aggregate_kernel(
    x_hbm, inc_ref, recv_hbm, sum_hbm, hub_hbm, cot_hbm, out_ref, degree_ref,
    slots, table, recv_ref, hub_ref, x_ref, cot_ref, sum_ref, sems,
):
    staged = copies(
        sems,
        (recv_hbm, recv_ref),
        (hub_hbm, hub_ref),
        (x_hbm, x_ref),
        (cot_hbm, cot_ref),
        (sum_hbm.at[:FEATS], sum_ref),
    )
    for peer in range(PEERS):
        slots[:FEATS, SLOTS * peer : SLOTS * (peer + 1)] = inc_ref[peer, :FEATS, :]
    slots[FEATS:, :] = jnp.ones((16, PEERS * SLOTS), BF16)
    rows = inc_ref[:, FEATS:, :].astype(F32).reshape(HUBS, SLOTS)
    table[...] = rows.T[:FEATS, :].astype(BF16)
    staged[0].wait()
    for tile in range(NODES // AGG):
        lanes = slice(AGG * tile, AGG * (tile + 1))
        node = lax.broadcasted_iota(jnp.int32, (AGG, 2 * SLOTS), 0) + AGG * tile
        remote = jnp.zeros((ROWS, AGG), F32)
        for pair in range(PEERS // 2):
            remote = remote + matmul(
                slots[:, 2 * SLOTS * pair : 2 * SLOTS * (pair + 1)],
                one_hot(node == pair_lanes(recv_ref, pair)),
                NT,
            )
        if tile == 0:
            for copy in staged[1:]:
                copy.wait()
        hubs = counts_of(hub_ref[:, lanes], HUBS)
        total = remote[:FEATS, :] + sum_ref[:, lanes] + matmul(table[...], hubs, NN)
        degree = remote[FEATS : FEATS + 8, :] + NEIGHBOURS
        degree_ref[:, lanes] = degree
        mean = (total / degree[0:1, :]).T
        nodes = jnp.concatenate([x_ref[:, lanes].astype(F32).T, mean], axis=1).astype(BF16)
        slopes = cot_ref[:, lanes].astype(F32).T
        for part in range(AGG // OWN):
            layer = AGG // OWN * tile + part
            out_ref[layer, :OWN, :] = nodes[OWN * part : OWN * (part + 1), :]
            out_ref[layer, OWN:, :] = fold_halves(slopes[OWN * part : OWN * (part + 1), :]).astype(BF16)


def aggregate(feats, incoming, recv_lanes, local_sum, hub_lanes, cotangent):
    return pl.pallas_call(
        aggregate_kernel,
        out_shape=[
            jax.ShapeDtypeStruct((LAYERS, 96, SLOTS), BF16),
            jax.ShapeDtypeStruct((8, NODES), F32),
        ],
        in_specs=[HBM, VMEM, HBM, HBM, HBM, HBM],
        scratch_shapes=[
            pltpu.VMEM((ROWS, PEERS * SLOTS), BF16),
            pltpu.VMEM((FEATS, HUBS), BF16),
            pltpu.VMEM((PEERS, SLOTS), jnp.int32),
            pltpu.VMEM((2, NODES), jnp.int32),
            pltpu.VMEM((FEATS, NODES), BF16),
            pltpu.VMEM((FEATS, NODES), BF16),
            pltpu.VMEM((FEATS, NODES), F32),
            pltpu.SemaphoreType.DMA((5,)),
        ],
        compiler_params=params(52),
        cost_estimate=cost(2 * 256 * 5632 * 1024, 3 << 20),
        name="aggregate",
    )(feats, incoming, recv_lanes, local_sum, hub_lanes, cotangent)


PIECE = 16
TILE = 256


def regroup_kernel(inc_ref, out_ref):
    group = lax.broadcasted_iota(jnp.int32, (OWN, SLOTS), 1) // PIECE
    for half in range(2):
        blocks = [inc_ref[8 * half + i, :OWN, :].astype(F32) for i in range(8)]
        for slice_of in range(8):
            tile = jnp.zeros((OWN, SLOTS), F32)
            for i in range(8):
                moved = blocks[i]
                if i != slice_of:
                    moved = pltpu.roll(moved, (PIECE * (i - slice_of)) % SLOTS, 1)
                tile = jnp.where(group == i, moved, tile)
            tile = tile.astype(BF16)
            for outs in range(4):
                out_ref[4 * slice_of + outs, :, SLOTS * half : SLOTS * (half + 1)] = tile


def regroup(node_block):
    return pl.pallas_call(
        regroup_kernel,
        out_shape=jax.ShapeDtypeStruct((PEERS, OWN, TILE), BF16),
        compiler_params=params(16),
        cost_estimate=cost(1 << 24, 2 << 20),
        name="regroup",
    )(node_block)


HALF = OUTS // 2
CHIPS = PEERS // 2


SIDE = 4
BAND = 16


def place_kernel(*refs):
    stacks, out_hbm, sems = refs[:SIDE], refs[SIDE], refs[SIDE + 1]
    chip = lax.axis_index("row") // 2
    y, x = chip // SIDE, chip % SIDE
    pairs = []
    for shift_y in range(SIDE):
        for shift_x in range(SIDE):
            source = (y + SIDE - shift_y) % SIDE * SIDE + (x + SIDE - shift_x) % SIDE
            band = pl.ds(pl.multiple_of(BAND * (source % 8), BAND), BAND)
            pairs.append((stacks[shift_y].at[shift_x], out_hbm.at[source // 8, :, band, :]))
    for copy in copies(sems, *pairs):
        copy.wait()


def place_weights(stacks):
    return pl.pallas_call(
        place_kernel,
        in_specs=[HBM] * SIDE,
        out_specs=HBM,
        out_shape=jax.ShapeDtypeStruct((2, LAYERS, SLOTS, TILE), BF16),
        scratch_shapes=[pltpu.SemaphoreType.DMA((SIDE * SIDE,))],
        compiler_params=params(60),
        cost_estimate=cost(0, 4 << 20),
        name="place_weights",
    )(*stacks)


def chip_shift(block, shift_y, shift_x):
    moves = []
    for device in range(PEERS):
        y, x, core = device // 8, device // 2 % SIDE, device % 2
        moves.append((device, (y + shift_y) % SIDE * 8 + (x + shift_x) % SIDE * 2 + core))
    return lax.ppermute(block, "row", moves)


def prepare_kernel(own_block, other_block, joined_ref, cot_ref):
    core = lax.axis_index("row") % 2
    for layer in range(LAYERS):
        lanes = slice(SLOTS * layer, SLOTS * (layer + 1))
        joined_ref[core, :, lanes] = own_block[layer, :OWN, :]
        joined_ref[1 - core, :, lanes] = other_block[layer, :OWN, :]
    for side, block in ((core, own_block), (1 - core, other_block)):
        for pair in range(LAYERS // 4):
            even = block[8 * core + 2 * pair, OWN:, :].astype(F32)
            odd = block[8 * core + 2 * pair + 1, OWN:, :].astype(F32)
            top = jnp.concatenate([even[:, :FEATS], odd[:, :FEATS]], axis=1)
            bottom = jnp.concatenate([even[:, FEATS:], odd[:, FEATS:]], axis=1)
            cot_ref[side, :, SLOTS * pair : SLOTS * (pair + 1)] = jnp.concatenate(
                [top, bottom], axis=0
            ).astype(BF16)


def prepare(own_block, other_block):
    return pl.pallas_call(
        prepare_kernel,
        out_shape=[
            jax.ShapeDtypeStruct((2, OWN, 2 * OUTS), BF16),
            jax.ShapeDtypeStruct((2, OWN, HALF), BF16),
        ],
        compiler_params=params(16),
        cost_estimate=cost(1 << 20, 2 << 20),
        name="prepare",
    )(own_block, other_block)


def forward_kernel(
    joined_hbm, cot_hbm, weights_hbm, slopes_hbm, flat_hbm, hidden_hbm,
    joined, cots, weights, out_tile, flat, hidden, in_sems, out_sems,
):
    staged = copies(
        in_sems,
        (joined_hbm, joined),
        (weights_hbm.at[0], weights.at[0]),
        (cot_hbm, cots),
        (weights_hbm.at[1], weights.at[1]),
    )
    staged[0].wait()
    sent = []
    for side in range(2):
        staged[2 * side + 1].wait()
        columns = slice(TILE * side, TILE * (side + 1))
        preact = matmul(joined[...].reshape(2 * OWN, 2 * OUTS), weights[side].reshape(2 * OUTS, TILE), NN)
        if side == 0:
            staged[2].wait()
        sigmoid_part = jax.nn.sigmoid(preact)
        silu = preact * sigmoid_part
        slope = sigmoid_part * (1.0 + preact * (1.0 - sigmoid_part))
        cot = cots[:, :, columns].reshape(2 * OWN, TILE).astype(F32)
        slopes = (cot * slope).astype(BF16)
        out_tile[side] = slopes
        for chip in range(side, CHIPS, 2):
            copy = pltpu.make_async_copy(out_tile.at[side], slopes_hbm.at[chip], out_sems.at[chip])
            copy.start()
            sent.append(copy)
        flat[:, columns] = slopes
        for block in range(2):
            for layer in range(4):
                tile = silu[OWN * block : OWN * (block + 1), FEATS * layer : FEATS * (layer + 1)]
                hidden[block, 4 * side + layer] = fold_halves(tile).astype(BF16)
    for i, (source, target) in enumerate(((flat, flat_hbm), (hidden, hidden_hbm))):
        copy = pltpu.make_async_copy(source, target, out_sems.at[CHIPS + i])
        copy.start()
        sent.append(copy)
    for copy in sent:
        copy.wait()


def forward(joined, cots, weights):
    return pl.pallas_call(
        forward_kernel,
        in_specs=[HBM, HBM, HBM],
        out_specs=[HBM, HBM, HBM],
        out_shape=[
            jax.ShapeDtypeStruct((CHIPS, 2 * OWN, TILE), BF16),
            jax.ShapeDtypeStruct((2 * OWN, HALF), BF16),
            jax.ShapeDtypeStruct((2, LAYERS // 2, OWN // 2, SLOTS), BF16),
        ],
        scratch_shapes=[
            pltpu.VMEM((2, OWN, 2 * OUTS), BF16),
            pltpu.VMEM((2, OWN, HALF), BF16),
            pltpu.VMEM((2, LAYERS, SLOTS, TILE), BF16),
            pltpu.VMEM((2, 2 * OWN, TILE), BF16),
            pltpu.VMEM((2 * OWN, HALF), BF16),
            pltpu.VMEM((2, LAYERS // 2, OWN // 2, SLOTS), BF16),
            pltpu.SemaphoreType.DMA((4,)),
            pltpu.SemaphoreType.DMA((CHIPS + 2,)),
        ],
        compiler_params=params(60),
        cost_estimate=cost(2 * 256 * 2048 * 512, 4 << 20),
        name="forward",
    )(joined, cots, weights)


def backward_kernel(slopes_ref, hidden_ref, weights_ref, keep_ref, send_ref, keep_hidden, send_hidden, parts):
    core = lax.axis_index("row") % 2
    back = matmul(slopes_ref[:, :TILE], weights_ref[0].reshape(2 * OUTS, TILE), NT) + matmul(
        slopes_ref[:, TILE:], weights_ref[1].reshape(2 * OUTS, TILE), NT
    )
    parts[0] = back[:OWN, :]
    parts[1] = back[OWN:, :]
    keep_ref[...] = parts[core]
    send_ref[...] = parts[1 - core]
    keep_hidden[...] = hidden_ref[core]
    send_hidden[...] = hidden_ref[1 - core]


def backward(slopes, hidden, weights):
    part = jax.ShapeDtypeStruct((OWN, 2 * OUTS), F32)
    block = jax.ShapeDtypeStruct((LAYERS // 2, OWN // 2, SLOTS), BF16)
    return pl.pallas_call(
        backward_kernel,
        out_shape=[part, part, block, block],
        scratch_shapes=[pltpu.VMEM((2, OWN, 2 * OUTS), F32)],
        compiler_params=params(16),
        cost_estimate=cost(2 * 256 * 2048 * 512, 4 << 20),
        name="backward",
    )(slopes, hidden, weights)


def combine_kernel(mine_ref, theirs_ref, my_hidden, their_hidden, degree_ref, out_ref):
    core = lax.axis_index("row") % 2
    direct = lax.broadcasted_iota(jnp.int32, (OWN, SLOTS), 1) < FEATS
    divisor = jnp.where(direct, 1.0, degree_ref[...])
    for layer in range(LAYERS):
        lanes = slice(SLOTS * layer, SLOTS * (layer + 1))
        back = mine_ref[:, lanes] + theirs_ref[:, lanes]
        out_ref[layer, :OWN, :] = (back / divisor).astype(BF16)
    for layer in range(LAYERS // 2):
        out_ref[8 * core + layer, OWN:, :] = my_hidden[layer]
        out_ref[8 * (1 - core) + layer, OWN:, :] = their_hidden[layer]


def combine(mine, theirs, my_hidden, their_hidden, own_degree):
    return pl.pallas_call(
        combine_kernel,
        out_shape=jax.ShapeDtypeStruct((LAYERS, 96, SLOTS), BF16),
        compiler_params=params(16),
        cost_estimate=cost(1 << 20, 2 << 20),
        name="combine",
    )(mine, theirs, my_hidden, their_hidden, own_degree)


STEPS = 4


def weight_kernel(joined_hbm, slopes_ref, back_hbm, out_ref, joined, back, sems):
    depth = PEERS * OWN // STEPS
    staged = copies(
        sems,
        *[
            (joined_hbm.at[:, depth * i : depth * (i + 1)], joined.at[:, depth * i : depth * (i + 1)])
            for i in range(STEPS)
        ],
        (back_hbm, back),
    )
    part = jnp.zeros((TILE, TILE), F32)
    for i in range(STEPS):
        staged[i].wait()
        rows = slice(depth * i, depth * (i + 1))
        part = part + matmul(joined[:, rows], slopes_ref[rows, :], NN)
    part = part.astype(BF16)
    for layer in range(LAYERS):
        out_ref[layer, 96:112, :] = part[PIECE * layer : PIECE * (layer + 1), :SLOTS]
        out_ref[layer, 112:, :] = part[PIECE * layer : PIECE * (layer + 1), SLOTS:]
    staged[STEPS].wait()
    out_ref[:, :96, :] = back[...]


def weight_parts(joined_cols, slopes_rows, back):
    return pl.pallas_call(
        weight_kernel,
        in_specs=[HBM, VMEM, HBM],
        out_shape=jax.ShapeDtypeStruct((LAYERS, SLOTS, SLOTS), BF16),
        scratch_shapes=[
            pltpu.VMEM((TILE, PEERS * OWN), BF16),
            pltpu.VMEM((LAYERS, 96, SLOTS), BF16),
            pltpu.SemaphoreType.DMA((STEPS + 1,)),
        ],
        compiler_params=params(16),
        cost_estimate=cost(2 * 256 * 2048 * 256, 3 << 20),
        name="weight_parts",
    )(joined_cols, slopes_rows, back)


RETURN_ROWS = 112


def return_kernel(
    back_hbm, recv_hbm, hubs_hbm, out_hbm,
    back_ref, part_ref, recv_ref, hubs_ref, out_ref, in_sems, out_sems,
):
    staged = copies(
        in_sems,
        (recv_hbm, recv_ref),
        (hubs_hbm, hubs_ref),
        (back_hbm.at[:, :OWN, :], back_ref),
        (back_hbm.at[:, 96:, :], part_ref),
    )
    node = lax.broadcasted_iota(jnp.int32, (NODES, 2 * SLOTS), 0)
    staged[2].wait()
    share = back_ref[...].astype(F32).reshape(NODES, SLOTS).T[FEATS:, :].astype(BF16)
    staged[0].wait()
    staged[3].wait()
    sums = jnp.sum(part_ref[...].astype(F32), axis=0).astype(BF16)
    sent = []
    for pair in range(PEERS // 2):
        values = matmul(share, one_hot(node == pair_lanes(recv_ref, pair)), NN).astype(BF16)
        for side in range(2):
            peer = 2 * pair + side
            out_ref[peer, :FEATS, :] = values[:, SLOTS * side : SLOTS * (side + 1)]
            out_ref[peer, ROWS:, :] = sums
        if pair == 3:
            staged[1].wait()
            terms = matmul(share, hubs_ref[...], NT).T
            high = terms.astype(BF16).astype(F32)
            both = jnp.concatenate([high, terms - high], axis=1)
            out_ref[:, FEATS:ROWS, :] = both.reshape(PEERS, HUBS_OWN, SLOTS).astype(BF16)
        if pair % 4 == 3:
            part = pl.ds(2 * pair - 6, 8)
            copy = pltpu.make_async_copy(out_ref.at[part], out_hbm.at[part], out_sems.at[pair // 4])
            copy.start()
            sent.append(copy)
    for copy in sent:
        copy.wait()


def return_slots(back_block, recv_lanes, hubs):
    return pl.pallas_call(
        return_kernel,
        in_specs=[HBM, HBM, HBM],
        out_specs=HBM,
        out_shape=jax.ShapeDtypeStruct((PEERS, RETURN_ROWS, SLOTS), BF16),
        scratch_shapes=[
            pltpu.VMEM((LAYERS, OWN, SLOTS), BF16),
            pltpu.VMEM((LAYERS, 32, SLOTS), BF16),
            pltpu.VMEM((PEERS, SLOTS), jnp.int32),
            pltpu.VMEM((HUBS, NODES), BF16),
            pltpu.VMEM((PEERS, RETURN_ROWS, SLOTS), BF16),
            pltpu.SemaphoreType.DMA((4,)),
            pltpu.SemaphoreType.DMA((4,)),
        ],
        compiler_params=params(60),
        cost_estimate=cost(2 * 256 * 4608 * 1024, 3 << 20),
        name="return_slots",
    )(back_block, recv_lanes, hubs)


def local_kernel(back_ref, local_ref, base_hbm, hidden_ref, base_ref, sems):
    columns = back_ref[:, :OWN, :].astype(F32).reshape(NODES, SLOTS).T
    share = columns[FEATS:, :].astype(BF16)
    base_ref[...] = columns[:FEATS, :] + matmul(share, local_ref[...], NT)
    (sent,) = copies(sems, (base_ref, base_hbm.at[:FEATS]))
    folded = back_ref[:, OWN:96, :].astype(F32)
    rows = jnp.concatenate([folded[:, :, :FEATS], folded[:, :, FEATS:]], axis=1)
    hidden_ref[...] = rows.reshape(NODES, FEATS).T.astype(BF16)
    sent.wait()


def local_grads(back_block, local):
    return pl.pallas_call(
        local_kernel,
        out_specs=[HBM, VMEM],
        out_shape=[
            jax.ShapeDtypeStruct((KEPT, NODES), F32),
            jax.ShapeDtypeStruct((FEATS, NODES), BF16),
        ],
        scratch_shapes=[pltpu.VMEM((FEATS, NODES), F32), pltpu.SemaphoreType.DMA((1,))],
        compiler_params=params(60),
        cost_estimate=cost(2 * 256 * 1024 * 1024, 3 << 20),
        name="local_grads",
    )(back_block, local)


SPREAD = 256


def spread_kernel(
    back_ref, send_hbm, hub_hbm, base_hbm, out_ref, self_hbm, neigh_hbm,
    send_ref, hub_ref, base_ref, grads_ref, slots, in_sems, out_sems,
):
    staged = copies(in_sems, (send_hbm, send_ref), (hub_hbm, hub_ref), (base_hbm.at[:FEATS], base_ref))
    for peer in range(PEERS):
        slots[:, SLOTS * peer : SLOTS * (peer + 1)] = back_ref[peer, :FEATS, :]
        grads = back_ref[peer, ROWS:, :].astype(F32)
        slice_of, outs = peer // 4, 2 * (peer % 2) + peer // 2 % 2
        rows = slice(PIECE * slice_of, PIECE * (slice_of + 1))
        grads_ref[rows, TILE * outs : TILE * outs + SLOTS] = grads[:PIECE, :]
        grads_ref[rows, TILE * outs + SLOTS : TILE * (outs + 1)] = grads[PIECE:, :]
    sent = copies(
        out_sems, (grads_ref.at[:FEATS], self_hbm), (grads_ref.at[FEATS:], neigh_hbm)
    )
    sums = jnp.sum(back_ref[:, FEATS:ROWS, :].astype(F32), axis=0)
    total = sums[:, :FEATS] + sums[:, FEATS:]
    high = total.astype(BF16).astype(F32)
    hub_high = high.T.astype(BF16)
    hub_low = (total - high).T.astype(BF16)
    for copy in staged:
        copy.wait()
    for tile in range(NODES // SPREAD):
        lanes = slice(SPREAD * tile, SPREAD * (tile + 1))
        node = lax.broadcasted_iota(jnp.int32, (SPREAD, 2 * SLOTS), 0) + SPREAD * tile
        grad = base_ref[:, lanes]
        for pair in range(PEERS // 2):
            grad = grad + matmul(
                slots[:, 2 * SLOTS * pair : 2 * SLOTS * (pair + 1)],
                one_hot(node == pair_lanes(send_ref, pair)),
                NT,
            )
        hub_node = lax.broadcasted_iota(jnp.int32, (SPREAD, HUBS_OWN), 0) + SPREAD * tile
        hub_hot = one_hot(hub_node == hub_ref[...])
        grad = grad + matmul(hub_high, hub_hot, NT) + matmul(hub_low, hub_hot, NT)
        out_ref[:, lanes] = grad.astype(BF16)
    for copy in sent:
        copy.wait()


def spread_grads(returned, send_lanes, hub_own, base):
    return pl.pallas_call(
        spread_kernel,
        in_specs=[VMEM, HBM, HBM, HBM],
        out_specs=[VMEM, HBM, HBM],
        out_shape=[
            jax.ShapeDtypeStruct((FEATS, NODES), BF16),
            jax.ShapeDtypeStruct((FEATS, OUTS), F32),
            jax.ShapeDtypeStruct((FEATS, OUTS), F32),
        ],
        scratch_shapes=[
            pltpu.VMEM((PEERS, SLOTS), jnp.int32),
            pltpu.VMEM((1, HUBS_OWN), jnp.int32),
            pltpu.VMEM((FEATS, NODES), F32),
            pltpu.VMEM((2 * FEATS, OUTS), F32),
            pltpu.VMEM((FEATS, PEERS * SLOTS), BF16),
            pltpu.SemaphoreType.DMA((3,)),
            pltpu.SemaphoreType.DMA((2,)),
        ],
        compiler_params=params(52),
        cost_estimate=cost(2 * 256 * 4224 * 1024, 2 << 20),
        name="spread_grads",
    )(returned, send_lanes, hub_own, base)


SAME_CORE = [list(range(core, PEERS, 2)) for core in range(2)]


def exchange(blocks, axis, groups=None):
    return lax.all_to_all(blocks, axis, 0, 0, axis_index_groups=groups, tiled=True)


def other_core(block):
    return lax.ppermute(block, "row", [(i, i ^ 1) for i in range(PEERS)])


def per_device(feats, w_self, w_neigh, cotangent, loc_nbr, send_rows, recv_node, hub_rows, hub_nbr):
    send_lanes = send_rows.reshape(PEERS, SLOTS)
    recv_lanes = recv_node.reshape(PEERS, SLOTS)
    hub_own = hub_rows[None, :]
    device = lax.axis_index("row")
    piece = lax.dynamic_slice(
        jnp.concatenate([w_self, w_neigh], axis=0),
        (BAND * (device // 2 % 8), HALF * (device % 2) + TILE * (device // 16)),
        (BAND, TILE),
    )
    piece = exchange(jnp.broadcast_to(piece[None], (LAYERS, BAND, TILE)), "col")
    slots_out = gather_slots(feats, send_lanes, hub_own)
    slots_out, piece = lax.optimization_barrier((slots_out, piece))
    stack = jnp.stack([piece] + [chip_shift(piece, 0, shift) for shift in range(1, SIDE)])
    incoming = exchange(slots_out, "row")
    incoming, stack = lax.optimization_barrier((incoming, stack))
    stacks = [stack] + [chip_shift(stack, shift, 0) for shift in range(1, SIDE)]
    hub_lanes = hub_nbr.T
    local, hubs, local_sum = build_counts(feats, loc_nbr.T, hub_lanes)
    outgoing, degree = aggregate(feats, incoming, recv_lanes, local_sum, hub_lanes, cotangent)
    node_block = exchange(outgoing, "col")
    node_block, stacks = lax.optimization_barrier((node_block, stacks))
    weights = place_weights(stacks)
    own_degree = lax.dynamic_slice_in_dim(degree[0], OWN * lax.axis_index("col"), OWN)[:, None]
    joined_cols = exchange(regroup(node_block), "row").reshape(PEERS * OWN, TILE).T
    joined, cots = prepare(node_block, other_core(node_block))
    slopes_out, slopes, hidden = forward(joined, cots, weights)
    slopes_rows = exchange(slopes_out, "row", SAME_CORE).reshape(PEERS * OWN, TILE)
    mine, theirs, my_hidden, their_hidden = backward(slopes, hidden, weights)
    back = combine(mine, other_core(theirs), my_hidden, other_core(their_hidden), own_degree)
    back_block = exchange(weight_parts(joined_cols, slopes_rows, back), "col")
    returned = exchange(return_slots(back_block, recv_lanes, hubs), "row")
    base, hidden_out = local_grads(back_block, local)
    grad_feats, grad_self, grad_neigh = spread_grads(returned, send_lanes, hub_own, base)
    return (hidden_out, grad_feats, grad_self, grad_neigh)


def solution(mesh):
    return jax.shard_map(
        per_device,
        mesh=mesh,
        in_specs=(
            P("col", "row"),
            P("col", None),
            P("col", None),
            P("col", "row"),
            P("row", None),
            P("row", None, None),
            P("row", None, None),
            P("row"),
            P("row", None),
        ),
        out_specs=(P("col", "row"), P("col", "row"), P("col", None), P("col", None)),
        check_vma=False,
    )
```

```python
import jax
import jax.numpy as jnp
from jax import lax
from jax.experimental import pallas as pl
from jax.experimental.pallas import tpu as pltpu
from jax.sharding import PartitionSpec as P

NODES = 1024
FEATS = 64
PEERS = 32
SLOTS = 128
HUBS_OWN = 16
HUBS = 512
ROWS = 80
LAYERS = 16
OWN = 64
OUTS = 1024
BF16 = jnp.bfloat16
F32 = jnp.float32
NT = (((1,), (1,)), ((), ()))
NN = (((1,), (0,)), ((), ()))
MIB = 1 << 20


def params(mib):
    return pltpu.CompilerParams(vmem_limit_bytes=mib * MIB)


def cost(flops, moved):
    return pl.CostEstimate(flops=flops, bytes_accessed=moved, transcendentals=0)


def whole(shape):
    return pl.BlockSpec(shape, lambda *_: (0,) * len(shape))


HBM = pl.BlockSpec(memory_space=pltpu.HBM)
VMEM = pl.BlockSpec(memory_space=pltpu.VMEM)


def copies(sems, *pairs):
    started = []
    for i, (source, target) in enumerate(pairs):
        copy = pltpu.make_async_copy(source, target, sems.at[i])
        copy.start()
        started.append(copy)
    return started


def one_hot(mask):
    return jnp.where(mask, 1.0, 0.0).astype(BF16)


def matmul(a, b, dims):
    return lax.dot_general(a, b, dims, preferred_element_type=F32)


def pair_lanes(ref, pair):
    return jnp.concatenate([ref[2 * pair : 2 * pair + 1, :], ref[2 * pair + 1 : 2 * pair + 2, :]], axis=1)


def gather_kernel(x_hbm, send_hbm, hub_hbm, out_ref, x_ref, send_ref, hub_ref, sems):
    for copy in copies(sems, (x_hbm, x_ref), (send_hbm, send_ref), (hub_hbm, hub_ref)):
        copy.wait()
    x = x_ref[...]
    node = lax.broadcasted_iota(jnp.int32, (NODES, 2 * SLOTS), 0)
    hub_node = lax.broadcasted_iota(jnp.int32, (NODES, HUBS_OWN), 0)
    hub_feats = matmul(x, one_hot(hub_node == hub_ref[...]), NN)
    hub_rows = hub_feats.T
    hub_block = jnp.concatenate([hub_rows, jnp.zeros_like(hub_rows)], axis=1).astype(BF16)
    for pair in range(PEERS // 2):
        picked = matmul(x, one_hot(node == pair_lanes(send_ref, pair)), NN).astype(BF16)
        out_ref[2 * pair, :FEATS, :] = picked[:, :SLOTS]
        out_ref[2 * pair + 1, :FEATS, :] = picked[:, SLOTS:]
        out_ref[2 * pair, FEATS:, :] = hub_block
        out_ref[2 * pair + 1, FEATS:, :] = hub_block


def gather_slots(feats, send_lanes, hub_own):
    return pl.pallas_call(
        gather_kernel,
        in_specs=[HBM, HBM, HBM],
        out_shape=jax.ShapeDtypeStruct((PEERS, ROWS, SLOTS), BF16),
        scratch_shapes=[
            pltpu.VMEM((FEATS, NODES), BF16),
            pltpu.VMEM((PEERS, SLOTS), jnp.int32),
            pltpu.VMEM((1, HUBS_OWN), jnp.int32),
            pltpu.SemaphoreType.DMA((3,)),
        ],
        compiler_params=params(60),
        cost_estimate=cost(2 * 256 * 4096 * 1024, 1 << 20),
        name="gather_slots",
    )(feats, send_lanes, hub_own)


BUILD = 256
KEPT = 512


def counts_of(nbr_ref, rows):
    first = lax.broadcasted_iota(jnp.int32, (rows, nbr_ref.shape[1]), 0)
    counts = jnp.zeros(first.shape, F32)
    for k in range(nbr_ref.shape[0]):
        counts = counts + jnp.where(first == nbr_ref[k : k + 1, :], 1.0, 0.0)
    return counts.astype(BF16)


def build_kernel(x_ref, loc_ref, hub_ref, local_ref, hubs_ref, sum_ref):
    counts = counts_of(loc_ref, NODES)
    local_ref[...] = counts
    hubs_ref[...] = counts_of(hub_ref, HUBS)
    sum_ref[...] = matmul(x_ref[...], counts, NN)


def build_counts(feats, loc_lanes, hub_lanes):
    return pl.pallas_call(
        build_kernel,
        grid=(NODES // BUILD,),
        in_specs=[
            whole((FEATS, NODES)),
            pl.BlockSpec((loc_lanes.shape[0], BUILD), lambda i: (0, i)),
            pl.BlockSpec((hub_lanes.shape[0], BUILD), lambda i: (0, i)),
        ],
        out_specs=[
            pl.BlockSpec((NODES, BUILD), lambda i: (0, i)),
            pl.BlockSpec((HUBS, BUILD), lambda i: (0, i)),
            pl.BlockSpec((FEATS, BUILD), lambda i: (0, i)),
        ],
        out_shape=[
            jax.ShapeDtypeStruct((NODES, NODES), BF16),
            jax.ShapeDtypeStruct((HUBS, NODES), BF16),
            jax.ShapeDtypeStruct((KEPT, NODES), F32),
        ],
        compiler_params=params(60),
        cost_estimate=cost(1 << 30, 4 << 20),
        name="build_counts",
    )(feats, loc_lanes, hub_lanes)


AGG = 256


def fold_halves(block):
    return jnp.concatenate([block[: OWN // 2, :], block[OWN // 2 :, :]], axis=1)


NEIGHBOURS = 10.0


def aggregate_kernel(
    x_hbm, inc_ref, recv_hbm, sum_hbm, hub_hbm, cot_hbm, out_ref, degree_ref,
    slots, table, recv_ref, hub_ref, x_ref, cot_ref, sum_ref, sems,
):
    staged = copies(
        sems,
        (recv_hbm, recv_ref),
        (hub_hbm, hub_ref),
        (x_hbm, x_ref),
        (cot_hbm, cot_ref),
        (sum_hbm.at[:FEATS], sum_ref),
    )
    for peer in range(PEERS):
        slots[:FEATS, SLOTS * peer : SLOTS * (peer + 1)] = inc_ref[peer, :FEATS, :]
    slots[FEATS:, :] = jnp.ones((16, PEERS * SLOTS), BF16)
    rows = inc_ref[:, FEATS:, :].astype(F32).reshape(HUBS, SLOTS)
    table[...] = rows.T[:FEATS, :].astype(BF16)
    staged[0].wait()
    for tile in range(NODES // AGG):
        lanes = slice(AGG * tile, AGG * (tile + 1))
        node = lax.broadcasted_iota(jnp.int32, (AGG, 2 * SLOTS), 0) + AGG * tile
        remote = jnp.zeros((ROWS, AGG), F32)
        for pair in range(PEERS // 2):
            remote = remote + matmul(
                slots[:, 2 * SLOTS * pair : 2 * SLOTS * (pair + 1)],
                one_hot(node == pair_lanes(recv_ref, pair)),
                NT,
            )
        if tile == 0:
            for copy in staged[1:]:
                copy.wait()
        hubs = counts_of(hub_ref[:, lanes], HUBS)
        total = remote[:FEATS, :] + sum_ref[:, lanes] + matmul(table[...], hubs, NN)
        degree = remote[FEATS : FEATS + 8, :] + NEIGHBOURS
        degree_ref[:, lanes] = degree
        mean = (total / degree[0:1, :]).T
        nodes = jnp.concatenate([x_ref[:, lanes].astype(F32).T, mean], axis=1).astype(BF16)
        slopes = cot_ref[:, lanes].astype(F32).T
        for part in range(AGG // OWN):
            layer = AGG // OWN * tile + part
            out_ref[layer, :OWN, :] = nodes[OWN * part : OWN * (part + 1), :]
            out_ref[layer, OWN:, :] = fold_halves(slopes[OWN * part : OWN * (part + 1), :]).astype(BF16)


def aggregate(feats, incoming, recv_lanes, local_sum, hub_lanes, cotangent):
    return pl.pallas_call(
        aggregate_kernel,
        out_shape=[
            jax.ShapeDtypeStruct((LAYERS, 96, SLOTS), BF16),
            jax.ShapeDtypeStruct((8, NODES), F32),
        ],
        in_specs=[HBM, VMEM, HBM, HBM, HBM, HBM],
        scratch_shapes=[
            pltpu.VMEM((ROWS, PEERS * SLOTS), BF16),
            pltpu.VMEM((FEATS, HUBS), BF16),
            pltpu.VMEM((PEERS, SLOTS), jnp.int32),
            pltpu.VMEM((2, NODES), jnp.int32),
            pltpu.VMEM((FEATS, NODES), BF16),
            pltpu.VMEM((FEATS, NODES), BF16),
            pltpu.VMEM((FEATS, NODES), F32),
            pltpu.SemaphoreType.DMA((5,)),
        ],
        compiler_params=params(52),
        cost_estimate=cost(2 * 256 * 5632 * 1024, 3 << 20),
        name="aggregate",
    )(feats, incoming, recv_lanes, local_sum, hub_lanes, cotangent)


PIECE = 32
TILE = 256
CHIPS = PEERS // 2
SLICE = LAYERS * PIECE


def regroup_kernel(inc_ref, out_ref):
    group = lax.broadcasted_iota(jnp.int32, (OWN, SLOTS), 1) // PIECE
    for part in range(4):
        blocks = [inc_ref[4 * part + i, :OWN, :].astype(F32) for i in range(4)]
        for slice_of in range(4):
            tile = jnp.zeros((OWN, SLOTS), F32)
            for i in range(4):
                moved = blocks[i]
                if i != slice_of:
                    moved = pltpu.roll(moved, (PIECE * (i - slice_of)) % SLOTS, 1)
                tile = jnp.where(group == i, moved, tile)
            tile = tile.astype(BF16)
            for outs in range(4):
                out_ref[4 * slice_of + outs, :, SLOTS * part : SLOTS * (part + 1)] = tile


def regroup(node_block):
    return pl.pallas_call(
        regroup_kernel,
        out_shape=jax.ShapeDtypeStruct((CHIPS, OWN, SLICE), BF16),
        compiler_params=params(16),
        cost_estimate=cost(1 << 24, 2 << 20),
        name="regroup",
    )(node_block)


HALF = OUTS // 2


def prepare_kernel(own_block, other_block, joined_ref, cot_ref):
    core = lax.axis_index("row") % 2
    for layer in range(LAYERS):
        lanes = slice(SLOTS * layer, SLOTS * (layer + 1))
        joined_ref[0, :, lanes] = own_block[layer, :OWN, :]
        joined_ref[1, :, lanes] = other_block[layer, :OWN, :]
    for side, block in enumerate((own_block, other_block)):
        for pair in range(LAYERS // 4):
            even = block[8 * core + 2 * pair, OWN:, :].astype(F32)
            odd = block[8 * core + 2 * pair + 1, OWN:, :].astype(F32)
            top = jnp.concatenate([even[:, :FEATS], odd[:, :FEATS]], axis=1)
            bottom = jnp.concatenate([even[:, FEATS:], odd[:, FEATS:]], axis=1)
            cot_ref[side, :, SLOTS * pair : SLOTS * (pair + 1)] = jnp.concatenate(
                [top, bottom], axis=0
            ).astype(BF16)


def prepare(own_block, other_block):
    return pl.pallas_call(
        prepare_kernel,
        out_shape=[
            jax.ShapeDtypeStruct((2, OWN, 2 * OUTS), BF16),
            jax.ShapeDtypeStruct((2, OWN, HALF), BF16),
        ],
        compiler_params=params(16),
        cost_estimate=cost(1 << 20, 2 << 20),
        name="prepare",
    )(own_block, other_block)


def forward_kernel(
    joined_hbm, cot_hbm, weights_hbm, slopes_hbm, flat_hbm, hidden_hbm,
    joined, cots, weights, out_tile, flat, hidden, in_sems, out_sems,
):
    staged = copies(
        in_sems,
        (joined_hbm, joined),
        (weights_hbm.at[:, :TILE], weights.at[:, :TILE]),
        (cot_hbm, cots),
        (weights_hbm.at[:, TILE:], weights.at[:, TILE:]),
    )
    staged[0].wait()
    sent = []
    for side in range(2):
        staged[2 * side + 1].wait()
        columns = slice(TILE * side, TILE * (side + 1))
        preact = matmul(joined[...].reshape(2 * OWN, 2 * OUTS), weights[:, columns], NN)
        if side == 0:
            staged[2].wait()
        sigmoid_part = jax.nn.sigmoid(preact)
        silu = preact * sigmoid_part
        slope = sigmoid_part * (1.0 + preact * (1.0 - sigmoid_part))
        cot = cots[:, :, columns].reshape(2 * OWN, TILE).astype(F32)
        slopes = (cot * slope).astype(BF16)
        for outs in range(2):
            out_tile[2 * side + outs] = slopes[:, SLOTS * outs : SLOTS * (outs + 1)]
        for chip in range(CHIPS):
            if chip % 4 // 2 == side:
                copy = pltpu.make_async_copy(
                    out_tile.at[chip % 4], slopes_hbm.at[chip], out_sems.at[chip]
                )
                copy.start()
                sent.append(copy)
        flat[:, columns] = slopes
        for block in range(2):
            for layer in range(4):
                tile = silu[OWN * block : OWN * (block + 1), FEATS * layer : FEATS * (layer + 1)]
                hidden[block, 4 * side + layer] = fold_halves(tile).astype(BF16)
    for i, (source, target) in enumerate(((flat, flat_hbm), (hidden, hidden_hbm))):
        copy = pltpu.make_async_copy(source, target, out_sems.at[CHIPS + i])
        copy.start()
        sent.append(copy)
    for copy in sent:
        copy.wait()


def forward(joined, cots, weights):
    return pl.pallas_call(
        forward_kernel,
        in_specs=[HBM, HBM, HBM],
        out_specs=[HBM, HBM, HBM],
        out_shape=[
            jax.ShapeDtypeStruct((CHIPS, 2 * OWN, SLOTS), BF16),
            jax.ShapeDtypeStruct((2 * OWN, HALF), BF16),
            jax.ShapeDtypeStruct((2, LAYERS // 2, OWN // 2, SLOTS), BF16),
        ],
        scratch_shapes=[
            pltpu.VMEM((2, OWN, 2 * OUTS), BF16),
            pltpu.VMEM((2, OWN, HALF), BF16),
            pltpu.VMEM((2 * OUTS, HALF), BF16),
            pltpu.VMEM((4, 2 * OWN, SLOTS), BF16),
            pltpu.VMEM((2 * OWN, HALF), BF16),
            pltpu.VMEM((2, LAYERS // 2, OWN // 2, SLOTS), BF16),
            pltpu.SemaphoreType.DMA((4,)),
            pltpu.SemaphoreType.DMA((CHIPS + 2,)),
        ],
        compiler_params=params(60),
        cost_estimate=cost(2 * 256 * 2048 * 512, 4 << 20),
        name="forward",
    )(joined, cots, weights)


def backward_kernel(slopes_ref, hidden_ref, weights_ref, keep_ref, send_ref, keep_hidden, send_hidden):
    back = matmul(slopes_ref[...], weights_ref[...], NT)
    keep_ref[...] = back[:OWN, :]
    send_ref[...] = back[OWN:, :].astype(BF16)
    keep_hidden[...] = hidden_ref[0]
    send_hidden[...] = hidden_ref[1]


def backward(slopes, hidden, weights):
    part = jax.ShapeDtypeStruct((OWN, 2 * OUTS), F32)
    block = jax.ShapeDtypeStruct((LAYERS // 2, OWN // 2, SLOTS), BF16)
    return pl.pallas_call(
        backward_kernel,
        out_shape=[part, jax.ShapeDtypeStruct((OWN, 2 * OUTS), BF16), block, block],
        compiler_params=params(60),
        cost_estimate=cost(2 * 256 * 2048 * 512, 4 << 20),
        name="backward",
    )(slopes, hidden, weights)


def combine_kernel(mine_ref, theirs_ref, my_hidden, their_hidden, degree_ref, out_ref):
    core = lax.axis_index("row") % 2
    direct = lax.broadcasted_iota(jnp.int32, (OWN, SLOTS), 1) < FEATS
    divisor = jnp.where(direct, 1.0, degree_ref[...])
    for layer in range(LAYERS):
        lanes = slice(SLOTS * layer, SLOTS * (layer + 1))
        back = mine_ref[:, lanes] + theirs_ref[:, lanes].astype(F32)
        out_ref[layer, :OWN, :] = (back / divisor).astype(BF16)
    for layer in range(LAYERS // 2):
        out_ref[8 * core + layer, OWN:, :] = my_hidden[layer]
        out_ref[8 * (1 - core) + layer, OWN:, :] = their_hidden[layer]


def combine(mine, theirs, my_hidden, their_hidden, own_degree):
    return pl.pallas_call(
        combine_kernel,
        out_shape=jax.ShapeDtypeStruct((LAYERS, 96, SLOTS), BF16),
        compiler_params=params(16),
        cost_estimate=cost(1 << 20, 2 << 20),
        name="combine",
    )(mine, theirs, my_hidden, their_hidden, own_degree)


def weight_kernel(mine_hbm, theirs_hbm, slopes_ref, back_hbm, out_ref, mine, theirs, back, sems):
    staged = copies(sems, (mine_hbm, mine), (theirs_hbm, theirs), (back_hbm, back))
    part = jnp.zeros((SLOTS, SLICE), F32)
    for side, rows in enumerate((mine, theirs)):
        slopes = slopes_ref[:, OWN * side : OWN * (side + 1), :].astype(F32)
        columns = slopes.reshape(CHIPS * OWN, SLOTS).T.astype(BF16)
        staged[side].wait()
        part = part + matmul(columns, rows[...].reshape(CHIPS * OWN, SLICE), NN)
    part = part.T.astype(BF16)
    for layer in range(LAYERS):
        out_ref[layer, 96:, :] = part[PIECE * layer : PIECE * (layer + 1), :]
    staged[2].wait()
    out_ref[:, :96, :] = back[...]


def weight_parts(mine, theirs, slopes_rows, back):
    return pl.pallas_call(
        weight_kernel,
        in_specs=[HBM, HBM, VMEM, HBM],
        out_shape=jax.ShapeDtypeStruct((LAYERS, SLOTS, SLOTS), BF16),
        scratch_shapes=[
            pltpu.VMEM((CHIPS, OWN, SLICE), BF16),
            pltpu.VMEM((CHIPS, OWN, SLICE), BF16),
            pltpu.VMEM((LAYERS, 96, SLOTS), BF16),
            pltpu.SemaphoreType.DMA((3,)),
        ],
        compiler_params=params(16),
        cost_estimate=cost(2 * 256 * 2048 * 256, 3 << 20),
        name="weight_parts",
    )(mine, theirs, slopes_rows, back)


RETURN_ROWS = 112


def return_kernel(
    back_hbm, recv_hbm, hubs_hbm, out_hbm,
    back_ref, part_ref, recv_ref, hubs_ref, out_ref, in_sems, out_sems,
):
    staged = copies(
        in_sems,
        (recv_hbm, recv_ref),
        (hubs_hbm, hubs_ref),
        (back_hbm.at[:, :OWN, :], back_ref),
        (back_hbm.at[:, 96:, :], part_ref),
    )
    node = lax.broadcasted_iota(jnp.int32, (NODES, 2 * SLOTS), 0)
    staged[2].wait()
    share = back_ref[...].astype(F32).reshape(NODES, SLOTS).T[FEATS:, :].astype(BF16)
    staged[0].wait()
    staged[3].wait()
    sums = jnp.sum(part_ref[...].astype(F32), axis=0).astype(BF16)
    sent = []
    for pair in range(PEERS // 2):
        values = matmul(share, one_hot(node == pair_lanes(recv_ref, pair)), NN).astype(BF16)
        for side in range(2):
            peer = 2 * pair + side
            out_ref[peer, :FEATS, :] = values[:, SLOTS * side : SLOTS * (side + 1)]
            out_ref[peer, ROWS:, :] = sums
        if pair == 3:
            staged[1].wait()
            terms = matmul(share, hubs_ref[...], NT).T
            high = terms.astype(BF16).astype(F32)
            both = jnp.concatenate([high, terms - high], axis=1)
            out_ref[:, FEATS:ROWS, :] = both.reshape(PEERS, HUBS_OWN, SLOTS).astype(BF16)
        if pair % 4 == 3:
            part = pl.ds(2 * pair - 6, 8)
            copy = pltpu.make_async_copy(out_ref.at[part], out_hbm.at[part], out_sems.at[pair // 4])
            copy.start()
            sent.append(copy)
    for copy in sent:
        copy.wait()


def return_slots(back_block, recv_lanes, hubs):
    return pl.pallas_call(
        return_kernel,
        in_specs=[HBM, HBM, HBM],
        out_specs=HBM,
        out_shape=jax.ShapeDtypeStruct((PEERS, RETURN_ROWS, SLOTS), BF16),
        scratch_shapes=[
            pltpu.VMEM((LAYERS, OWN, SLOTS), BF16),
            pltpu.VMEM((LAYERS, 32, SLOTS), BF16),
            pltpu.VMEM((PEERS, SLOTS), jnp.int32),
            pltpu.VMEM((HUBS, NODES), BF16),
            pltpu.VMEM((PEERS, RETURN_ROWS, SLOTS), BF16),
            pltpu.SemaphoreType.DMA((4,)),
            pltpu.SemaphoreType.DMA((4,)),
        ],
        compiler_params=params(60),
        cost_estimate=cost(2 * 256 * 4608 * 1024, 3 << 20),
        name="return_slots",
    )(back_block, recv_lanes, hubs)


def local_kernel(back_ref, local_ref, base_hbm, hidden_ref, base_ref, sems):
    columns = back_ref[:, :OWN, :].astype(F32).reshape(NODES, SLOTS).T
    share = columns[FEATS:, :].astype(BF16)
    base_ref[...] = columns[:FEATS, :] + matmul(share, local_ref[...], NT)
    (sent,) = copies(sems, (base_ref, base_hbm.at[:FEATS]))
    folded = back_ref[:, OWN:96, :].astype(F32)
    rows = jnp.concatenate([folded[:, :, :FEATS], folded[:, :, FEATS:]], axis=1)
    hidden_ref[...] = rows.reshape(NODES, FEATS).T.astype(BF16)
    sent.wait()


def local_grads(back_block, local):
    return pl.pallas_call(
        local_kernel,
        out_specs=[HBM, VMEM],
        out_shape=[
            jax.ShapeDtypeStruct((KEPT, NODES), F32),
            jax.ShapeDtypeStruct((FEATS, NODES), BF16),
        ],
        scratch_shapes=[pltpu.VMEM((FEATS, NODES), F32), pltpu.SemaphoreType.DMA((1,))],
        compiler_params=params(60),
        cost_estimate=cost(2 * 256 * 1024 * 1024, 3 << 20),
        name="local_grads",
    )(back_block, local)


SPREAD = 256


def spread_kernel(
    back_ref, send_hbm, hub_hbm, base_hbm, out_ref, self_hbm, neigh_hbm,
    send_ref, hub_ref, base_ref, grads_ref, slots, in_sems, out_sems,
):
    staged = copies(in_sems, (send_hbm, send_ref), (hub_hbm, hub_ref), (base_hbm.at[:FEATS], base_ref))
    for peer in range(PEERS):
        slots[:, SLOTS * peer : SLOTS * (peer + 1)] = back_ref[peer, :FEATS, :]
        grads = back_ref[peer, ROWS:, :].astype(F32)
        slice_of, start = peer // 8, HALF * (peer % 2) + SLOTS * (peer // 2 % 4)
        grads_ref[PIECE * slice_of : PIECE * (slice_of + 1), start : start + SLOTS] = grads
    sent = copies(
        out_sems, (grads_ref.at[:FEATS], self_hbm), (grads_ref.at[FEATS:], neigh_hbm)
    )
    sums = jnp.sum(back_ref[:, FEATS:ROWS, :].astype(F32), axis=0)
    total = sums[:, :FEATS] + sums[:, FEATS:]
    high = total.astype(BF16).astype(F32)
    hub_high = high.T.astype(BF16)
    hub_low = (total - high).T.astype(BF16)
    for copy in staged:
        copy.wait()
    for tile in range(NODES // SPREAD):
        lanes = slice(SPREAD * tile, SPREAD * (tile + 1))
        node = lax.broadcasted_iota(jnp.int32, (SPREAD, 2 * SLOTS), 0) + SPREAD * tile
        grad = base_ref[:, lanes]
        for pair in range(PEERS // 2):
            grad = grad + matmul(
                slots[:, 2 * SLOTS * pair : 2 * SLOTS * (pair + 1)],
                one_hot(node == pair_lanes(send_ref, pair)),
                NT,
            )
        hub_node = lax.broadcasted_iota(jnp.int32, (SPREAD, HUBS_OWN), 0) + SPREAD * tile
        hub_hot = one_hot(hub_node == hub_ref[...])
        grad = grad + matmul(hub_high, hub_hot, NT) + matmul(hub_low, hub_hot, NT)
        out_ref[:, lanes] = grad.astype(BF16)
    for copy in sent:
        copy.wait()


def spread_grads(returned, send_lanes, hub_own, base):
    return pl.pallas_call(
        spread_kernel,
        in_specs=[VMEM, HBM, HBM, HBM],
        out_specs=[VMEM, HBM, HBM],
        out_shape=[
            jax.ShapeDtypeStruct((FEATS, NODES), BF16),
            jax.ShapeDtypeStruct((FEATS, OUTS), F32),
            jax.ShapeDtypeStruct((FEATS, OUTS), F32),
        ],
        scratch_shapes=[
            pltpu.VMEM((PEERS, SLOTS), jnp.int32),
            pltpu.VMEM((1, HUBS_OWN), jnp.int32),
            pltpu.VMEM((FEATS, NODES), F32),
            pltpu.VMEM((2 * FEATS, OUTS), F32),
            pltpu.VMEM((FEATS, PEERS * SLOTS), BF16),
            pltpu.SemaphoreType.DMA((3,)),
            pltpu.SemaphoreType.DMA((2,)),
        ],
        compiler_params=params(52),
        cost_estimate=cost(2 * 256 * 4224 * 1024, 2 << 20),
        name="spread_grads",
    )(returned, send_lanes, hub_own, base)


SAME_CORE = [list(range(core, PEERS, 2)) for core in range(2)]


def exchange(blocks, axis, groups=None):
    return lax.all_to_all(blocks, axis, 0, 0, axis_index_groups=groups, tiled=True)


def other_core(block):
    return lax.ppermute(block, "row", [(i, i ^ 1) for i in range(PEERS)])


def per_device(feats, w_self, w_neigh, cotangent, loc_nbr, send_rows, recv_node, hub_rows, hub_nbr):
    send_lanes = send_rows.reshape(PEERS, SLOTS)
    recv_lanes = recv_node.reshape(PEERS, SLOTS)
    hub_own = hub_rows[None, :]
    half = HALF * (lax.axis_index("row") % 2)
    weights = lax.all_gather(
        lax.dynamic_slice_in_dim(jnp.concatenate([w_self, w_neigh], axis=0), half, HALF, 1),
        "col",
        axis=0,
        tiled=True,
    )
    incoming = exchange(gather_slots(feats, send_lanes, hub_own), "row")
    hub_lanes = hub_nbr.T
    local, hubs, local_sum = build_counts(feats, loc_nbr.T, hub_lanes)
    outgoing, degree = aggregate(feats, incoming, recv_lanes, local_sum, hub_lanes, cotangent)
    node_block = exchange(outgoing, "col")
    own_degree = lax.dynamic_slice_in_dim(degree[0], OWN * lax.axis_index("col"), OWN)[:, None]
    joined_mine = exchange(regroup(node_block), "row", SAME_CORE)
    joined, cots = prepare(node_block, other_core(node_block))
    slopes_out, slopes, hidden = forward(joined, cots, weights)
    slopes_rows = exchange(slopes_out, "row", SAME_CORE)
    joined_mine, slopes = lax.optimization_barrier((joined_mine, slopes))
    joined_theirs = other_core(joined_mine)
    mine, theirs, my_hidden, their_hidden = backward(slopes, hidden, weights)
    back = combine(mine, other_core(theirs), my_hidden, other_core(their_hidden), own_degree)
    back_block = exchange(weight_parts(joined_mine, joined_theirs, slopes_rows, back), "col")
    returned = exchange(return_slots(back_block, recv_lanes, hubs), "row")
    base, hidden_out = local_grads(back_block, local)
    grad_feats, grad_self, grad_neigh = spread_grads(returned, send_lanes, hub_own, base)
    return (hidden_out, grad_feats, grad_self, grad_neigh)


def solution(mesh):
    return jax.shard_map(
        per_device,
        mesh=mesh,
        in_specs=(
            P("col", "row"),
            P("col", None),
            P("col", None),
            P("col", "row"),
            P("row", None),
            P("row", None, None),
            P("row", None, None),
            P("row"),
            P("row", None),
        ),
        out_specs=(P("col", "row"), P("col", "row"), P("col", None), P("col", None)),
        check_vma=False,
    )
```

```python
import jax
import jax.numpy as jnp
from jax import lax
from jax.experimental import pallas as pl
from jax.experimental.pallas import tpu as pltpu
from jax.sharding import PartitionSpec as P

NODES = 1024
FEATS = 64
PEERS = 32
SLOTS = 128
HUBS_OWN = 16
HUBS = 512
ROWS = 80
LAYERS = 16
OWN = 64
OUTS = 1024
BF16 = jnp.bfloat16
F32 = jnp.float32
NT = (((1,), (1,)), ((), ()))
NN = (((1,), (0,)), ((), ()))
MIB = 1 << 20


def params(mib):
    return pltpu.CompilerParams(vmem_limit_bytes=mib * MIB)


def cost(flops, moved):
    return pl.CostEstimate(flops=flops, bytes_accessed=moved, transcendentals=0)


def whole(shape):
    return pl.BlockSpec(shape, lambda *_: (0,) * len(shape))


HBM = pl.BlockSpec(memory_space=pltpu.HBM)
VMEM = pl.BlockSpec(memory_space=pltpu.VMEM)


def copies(sems, *pairs):
    started = []
    for i, (source, target) in enumerate(pairs):
        copy = pltpu.make_async_copy(source, target, sems.at[i])
        copy.start()
        started.append(copy)
    return started


def one_hot(mask):
    return jnp.where(mask, 1.0, 0.0).astype(BF16)


def matmul(a, b, dims):
    return lax.dot_general(a, b, dims, preferred_element_type=F32)


def pair_lanes(ref, pair):
    return jnp.concatenate([ref[2 * pair : 2 * pair + 1, :], ref[2 * pair + 1 : 2 * pair + 2, :]], axis=1)


def gather_kernel(x_hbm, send_hbm, hub_hbm, out_ref, x_ref, send_ref, hub_ref, sems):
    for copy in copies(sems, (x_hbm, x_ref), (send_hbm, send_ref), (hub_hbm, hub_ref)):
        copy.wait()
    x = x_ref[...]
    node = lax.broadcasted_iota(jnp.int32, (NODES, 2 * SLOTS), 0)
    hub_node = lax.broadcasted_iota(jnp.int32, (NODES, HUBS_OWN), 0)
    hub_feats = matmul(x, one_hot(hub_node == hub_ref[...]), NN)
    hub_rows = hub_feats.T
    hub_block = jnp.concatenate([hub_rows, jnp.zeros_like(hub_rows)], axis=1).astype(BF16)
    for pair in range(PEERS // 2):
        picked = matmul(x, one_hot(node == pair_lanes(send_ref, pair)), NN).astype(BF16)
        out_ref[2 * pair, :FEATS, :] = picked[:, :SLOTS]
        out_ref[2 * pair + 1, :FEATS, :] = picked[:, SLOTS:]
        out_ref[2 * pair, FEATS:, :] = hub_block
        out_ref[2 * pair + 1, FEATS:, :] = hub_block


def gather_slots(feats, send_lanes, hub_own):
    return pl.pallas_call(
        gather_kernel,
        in_specs=[HBM, HBM, HBM],
        out_shape=jax.ShapeDtypeStruct((PEERS, ROWS, SLOTS), BF16),
        scratch_shapes=[
            pltpu.VMEM((FEATS, NODES), BF16),
            pltpu.VMEM((PEERS, SLOTS), jnp.int32),
            pltpu.VMEM((1, HUBS_OWN), jnp.int32),
            pltpu.SemaphoreType.DMA((3,)),
        ],
        compiler_params=params(60),
        cost_estimate=cost(2 * 256 * 4096 * 1024, 1 << 20),
        name="gather_slots",
    )(feats, send_lanes, hub_own)


BUILD = 256
KEPT = 512


def counts_of(nbr_ref, rows):
    first = lax.broadcasted_iota(jnp.int32, (rows, nbr_ref.shape[1]), 0)
    counts = jnp.zeros(first.shape, F32)
    for k in range(nbr_ref.shape[0]):
        counts = counts + jnp.where(first == nbr_ref[k : k + 1, :], 1.0, 0.0)
    return counts.astype(BF16)


def build_kernel(x_ref, loc_ref, hub_ref, local_ref, hubs_ref, sum_ref):
    counts = counts_of(loc_ref, NODES)
    local_ref[...] = counts
    hubs_ref[...] = counts_of(hub_ref, HUBS)
    sum_ref[...] = matmul(x_ref[...], counts, NN)


def build_counts(feats, loc_lanes, hub_lanes):
    return pl.pallas_call(
        build_kernel,
        grid=(NODES // BUILD,),
        in_specs=[
            whole((FEATS, NODES)),
            pl.BlockSpec((loc_lanes.shape[0], BUILD), lambda i: (0, i)),
            pl.BlockSpec((hub_lanes.shape[0], BUILD), lambda i: (0, i)),
        ],
        out_specs=[
            pl.BlockSpec((NODES, BUILD), lambda i: (0, i)),
            pl.BlockSpec((HUBS, BUILD), lambda i: (0, i)),
            pl.BlockSpec((FEATS, BUILD), lambda i: (0, i)),
        ],
        out_shape=[
            jax.ShapeDtypeStruct((NODES, NODES), BF16),
            jax.ShapeDtypeStruct((HUBS, NODES), BF16),
            jax.ShapeDtypeStruct((KEPT, NODES), F32),
        ],
        compiler_params=params(60),
        cost_estimate=cost(1 << 30, 4 << 20),
        name="build_counts",
    )(feats, loc_lanes, hub_lanes)


AGG = 256


def fold_halves(block):
    return jnp.concatenate([block[: OWN // 2, :], block[OWN // 2 :, :]], axis=1)


NEIGHBOURS = 10.0


def aggregate_kernel(
    x_hbm, inc_ref, recv_hbm, sum_hbm, hub_hbm, cot_hbm, out_ref, degree_ref,
    slots, table, recv_ref, hub_ref, x_ref, cot_ref, sum_ref, sems,
):
    staged = copies(
        sems,
        (recv_hbm, recv_ref),
        (hub_hbm, hub_ref),
        (x_hbm, x_ref),
        (cot_hbm, cot_ref),
        (sum_hbm.at[:FEATS], sum_ref),
    )
    for peer in range(PEERS):
        slots[:FEATS, SLOTS * peer : SLOTS * (peer + 1)] = inc_ref[peer, :FEATS, :]
    slots[FEATS:, :] = jnp.ones((16, PEERS * SLOTS), BF16)
    rows = inc_ref[:, FEATS:, :].astype(F32).reshape(HUBS, SLOTS)
    table[...] = rows.T[:FEATS, :].astype(BF16)
    staged[0].wait()
    for tile in range(NODES // AGG):
        lanes = slice(AGG * tile, AGG * (tile + 1))
        node = lax.broadcasted_iota(jnp.int32, (AGG, 2 * SLOTS), 0) + AGG * tile
        remote = jnp.zeros((ROWS, AGG), F32)
        for pair in range(PEERS // 2):
            remote = remote + matmul(
                slots[:, 2 * SLOTS * pair : 2 * SLOTS * (pair + 1)],
                one_hot(node == pair_lanes(recv_ref, pair)),
                NT,
            )
        if tile == 0:
            for copy in staged[1:]:
                copy.wait()
        hubs = counts_of(hub_ref[:, lanes], HUBS)
        total = remote[:FEATS, :] + sum_ref[:, lanes] + matmul(table[...], hubs, NN)
        degree = remote[FEATS : FEATS + 8, :] + NEIGHBOURS
        degree_ref[:, lanes] = degree
        mean = (total / degree[0:1, :]).T
        nodes = jnp.concatenate([x_ref[:, lanes].astype(F32).T, mean], axis=1).astype(BF16)
        slopes = cot_ref[:, lanes].astype(F32).T
        for part in range(AGG // OWN):
            layer = AGG // OWN * tile + part
            out_ref[layer, :OWN, :] = nodes[OWN * part : OWN * (part + 1), :]
            out_ref[layer, OWN:, :] = fold_halves(slopes[OWN * part : OWN * (part + 1), :]).astype(BF16)


def aggregate(feats, incoming, recv_lanes, local_sum, hub_lanes, cotangent):
    return pl.pallas_call(
        aggregate_kernel,
        out_shape=[
            jax.ShapeDtypeStruct((LAYERS, 96, SLOTS), BF16),
            jax.ShapeDtypeStruct((8, NODES), F32),
        ],
        in_specs=[HBM, VMEM, HBM, HBM, HBM, HBM],
        scratch_shapes=[
            pltpu.VMEM((ROWS, PEERS * SLOTS), BF16),
            pltpu.VMEM((FEATS, HUBS), BF16),
            pltpu.VMEM((PEERS, SLOTS), jnp.int32),
            pltpu.VMEM((2, NODES), jnp.int32),
            pltpu.VMEM((FEATS, NODES), BF16),
            pltpu.VMEM((FEATS, NODES), BF16),
            pltpu.VMEM((FEATS, NODES), F32),
            pltpu.SemaphoreType.DMA((5,)),
        ],
        compiler_params=params(52),
        cost_estimate=cost(2 * 256 * 5632 * 1024, 3 << 20),
        name="aggregate",
    )(feats, incoming, recv_lanes, local_sum, hub_lanes, cotangent)


PIECE = 32
TILE = 256
CHIPS = PEERS // 2
SLICE = LAYERS * PIECE


def regroup_kernel(inc_ref, out_ref):
    group = lax.broadcasted_iota(jnp.int32, (OWN, SLOTS), 1) // PIECE
    for part in range(4):
        blocks = [inc_ref[4 * part + i, :OWN, :].astype(F32) for i in range(4)]
        for slice_of in range(4):
            tile = jnp.zeros((OWN, SLOTS), F32)
            for i in range(4):
                moved = blocks[i]
                if i != slice_of:
                    moved = pltpu.roll(moved, (PIECE * (i - slice_of)) % SLOTS, 1)
                tile = jnp.where(group == i, moved, tile)
            tile = tile.astype(BF16)
            for outs in range(4):
                out_ref[4 * slice_of + outs, :, SLOTS * part : SLOTS * (part + 1)] = tile


def regroup(node_block):
    return pl.pallas_call(
        regroup_kernel,
        out_shape=jax.ShapeDtypeStruct((CHIPS, OWN, SLICE), BF16),
        compiler_params=params(16),
        cost_estimate=cost(1 << 24, 2 << 20),
        name="regroup",
    )(node_block)


HALF = OUTS // 2


def prepare_kernel(own_block, other_block, joined_ref, cot_ref):
    core = lax.axis_index("row") % 2
    for layer in range(LAYERS):
        lanes = slice(SLOTS * layer, SLOTS * (layer + 1))
        joined_ref[0, :, lanes] = own_block[layer, :OWN, :]
        joined_ref[1, :, lanes] = other_block[layer, :OWN, :]
    for side, block in enumerate((own_block, other_block)):
        for pair in range(LAYERS // 4):
            even = block[8 * core + 2 * pair, OWN:, :].astype(F32)
            odd = block[8 * core + 2 * pair + 1, OWN:, :].astype(F32)
            top = jnp.concatenate([even[:, :FEATS], odd[:, :FEATS]], axis=1)
            bottom = jnp.concatenate([even[:, FEATS:], odd[:, FEATS:]], axis=1)
            cot_ref[side, :, SLOTS * pair : SLOTS * (pair + 1)] = jnp.concatenate(
                [top, bottom], axis=0
            ).astype(BF16)


def prepare(own_block, other_block):
    return pl.pallas_call(
        prepare_kernel,
        out_shape=[
            jax.ShapeDtypeStruct((2, OWN, 2 * OUTS), BF16),
            jax.ShapeDtypeStruct((2, OWN, HALF), BF16),
        ],
        compiler_params=params(16),
        cost_estimate=cost(1 << 20, 2 << 20),
        name="prepare",
    )(own_block, other_block)


def forward_kernel(
    joined_hbm, cot_hbm, weights_hbm, slopes_hbm, flat_hbm, hidden_hbm,
    joined, cots, weights, out_tile, flat, hidden, in_sems, out_sems,
):
    staged = copies(
        in_sems,
        (joined_hbm, joined),
        (weights_hbm.at[:, :TILE], weights.at[:, :TILE]),
        (cot_hbm, cots),
        (weights_hbm.at[:, TILE:], weights.at[:, TILE:]),
    )
    staged[0].wait()
    sent = []
    for side in range(2):
        staged[2 * side + 1].wait()
        columns = slice(TILE * side, TILE * (side + 1))
        preact = matmul(joined[...].reshape(2 * OWN, 2 * OUTS), weights[:, columns], NN)
        if side == 0:
            staged[2].wait()
        sigmoid_part = jax.nn.sigmoid(preact)
        silu = preact * sigmoid_part
        slope = sigmoid_part * (1.0 + preact * (1.0 - sigmoid_part))
        cot = cots[:, :, columns].reshape(2 * OWN, TILE).astype(F32)
        slopes = (cot * slope).astype(BF16)
        for outs in range(2):
            out_tile[2 * side + outs] = slopes[:, SLOTS * outs : SLOTS * (outs + 1)]
        for chip in range(CHIPS):
            if chip % 4 // 2 == side:
                copy = pltpu.make_async_copy(
                    out_tile.at[chip % 4], slopes_hbm.at[chip], out_sems.at[chip]
                )
                copy.start()
                sent.append(copy)
        flat[:, columns] = slopes
        for block in range(2):
            for layer in range(4):
                tile = silu[OWN * block : OWN * (block + 1), FEATS * layer : FEATS * (layer + 1)]
                hidden[block, 4 * side + layer] = fold_halves(tile).astype(BF16)
    for i, (source, target) in enumerate(((flat, flat_hbm), (hidden, hidden_hbm))):
        copy = pltpu.make_async_copy(source, target, out_sems.at[CHIPS + i])
        copy.start()
        sent.append(copy)
    for copy in sent:
        copy.wait()


def forward(joined, cots, weights):
    return pl.pallas_call(
        forward_kernel,
        in_specs=[HBM, HBM, HBM],
        out_specs=[HBM, HBM, HBM],
        out_shape=[
            jax.ShapeDtypeStruct((CHIPS, 2 * OWN, SLOTS), BF16),
            jax.ShapeDtypeStruct((2 * OWN, HALF), BF16),
            jax.ShapeDtypeStruct((2, LAYERS // 2, OWN // 2, SLOTS), BF16),
        ],
        scratch_shapes=[
            pltpu.VMEM((2, OWN, 2 * OUTS), BF16),
            pltpu.VMEM((2, OWN, HALF), BF16),
            pltpu.VMEM((2 * OUTS, HALF), BF16),
            pltpu.VMEM((4, 2 * OWN, SLOTS), BF16),
            pltpu.VMEM((2 * OWN, HALF), BF16),
            pltpu.VMEM((2, LAYERS // 2, OWN // 2, SLOTS), BF16),
            pltpu.SemaphoreType.DMA((4,)),
            pltpu.SemaphoreType.DMA((CHIPS + 2,)),
        ],
        compiler_params=params(60),
        cost_estimate=cost(2 * 256 * 2048 * 512, 4 << 20),
        name="forward",
    )(joined, cots, weights)


SWAP = LAYERS + 4


def backward_kernel(slopes_ref, hidden_ref, weights_ref, keep_ref, send_ref):
    back = matmul(slopes_ref[...], weights_ref[...], NT)
    keep_ref[...] = back[:OWN, :]
    for layer in range(LAYERS):
        send_ref[layer] = back[OWN:, SLOTS * layer : SLOTS * (layer + 1)].astype(BF16)
    for pair in range(LAYERS // 4):
        send_ref[LAYERS + pair] = hidden_ref[1, 2 * pair : 2 * pair + 2].reshape(OWN, SLOTS)


def backward(slopes, hidden, weights):
    return pl.pallas_call(
        backward_kernel,
        out_shape=[
            jax.ShapeDtypeStruct((OWN, 2 * OUTS), F32),
            jax.ShapeDtypeStruct((SWAP, OWN, SLOTS), BF16),
        ],
        compiler_params=params(16),
        cost_estimate=cost(2 * 256 * 2048 * 512, 4 << 20),
        name="backward",
    )(slopes, hidden, weights)


def weight_kernel(
    mine_hbm, theirs_hbm, slopes_ref, keep_hbm, swapped_hbm, hidden_hbm, degree_hbm, out_ref,
    mine, theirs, keep, swapped, hidden, degree, sems,
):
    core = lax.axis_index("row") % 2
    staged = copies(
        sems,
        (degree_hbm, degree),
        (keep_hbm, keep),
        (swapped_hbm, swapped),
        (hidden_hbm.at[0], hidden),
        (mine_hbm, mine),
        (theirs_hbm, theirs),
    )
    slopes = [
        slopes_ref[:, OWN * side : OWN * (side + 1), :].astype(F32).reshape(CHIPS * OWN, SLOTS)
        for side in range(2)
    ]
    columns = [rows.T.astype(BF16) for rows in slopes]
    for copy in staged[:4]:
        copy.wait()
    direct = lax.broadcasted_iota(jnp.int32, (OWN, SLOTS), 1) < FEATS
    divisor = jnp.where(direct, 1.0, degree[...])
    for layer in range(LAYERS):
        back = keep[:, SLOTS * layer : SLOTS * (layer + 1)] + swapped[layer].astype(F32)
        out_ref[layer, :OWN, :] = (back / divisor).astype(BF16)
    for pair in range(LAYERS // 4):
        for side in range(2):
            layer = 2 * pair + side
            out_ref[8 * core + layer, OWN:96, :] = hidden[layer]
            out_ref[8 * (1 - core) + layer, OWN:96, :] = swapped[
                LAYERS + pair, OWN // 2 * side : OWN // 2 * (side + 1), :
            ]
    part = jnp.zeros((SLOTS, SLICE), F32)
    for side, rows in enumerate((mine, theirs)):
        staged[4 + side].wait()
        part = part + matmul(columns[side], rows[...].reshape(CHIPS * OWN, SLICE), NN)
    part = part.T.astype(BF16)
    for layer in range(LAYERS):
        out_ref[layer, 96:, :] = part[PIECE * layer : PIECE * (layer + 1), :]


def weight_parts(mine, theirs, slopes_rows, keep, swapped, hidden, own_degree):
    return pl.pallas_call(
        weight_kernel,
        in_specs=[HBM, HBM, VMEM, HBM, HBM, HBM, HBM],
        out_shape=jax.ShapeDtypeStruct((LAYERS, SLOTS, SLOTS), BF16),
        scratch_shapes=[
            pltpu.VMEM((CHIPS, OWN, SLICE), BF16),
            pltpu.VMEM((CHIPS, OWN, SLICE), BF16),
            pltpu.VMEM((OWN, 2 * OUTS), F32),
            pltpu.VMEM((SWAP, OWN, SLOTS), BF16),
            pltpu.VMEM((LAYERS // 2, OWN // 2, SLOTS), BF16),
            pltpu.VMEM((OWN, 1), F32),
            pltpu.SemaphoreType.DMA((6,)),
        ],
        compiler_params=params(52),
        cost_estimate=cost(2 * 256 * 2048 * 256, 4 << 20),
        name="weight_parts",
    )(mine, theirs, slopes_rows, keep, swapped, hidden, own_degree)


RETURN_ROWS = 112


def return_kernel(
    back_hbm, recv_hbm, hubs_hbm, out_hbm,
    back_ref, part_ref, recv_ref, hubs_ref, out_ref, in_sems, out_sems,
):
    staged = copies(
        in_sems,
        (recv_hbm, recv_ref),
        (hubs_hbm, hubs_ref),
        (back_hbm.at[:, :OWN, :], back_ref),
        (back_hbm.at[:, 96:, :], part_ref),
    )
    node = lax.broadcasted_iota(jnp.int32, (NODES, 2 * SLOTS), 0)
    staged[2].wait()
    share = back_ref[...].astype(F32).reshape(NODES, SLOTS).T[FEATS:, :].astype(BF16)
    staged[0].wait()
    staged[3].wait()
    sums = jnp.sum(part_ref[...].astype(F32), axis=0).astype(BF16)
    sent = []
    for pair in range(PEERS // 2):
        values = matmul(share, one_hot(node == pair_lanes(recv_ref, pair)), NN).astype(BF16)
        for side in range(2):
            peer = 2 * pair + side
            out_ref[peer, :FEATS, :] = values[:, SLOTS * side : SLOTS * (side + 1)]
            out_ref[peer, ROWS:, :] = sums
        if pair == 3:
            staged[1].wait()
            terms = matmul(share, hubs_ref[...], NT).T
            high = terms.astype(BF16).astype(F32)
            both = jnp.concatenate([high, terms - high], axis=1)
            out_ref[:, FEATS:ROWS, :] = both.reshape(PEERS, HUBS_OWN, SLOTS).astype(BF16)
        if pair % 4 == 3:
            part = pl.ds(2 * pair - 6, 8)
            copy = pltpu.make_async_copy(out_ref.at[part], out_hbm.at[part], out_sems.at[pair // 4])
            copy.start()
            sent.append(copy)
    for copy in sent:
        copy.wait()


def return_slots(back_block, recv_lanes, hubs):
    return pl.pallas_call(
        return_kernel,
        in_specs=[HBM, HBM, HBM],
        out_specs=HBM,
        out_shape=jax.ShapeDtypeStruct((PEERS, RETURN_ROWS, SLOTS), BF16),
        scratch_shapes=[
            pltpu.VMEM((LAYERS, OWN, SLOTS), BF16),
            pltpu.VMEM((LAYERS, 32, SLOTS), BF16),
            pltpu.VMEM((PEERS, SLOTS), jnp.int32),
            pltpu.VMEM((HUBS, NODES), BF16),
            pltpu.VMEM((PEERS, RETURN_ROWS, SLOTS), BF16),
            pltpu.SemaphoreType.DMA((4,)),
            pltpu.SemaphoreType.DMA((4,)),
        ],
        compiler_params=params(60),
        cost_estimate=cost(2 * 256 * 4608 * 1024, 3 << 20),
        name="return_slots",
    )(back_block, recv_lanes, hubs)


def local_kernel(back_ref, local_ref, base_hbm, hidden_ref, base_ref, sems):
    columns = back_ref[:, :OWN, :].astype(F32).reshape(NODES, SLOTS).T
    share = columns[FEATS:, :].astype(BF16)
    base_ref[...] = columns[:FEATS, :] + matmul(share, local_ref[...], NT)
    (sent,) = copies(sems, (base_ref, base_hbm.at[:FEATS]))
    folded = back_ref[:, OWN:96, :].astype(F32)
    rows = jnp.concatenate([folded[:, :, :FEATS], folded[:, :, FEATS:]], axis=1)
    hidden_ref[...] = rows.reshape(NODES, FEATS).T.astype(BF16)
    sent.wait()


def local_grads(back_block, local):
    return pl.pallas_call(
        local_kernel,
        out_specs=[HBM, VMEM],
        out_shape=[
            jax.ShapeDtypeStruct((KEPT, NODES), F32),
            jax.ShapeDtypeStruct((FEATS, NODES), BF16),
        ],
        scratch_shapes=[pltpu.VMEM((FEATS, NODES), F32), pltpu.SemaphoreType.DMA((1,))],
        compiler_params=params(60),
        cost_estimate=cost(2 * 256 * 1024 * 1024, 3 << 20),
        name="local_grads",
    )(back_block, local)


SPREAD = 256


def spread_kernel(
    back_ref, send_hbm, hub_hbm, base_hbm, out_ref, self_hbm, neigh_hbm,
    send_ref, hub_ref, base_ref, grads_ref, slots, in_sems, out_sems,
):
    staged = copies(in_sems, (send_hbm, send_ref), (hub_hbm, hub_ref), (base_hbm.at[:FEATS], base_ref))
    for peer in range(PEERS):
        slots[:, SLOTS * peer : SLOTS * (peer + 1)] = back_ref[peer, :FEATS, :]
        grads = back_ref[peer, ROWS:, :].astype(F32)
        slice_of, start = peer // 8, HALF * (peer % 2) + SLOTS * (peer // 2 % 4)
        grads_ref[PIECE * slice_of : PIECE * (slice_of + 1), start : start + SLOTS] = grads
    sent = copies(
        out_sems, (grads_ref.at[:FEATS], self_hbm), (grads_ref.at[FEATS:], neigh_hbm)
    )
    sums = jnp.sum(back_ref[:, FEATS:ROWS, :].astype(F32), axis=0)
    total = sums[:, :FEATS] + sums[:, FEATS:]
    high = total.astype(BF16).astype(F32)
    hub_high = high.T.astype(BF16)
    hub_low = (total - high).T.astype(BF16)
    for copy in staged:
        copy.wait()
    for tile in range(NODES // SPREAD):
        lanes = slice(SPREAD * tile, SPREAD * (tile + 1))
        node = lax.broadcasted_iota(jnp.int32, (SPREAD, 2 * SLOTS), 0) + SPREAD * tile
        grad = base_ref[:, lanes]
        for pair in range(PEERS // 2):
            grad = grad + matmul(
                slots[:, 2 * SLOTS * pair : 2 * SLOTS * (pair + 1)],
                one_hot(node == pair_lanes(send_ref, pair)),
                NT,
            )
        hub_node = lax.broadcasted_iota(jnp.int32, (SPREAD, HUBS_OWN), 0) + SPREAD * tile
        hub_hot = one_hot(hub_node == hub_ref[...])
        grad = grad + matmul(hub_high, hub_hot, NT) + matmul(hub_low, hub_hot, NT)
        out_ref[:, lanes] = grad.astype(BF16)
    for copy in sent:
        copy.wait()


def spread_grads(returned, send_lanes, hub_own, base):
    return pl.pallas_call(
        spread_kernel,
        in_specs=[VMEM, HBM, HBM, HBM],
        out_specs=[VMEM, HBM, HBM],
        out_shape=[
            jax.ShapeDtypeStruct((FEATS, NODES), BF16),
            jax.ShapeDtypeStruct((FEATS, OUTS), F32),
            jax.ShapeDtypeStruct((FEATS, OUTS), F32),
        ],
        scratch_shapes=[
            pltpu.VMEM((PEERS, SLOTS), jnp.int32),
            pltpu.VMEM((1, HUBS_OWN), jnp.int32),
            pltpu.VMEM((FEATS, NODES), F32),
            pltpu.VMEM((2 * FEATS, OUTS), F32),
            pltpu.VMEM((FEATS, PEERS * SLOTS), BF16),
            pltpu.SemaphoreType.DMA((3,)),
            pltpu.SemaphoreType.DMA((2,)),
        ],
        compiler_params=params(52),
        cost_estimate=cost(2 * 256 * 4224 * 1024, 2 << 20),
        name="spread_grads",
    )(returned, send_lanes, hub_own, base)


SAME_CORE = [list(range(core, PEERS, 2)) for core in range(2)]


def exchange(blocks, axis, groups=None):
    return lax.all_to_all(blocks, axis, 0, 0, axis_index_groups=groups, tiled=True)


def other_core(block):
    return lax.ppermute(block, "row", [(i, i ^ 1) for i in range(PEERS)])


def per_device(feats, w_self, w_neigh, cotangent, loc_nbr, send_rows, recv_node, hub_rows, hub_nbr):
    send_lanes = send_rows.reshape(PEERS, SLOTS)
    recv_lanes = recv_node.reshape(PEERS, SLOTS)
    hub_own = hub_rows[None, :]
    half = HALF * (lax.axis_index("row") % 2)
    weights = lax.all_gather(
        lax.dynamic_slice_in_dim(jnp.concatenate([w_self, w_neigh], axis=0), half, HALF, 1),
        "col",
        axis=0,
        tiled=True,
    )
    incoming = exchange(gather_slots(feats, send_lanes, hub_own), "row")
    hub_lanes = hub_nbr.T
    local, hubs, local_sum = build_counts(feats, loc_nbr.T, hub_lanes)
    outgoing, degree = aggregate(feats, incoming, recv_lanes, local_sum, hub_lanes, cotangent)
    node_block = exchange(outgoing, "col")
    own_degree = lax.dynamic_slice_in_dim(degree[0], OWN * lax.axis_index("col"), OWN)[:, None]
    joined_mine = exchange(regroup(node_block), "row", SAME_CORE)
    joined, cots = prepare(node_block, other_core(node_block))
    slopes_out, slopes, hidden = forward(joined, cots, weights)
    slopes_rows = exchange(slopes_out, "row", SAME_CORE)
    joined_mine, slopes = lax.optimization_barrier((joined_mine, slopes))
    joined_theirs = other_core(joined_mine)
    keep, sent = backward(slopes, hidden, weights)
    parts = weight_parts(
        joined_mine, joined_theirs, slopes_rows, keep, other_core(sent), hidden, own_degree
    )
    back_block = exchange(parts, "col")
    returned = exchange(return_slots(back_block, recv_lanes, hubs), "row")
    base, hidden_out = local_grads(back_block, local)
    grad_feats, grad_self, grad_neigh = spread_grads(returned, send_lanes, hub_own, base)
    return (hidden_out, grad_feats, grad_self, grad_neigh)


def solution(mesh):
    return jax.shard_map(
        per_device,
        mesh=mesh,
        in_specs=(
            P("col", "row"),
            P("col", None),
            P("col", None),
            P("col", "row"),
            P("row", None),
            P("row", None, None),
            P("row", None, None),
            P("row"),
            P("row", None),
        ),
        out_specs=(P("col", "row"), P("col", "row"), P("col", None), P("col", None)),
        check_vma=False,
    )
```

```python
import jax
import jax.numpy as jnp
from jax import lax
from jax.experimental import pallas as pl
from jax.experimental.pallas import tpu as pltpu
from jax.sharding import PartitionSpec as P

NODES = 1024
FEATS = 64
PEERS = 32
SLOTS = 128
HUBS_OWN = 16
HUBS = 512
ROWS = 80
LAYERS = 16
OWN = 64
OUTS = 1024
BF16 = jnp.bfloat16
F32 = jnp.float32
NT = (((1,), (1,)), ((), ()))
NN = (((1,), (0,)), ((), ()))
MIB = 1 << 20


def params(mib):
    return pltpu.CompilerParams(vmem_limit_bytes=mib * MIB)


def cost(flops, moved):
    return pl.CostEstimate(flops=flops, bytes_accessed=moved, transcendentals=0)


def whole(shape):
    return pl.BlockSpec(shape, lambda *_: (0,) * len(shape))


HBM = pl.BlockSpec(memory_space=pltpu.HBM)
VMEM = pl.BlockSpec(memory_space=pltpu.VMEM)


def copies(sems, *pairs):
    started = []
    for i, (source, target) in enumerate(pairs):
        copy = pltpu.make_async_copy(source, target, sems.at[i])
        copy.start()
        started.append(copy)
    return started


def one_hot(mask):
    return jnp.where(mask, 1.0, 0.0).astype(BF16)


def matmul(a, b, dims):
    return lax.dot_general(a, b, dims, preferred_element_type=F32)


def pair_lanes(ref, pair):
    return jnp.concatenate([ref[2 * pair : 2 * pair + 1, :], ref[2 * pair + 1 : 2 * pair + 2, :]], axis=1)


def gather_kernel(x_hbm, send_hbm, hub_hbm, out_ref, x_ref, send_ref, hub_ref, sems):
    for copy in copies(sems, (x_hbm, x_ref), (send_hbm, send_ref), (hub_hbm, hub_ref)):
        copy.wait()
    x = x_ref[...]
    node = lax.broadcasted_iota(jnp.int32, (NODES, 2 * SLOTS), 0)
    hub_node = lax.broadcasted_iota(jnp.int32, (NODES, HUBS_OWN), 0)
    hub_feats = matmul(x, one_hot(hub_node == hub_ref[...]), NN)
    hub_rows = hub_feats.T
    hub_block = jnp.concatenate([hub_rows, jnp.zeros_like(hub_rows)], axis=1).astype(BF16)
    for pair in range(PEERS // 2):
        picked = matmul(x, one_hot(node == pair_lanes(send_ref, pair)), NN).astype(BF16)
        out_ref[2 * pair, :FEATS, :] = picked[:, :SLOTS]
        out_ref[2 * pair + 1, :FEATS, :] = picked[:, SLOTS:]
        out_ref[2 * pair, FEATS:, :] = hub_block
        out_ref[2 * pair + 1, FEATS:, :] = hub_block


def gather_slots(feats, send_lanes, hub_own):
    return pl.pallas_call(
        gather_kernel,
        in_specs=[HBM, HBM, HBM],
        out_shape=jax.ShapeDtypeStruct((PEERS, ROWS, SLOTS), BF16),
        scratch_shapes=[
            pltpu.VMEM((FEATS, NODES), BF16),
            pltpu.VMEM((PEERS, SLOTS), jnp.int32),
            pltpu.VMEM((1, HUBS_OWN), jnp.int32),
            pltpu.SemaphoreType.DMA((3,)),
        ],
        compiler_params=params(60),
        cost_estimate=cost(2 * 256 * 4096 * 1024, 1 << 20),
        name="gather_slots",
    )(feats, send_lanes, hub_own)


BUILD = 256
KEPT = 512


def counts_of(nbr_ref, rows):
    first = lax.broadcasted_iota(jnp.int32, (rows, nbr_ref.shape[1]), 0)
    counts = jnp.zeros(first.shape, F32)
    for k in range(nbr_ref.shape[0]):
        counts = counts + jnp.where(first == nbr_ref[k : k + 1, :], 1.0, 0.0)
    return counts.astype(BF16)


def build_kernel(x_ref, loc_ref, hub_ref, local_ref, hubs_ref, sum_ref):
    counts = counts_of(loc_ref, NODES)
    local_ref[...] = counts
    hubs_ref[...] = counts_of(hub_ref, HUBS)
    sum_ref[...] = matmul(x_ref[...], counts, NN)


def build_counts(feats, loc_lanes, hub_lanes):
    return pl.pallas_call(
        build_kernel,
        grid=(NODES // BUILD,),
        in_specs=[
            whole((FEATS, NODES)),
            pl.BlockSpec((loc_lanes.shape[0], BUILD), lambda i: (0, i)),
            pl.BlockSpec((hub_lanes.shape[0], BUILD), lambda i: (0, i)),
        ],
        out_specs=[
            pl.BlockSpec((NODES, BUILD), lambda i: (0, i)),
            pl.BlockSpec((HUBS, BUILD), lambda i: (0, i)),
            pl.BlockSpec((FEATS, BUILD), lambda i: (0, i)),
        ],
        out_shape=[
            jax.ShapeDtypeStruct((NODES, NODES), BF16),
            jax.ShapeDtypeStruct((HUBS, NODES), BF16),
            jax.ShapeDtypeStruct((KEPT, NODES), F32),
        ],
        compiler_params=params(60),
        cost_estimate=cost(1 << 30, 4 << 20),
        name="build_counts",
    )(feats, loc_lanes, hub_lanes)


AGG = 256


def fold_halves(block):
    return jnp.concatenate([block[: OWN // 2, :], block[OWN // 2 :, :]], axis=1)


NEIGHBOURS = 10.0


def aggregate_kernel(
    x_hbm, inc_ref, recv_hbm, sum_hbm, hub_hbm, cot_hbm, out_ref, degree_ref,
    slots, table, recv_ref, hub_ref, x_ref, cot_ref, sum_ref, sems,
):
    staged = copies(
        sems,
        (recv_hbm, recv_ref),
        (hub_hbm, hub_ref),
        (x_hbm, x_ref),
        (cot_hbm, cot_ref),
        (sum_hbm.at[:FEATS], sum_ref),
    )
    for peer in range(PEERS):
        slots[:FEATS, SLOTS * peer : SLOTS * (peer + 1)] = inc_ref[peer, :FEATS, :]
    slots[FEATS:, :] = jnp.ones((16, PEERS * SLOTS), BF16)
    rows = inc_ref[:, FEATS:, :].astype(F32).reshape(HUBS, SLOTS)
    table[...] = rows.T[:FEATS, :].astype(BF16)
    staged[0].wait()
    for tile in range(NODES // AGG):
        lanes = slice(AGG * tile, AGG * (tile + 1))
        node = lax.broadcasted_iota(jnp.int32, (AGG, 2 * SLOTS), 0) + AGG * tile
        remote = jnp.zeros((ROWS, AGG), F32)
        for pair in range(PEERS // 2):
            remote = remote + matmul(
                slots[:, 2 * SLOTS * pair : 2 * SLOTS * (pair + 1)],
                one_hot(node == pair_lanes(recv_ref, pair)),
                NT,
            )
        if tile == 0:
            for copy in staged[1:]:
                copy.wait()
        hubs = counts_of(hub_ref[:, lanes], HUBS)
        total = remote[:FEATS, :] + sum_ref[:, lanes] + matmul(table[...], hubs, NN)
        degree = remote[FEATS : FEATS + 8, :] + NEIGHBOURS
        degree_ref[:, lanes] = degree
        mean = (total / degree[0:1, :]).T
        nodes = jnp.concatenate([x_ref[:, lanes].astype(F32).T, mean], axis=1).astype(BF16)
        slopes = cot_ref[:, lanes].astype(F32).T
        for part in range(AGG // OWN):
            layer = AGG // OWN * tile + part
            out_ref[layer, :OWN, :] = nodes[OWN * part : OWN * (part + 1), :]
            out_ref[layer, OWN:, :] = fold_halves(slopes[OWN * part : OWN * (part + 1), :]).astype(BF16)


def aggregate(feats, incoming, recv_lanes, local_sum, hub_lanes, cotangent):
    return pl.pallas_call(
        aggregate_kernel,
        out_shape=[
            jax.ShapeDtypeStruct((LAYERS, 96, SLOTS), BF16),
            jax.ShapeDtypeStruct((8, NODES), F32),
        ],
        in_specs=[HBM, VMEM, HBM, HBM, HBM, HBM],
        scratch_shapes=[
            pltpu.VMEM((ROWS, PEERS * SLOTS), BF16),
            pltpu.VMEM((FEATS, HUBS), BF16),
            pltpu.VMEM((PEERS, SLOTS), jnp.int32),
            pltpu.VMEM((2, NODES), jnp.int32),
            pltpu.VMEM((FEATS, NODES), BF16),
            pltpu.VMEM((FEATS, NODES), BF16),
            pltpu.VMEM((FEATS, NODES), F32),
            pltpu.SemaphoreType.DMA((5,)),
        ],
        compiler_params=params(52),
        cost_estimate=cost(2 * 256 * 5632 * 1024, 3 << 20),
        name="aggregate",
    )(feats, incoming, recv_lanes, local_sum, hub_lanes, cotangent)


PIECE = 32
TILE = 256
CHIPS = PEERS // 2
SLICE = LAYERS * PIECE


def regroup_kernel(inc_ref, out_ref):
    group = lax.broadcasted_iota(jnp.int32, (OWN, SLOTS), 1) // PIECE
    for part in range(4):
        blocks = [inc_ref[4 * part + i, :OWN, :].astype(F32) for i in range(4)]
        for slice_of in range(4):
            tile = jnp.zeros((OWN, SLOTS), F32)
            for i in range(4):
                moved = blocks[i]
                if i != slice_of:
                    moved = pltpu.roll(moved, (PIECE * (i - slice_of)) % SLOTS, 1)
                tile = jnp.where(group == i, moved, tile)
            tile = tile.astype(BF16)
            for outs in range(4):
                out_ref[4 * slice_of + outs, :, SLOTS * part : SLOTS * (part + 1)] = tile


def regroup(node_block):
    return pl.pallas_call(
        regroup_kernel,
        out_shape=jax.ShapeDtypeStruct((CHIPS, OWN, SLICE), BF16),
        compiler_params=params(16),
        cost_estimate=cost(1 << 24, 2 << 20),
        name="regroup",
    )(node_block)


HALF = OUTS // 2
STEPS = 4


def prepare_kernel(own_block, other_block, joined_ref, cot_ref):
    core = lax.axis_index("row") % 2
    for layer in range(LAYERS):
        lanes = slice(SLOTS * layer, SLOTS * (layer + 1))
        joined_ref[0, :, lanes] = own_block[layer, :OWN, :]
        joined_ref[1, :, lanes] = other_block[layer, :OWN, :]
    for side, block in enumerate((own_block, other_block)):
        for pair in range(LAYERS // 4):
            even = block[8 * core + 2 * pair, OWN:, :].astype(F32)
            odd = block[8 * core + 2 * pair + 1, OWN:, :].astype(F32)
            top = jnp.concatenate([even[:, :FEATS], odd[:, :FEATS]], axis=1)
            bottom = jnp.concatenate([even[:, FEATS:], odd[:, FEATS:]], axis=1)
            cot_ref[side, :, SLOTS * pair : SLOTS * (pair + 1)] = jnp.concatenate(
                [top, bottom], axis=0
            ).astype(BF16)


def prepare(own_block, other_block):
    return pl.pallas_call(
        prepare_kernel,
        out_shape=[
            jax.ShapeDtypeStruct((2, OWN, 2 * OUTS), BF16),
            jax.ShapeDtypeStruct((2, OWN, HALF), BF16),
        ],
        compiler_params=params(16),
        cost_estimate=cost(1 << 20, 2 << 20),
        name="prepare",
    )(own_block, other_block)


def forward_kernel(
    joined_hbm, cot_hbm, weights_hbm, slopes_hbm, flat_hbm, hidden_hbm,
    joined, cots, weights, out_tile, flat, hidden, in_sems, out_sems,
):
    depth = 2 * OUTS // STEPS
    bands = [slice(depth * step, depth * (step + 1)) for step in range(STEPS)]
    staged = copies(
        in_sems,
        (joined_hbm, joined),
        *[(weights_hbm.at[band, :], weights.at[band, :]) for band in bands],
        (cot_hbm, cots),
    )
    staged[0].wait()
    preact = jnp.zeros((2 * OWN, HALF), F32)
    for step, band in enumerate(bands):
        staged[step + 1].wait()
        rows = joined[:, :, band].reshape(2 * OWN, depth)
        preact = preact + matmul(rows, weights[band, :], NN)
    staged[STEPS + 1].wait()
    sigmoid_part = jax.nn.sigmoid(preact)
    silu = preact * sigmoid_part
    slope = sigmoid_part * (1.0 + preact * (1.0 - sigmoid_part))
    slopes = (cots[...].reshape(2 * OWN, HALF).astype(F32) * slope).astype(BF16)
    for outs in range(4):
        out_tile[outs] = slopes[:, SLOTS * outs : SLOTS * (outs + 1)]
    sent = []
    for chip in range(CHIPS):
        copy = pltpu.make_async_copy(out_tile.at[chip % 4], slopes_hbm.at[chip], out_sems.at[chip])
        copy.start()
        sent.append(copy)
    flat[...] = slopes
    for block in range(2):
        for layer in range(LAYERS // 2):
            tile = silu[OWN * block : OWN * (block + 1), FEATS * layer : FEATS * (layer + 1)]
            hidden[block, layer] = fold_halves(tile).astype(BF16)
    for i, (source, target) in enumerate(((flat, flat_hbm), (hidden, hidden_hbm))):
        copy = pltpu.make_async_copy(source, target, out_sems.at[CHIPS + i])
        copy.start()
        sent.append(copy)
    for copy in sent:
        copy.wait()


def forward(joined, cots, weights):
    return pl.pallas_call(
        forward_kernel,
        in_specs=[HBM, HBM, HBM],
        out_specs=[HBM, HBM, HBM],
        out_shape=[
            jax.ShapeDtypeStruct((CHIPS, 2 * OWN, SLOTS), BF16),
            jax.ShapeDtypeStruct((2 * OWN, HALF), BF16),
            jax.ShapeDtypeStruct((2, LAYERS // 2, OWN // 2, SLOTS), BF16),
        ],
        scratch_shapes=[
            pltpu.VMEM((2, OWN, 2 * OUTS), BF16),
            pltpu.VMEM((2, OWN, HALF), BF16),
            pltpu.VMEM((2 * OUTS, HALF), BF16),
            pltpu.VMEM((4, 2 * OWN, SLOTS), BF16),
            pltpu.VMEM((2 * OWN, HALF), BF16),
            pltpu.VMEM((2, LAYERS // 2, OWN // 2, SLOTS), BF16),
            pltpu.SemaphoreType.DMA((STEPS + 2,)),
            pltpu.SemaphoreType.DMA((CHIPS + 2,)),
        ],
        compiler_params=params(60),
        cost_estimate=cost(2 * 256 * 2048 * 512, 4 << 20),
        name="forward",
    )(joined, cots, weights)


SWAP = LAYERS + 4


def backward_kernel(slopes_ref, hidden_ref, weights_ref, keep_ref, send_ref):
    back = matmul(slopes_ref[...], weights_ref[...], NT)
    keep_ref[...] = back[:OWN, :]
    for layer in range(LAYERS):
        send_ref[layer] = back[OWN:, SLOTS * layer : SLOTS * (layer + 1)].astype(BF16)
    for pair in range(LAYERS // 4):
        send_ref[LAYERS + pair] = hidden_ref[1, 2 * pair : 2 * pair + 2].reshape(OWN, SLOTS)


def backward(slopes, hidden, weights):
    return pl.pallas_call(
        backward_kernel,
        out_shape=[
            jax.ShapeDtypeStruct((OWN, 2 * OUTS), F32),
            jax.ShapeDtypeStruct((SWAP, OWN, SLOTS), BF16),
        ],
        compiler_params=params(16),
        cost_estimate=cost(2 * 256 * 2048 * 512, 4 << 20),
        name="backward",
    )(slopes, hidden, weights)


def weight_kernel(
    mine_hbm, theirs_hbm, slopes_ref, keep_hbm, swapped_hbm, hidden_hbm, degree_hbm, out_ref,
    mine, theirs, keep, swapped, hidden, degree, sems,
):
    core = lax.axis_index("row") % 2
    staged = copies(
        sems,
        (degree_hbm, degree),
        (keep_hbm, keep),
        (swapped_hbm, swapped),
        (hidden_hbm.at[0], hidden),
        (mine_hbm, mine),
        (theirs_hbm, theirs),
    )
    slopes = [
        slopes_ref[:, OWN * side : OWN * (side + 1), :].astype(F32).reshape(CHIPS * OWN, SLOTS)
        for side in range(2)
    ]
    columns = [rows.T.astype(BF16) for rows in slopes]
    for copy in staged[:4]:
        copy.wait()
    direct = lax.broadcasted_iota(jnp.int32, (OWN, SLOTS), 1) < FEATS
    divisor = jnp.where(direct, 1.0, degree[...])
    for layer in range(LAYERS):
        back = keep[:, SLOTS * layer : SLOTS * (layer + 1)] + swapped[layer].astype(F32)
        out_ref[layer, :OWN, :] = (back / divisor).astype(BF16)
    for pair in range(LAYERS // 4):
        for side in range(2):
            layer = 2 * pair + side
            out_ref[8 * core + layer, OWN:96, :] = hidden[layer]
            out_ref[8 * (1 - core) + layer, OWN:96, :] = swapped[
                LAYERS + pair, OWN // 2 * side : OWN // 2 * (side + 1), :
            ]
    part = jnp.zeros((SLOTS, SLICE), F32)
    for side, rows in enumerate((mine, theirs)):
        staged[4 + side].wait()
        part = part + matmul(columns[side], rows[...].reshape(CHIPS * OWN, SLICE), NN)
    part = part.T.astype(BF16)
    for layer in range(LAYERS):
        out_ref[layer, 96:, :] = part[PIECE * layer : PIECE * (layer + 1), :]


def weight_parts(mine, theirs, slopes_rows, keep, swapped, hidden, own_degree):
    return pl.pallas_call(
        weight_kernel,
        in_specs=[HBM, HBM, VMEM, HBM, HBM, HBM, HBM],
        out_shape=jax.ShapeDtypeStruct((LAYERS, SLOTS, SLOTS), BF16),
        scratch_shapes=[
            pltpu.VMEM((CHIPS, OWN, SLICE), BF16),
            pltpu.VMEM((CHIPS, OWN, SLICE), BF16),
            pltpu.VMEM((OWN, 2 * OUTS), F32),
            pltpu.VMEM((SWAP, OWN, SLOTS), BF16),
            pltpu.VMEM((LAYERS // 2, OWN // 2, SLOTS), BF16),
            pltpu.VMEM((OWN, 1), F32),
            pltpu.SemaphoreType.DMA((6,)),
        ],
        compiler_params=params(52),
        cost_estimate=cost(2 * 256 * 2048 * 256, 4 << 20),
        name="weight_parts",
    )(mine, theirs, slopes_rows, keep, swapped, hidden, own_degree)


RETURN_ROWS = 112


def return_kernel(
    back_hbm, recv_hbm, hubs_hbm, out_hbm,
    back_ref, part_ref, recv_ref, hubs_ref, out_ref, in_sems, out_sems,
):
    staged = copies(
        in_sems,
        (recv_hbm, recv_ref),
        (hubs_hbm, hubs_ref),
        (back_hbm.at[:, :OWN, :], back_ref),
        (back_hbm.at[:, 96:, :], part_ref),
    )
    node = lax.broadcasted_iota(jnp.int32, (NODES, 2 * SLOTS), 0)
    staged[2].wait()
    share = back_ref[...].astype(F32).reshape(NODES, SLOTS).T[FEATS:, :].astype(BF16)
    staged[0].wait()
    staged[3].wait()
    sums = jnp.sum(part_ref[...].astype(F32), axis=0).astype(BF16)
    sent = []
    for pair in range(PEERS // 2):
        values = matmul(share, one_hot(node == pair_lanes(recv_ref, pair)), NN).astype(BF16)
        for side in range(2):
            peer = 2 * pair + side
            out_ref[peer, :FEATS, :] = values[:, SLOTS * side : SLOTS * (side + 1)]
            out_ref[peer, ROWS:, :] = sums
        if pair == 3:
            staged[1].wait()
            terms = matmul(share, hubs_ref[...], NT).T
            high = terms.astype(BF16).astype(F32)
            both = jnp.concatenate([high, terms - high], axis=1)
            out_ref[:, FEATS:ROWS, :] = both.reshape(PEERS, HUBS_OWN, SLOTS).astype(BF16)
        if pair % 4 == 3:
            part = pl.ds(2 * pair - 6, 8)
            copy = pltpu.make_async_copy(out_ref.at[part], out_hbm.at[part], out_sems.at[pair // 4])
            copy.start()
            sent.append(copy)
    for copy in sent:
        copy.wait()


def return_slots(back_block, recv_lanes, hubs):
    return pl.pallas_call(
        return_kernel,
        in_specs=[HBM, HBM, HBM],
        out_specs=HBM,
        out_shape=jax.ShapeDtypeStruct((PEERS, RETURN_ROWS, SLOTS), BF16),
        scratch_shapes=[
            pltpu.VMEM((LAYERS, OWN, SLOTS), BF16),
            pltpu.VMEM((LAYERS, 32, SLOTS), BF16),
            pltpu.VMEM((PEERS, SLOTS), jnp.int32),
            pltpu.VMEM((HUBS, NODES), BF16),
            pltpu.VMEM((PEERS, RETURN_ROWS, SLOTS), BF16),
            pltpu.SemaphoreType.DMA((4,)),
            pltpu.SemaphoreType.DMA((4,)),
        ],
        compiler_params=params(60),
        cost_estimate=cost(2 * 256 * 4608 * 1024, 3 << 20),
        name="return_slots",
    )(back_block, recv_lanes, hubs)


def local_kernel(back_ref, local_ref, base_hbm, hidden_ref, base_ref, sems):
    columns = back_ref[:, :OWN, :].astype(F32).reshape(NODES, SLOTS).T
    share = columns[FEATS:, :].astype(BF16)
    base_ref[...] = columns[:FEATS, :] + matmul(share, local_ref[...], NT)
    (sent,) = copies(sems, (base_ref, base_hbm.at[:FEATS]))
    folded = back_ref[:, OWN:96, :].astype(F32)
    rows = jnp.concatenate([folded[:, :, :FEATS], folded[:, :, FEATS:]], axis=1)
    hidden_ref[...] = rows.reshape(NODES, FEATS).T.astype(BF16)
    sent.wait()


def local_grads(back_block, local):
    return pl.pallas_call(
        local_kernel,
        out_specs=[HBM, VMEM],
        out_shape=[
            jax.ShapeDtypeStruct((KEPT, NODES), F32),
            jax.ShapeDtypeStruct((FEATS, NODES), BF16),
        ],
        scratch_shapes=[pltpu.VMEM((FEATS, NODES), F32), pltpu.SemaphoreType.DMA((1,))],
        compiler_params=params(60),
        cost_estimate=cost(2 * 256 * 1024 * 1024, 3 << 20),
        name="local_grads",
    )(back_block, local)


SPREAD = 256


def spread_kernel(
    back_ref, send_hbm, hub_hbm, base_hbm, out_ref, self_hbm, neigh_hbm,
    send_ref, hub_ref, base_ref, grads_ref, slots, in_sems, out_sems,
):
    staged = copies(in_sems, (send_hbm, send_ref), (hub_hbm, hub_ref), (base_hbm.at[:FEATS], base_ref))
    for peer in range(PEERS):
        slots[:, SLOTS * peer : SLOTS * (peer + 1)] = back_ref[peer, :FEATS, :]
        grads = back_ref[peer, ROWS:, :].astype(F32)
        slice_of, start = peer // 8, HALF * (peer % 2) + SLOTS * (peer // 2 % 4)
        grads_ref[PIECE * slice_of : PIECE * (slice_of + 1), start : start + SLOTS] = grads
    sent = copies(
        out_sems, (grads_ref.at[:FEATS], self_hbm), (grads_ref.at[FEATS:], neigh_hbm)
    )
    sums = jnp.sum(back_ref[:, FEATS:ROWS, :].astype(F32), axis=0)
    total = sums[:, :FEATS] + sums[:, FEATS:]
    high = total.astype(BF16).astype(F32)
    hub_high = high.T.astype(BF16)
    hub_low = (total - high).T.astype(BF16)
    staged[0].wait()
    staged[1].wait()
    for tile in range(NODES // SPREAD):
        lanes = slice(SPREAD * tile, SPREAD * (tile + 1))
        node = lax.broadcasted_iota(jnp.int32, (SPREAD, 2 * SLOTS), 0) + SPREAD * tile
        grad = jnp.zeros((FEATS, SPREAD), F32)
        for pair in range(PEERS // 2):
            grad = grad + matmul(
                slots[:, 2 * SLOTS * pair : 2 * SLOTS * (pair + 1)],
                one_hot(node == pair_lanes(send_ref, pair)),
                NT,
            )
        hub_node = lax.broadcasted_iota(jnp.int32, (SPREAD, HUBS_OWN), 0) + SPREAD * tile
        hub_hot = one_hot(hub_node == hub_ref[...])
        grad = grad + matmul(hub_high, hub_hot, NT) + matmul(hub_low, hub_hot, NT)
        if tile == 0:
            staged[2].wait()
        out_ref[:, lanes] = (grad + base_ref[:, lanes]).astype(BF16)
    for copy in sent:
        copy.wait()


def spread_grads(returned, send_lanes, hub_own, base):
    return pl.pallas_call(
        spread_kernel,
        in_specs=[VMEM, HBM, HBM, HBM],
        out_specs=[VMEM, HBM, HBM],
        out_shape=[
            jax.ShapeDtypeStruct((FEATS, NODES), BF16),
            jax.ShapeDtypeStruct((FEATS, OUTS), F32),
            jax.ShapeDtypeStruct((FEATS, OUTS), F32),
        ],
        scratch_shapes=[
            pltpu.VMEM((PEERS, SLOTS), jnp.int32),
            pltpu.VMEM((1, HUBS_OWN), jnp.int32),
            pltpu.VMEM((FEATS, NODES), F32),
            pltpu.VMEM((2 * FEATS, OUTS), F32),
            pltpu.VMEM((FEATS, PEERS * SLOTS), BF16),
            pltpu.SemaphoreType.DMA((3,)),
            pltpu.SemaphoreType.DMA((2,)),
        ],
        compiler_params=params(52),
        cost_estimate=cost(2 * 256 * 4224 * 1024, 2 << 20),
        name="spread_grads",
    )(returned, send_lanes, hub_own, base)


SAME_CORE = [list(range(core, PEERS, 2)) for core in range(2)]


def exchange(blocks, axis, groups=None):
    return lax.all_to_all(blocks, axis, 0, 0, axis_index_groups=groups, tiled=True)


def other_core(block):
    return lax.ppermute(block, "row", [(i, i ^ 1) for i in range(PEERS)])


def per_device(feats, w_self, w_neigh, cotangent, loc_nbr, send_rows, recv_node, hub_rows, hub_nbr):
    send_lanes = send_rows.reshape(PEERS, SLOTS)
    recv_lanes = recv_node.reshape(PEERS, SLOTS)
    hub_own = hub_rows[None, :]
    half = HALF * (lax.axis_index("row") % 2)
    weights = lax.all_gather(
        lax.dynamic_slice_in_dim(jnp.concatenate([w_self, w_neigh], axis=0), half, HALF, 1),
        "col",
        axis=0,
        tiled=True,
    )
    incoming = exchange(gather_slots(feats, send_lanes, hub_own), "row")
    hub_lanes = hub_nbr.T
    local, hubs, local_sum = build_counts(feats, loc_nbr.T, hub_lanes)
    outgoing, degree = aggregate(feats, incoming, recv_lanes, local_sum, hub_lanes, cotangent)
    node_block = exchange(outgoing, "col")
    own_degree = lax.dynamic_slice_in_dim(degree[0], OWN * lax.axis_index("col"), OWN)[:, None]
    joined_mine = exchange(regroup(node_block), "row", SAME_CORE)
    joined, cots = prepare(node_block, other_core(node_block))
    slopes_out, slopes, hidden = forward(joined, cots, weights)
    slopes_rows = exchange(slopes_out, "row", SAME_CORE)
    joined_mine, slopes = lax.optimization_barrier((joined_mine, slopes))
    joined_theirs = other_core(joined_mine)
    keep, sent = backward(slopes, hidden, weights)
    parts = weight_parts(
        joined_mine, joined_theirs, slopes_rows, keep, other_core(sent), hidden, own_degree
    )
    back_block = exchange(parts, "col")
    returned = exchange(return_slots(back_block, recv_lanes, hubs), "row")
    base, hidden_out = local_grads(back_block, local)
    grad_feats, grad_self, grad_neigh = spread_grads(returned, send_lanes, hub_own, base)
    return (hidden_out, grad_feats, grad_self, grad_neigh)


def solution(mesh):
    return jax.shard_map(
        per_device,
        mesh=mesh,
        in_specs=(
            P("col", "row"),
            P("col", None),
            P("col", None),
            P("col", "row"),
            P("row", None),
            P("row", None, None),
            P("row", None, None),
            P("row"),
            P("row", None),
        ),
        out_specs=(P("col", "row"), P("col", "row"), P("col", None), P("col", None)),
        check_vma=False,
    )
```

```python
import jax
import jax.numpy as jnp
from jax import lax
from jax.experimental import pallas as pl
from jax.experimental.pallas import tpu as pltpu
from jax.sharding import PartitionSpec as P

NODES = 1024
FEATS = 64
PEERS = 32
SLOTS = 128
HUBS_OWN = 16
HUBS = 512
ROWS = 80
LAYERS = 16
OWN = 64
OUTS = 1024
BF16 = jnp.bfloat16
F32 = jnp.float32
NT = (((1,), (1,)), ((), ()))
NN = (((1,), (0,)), ((), ()))
MIB = 1 << 20


def params(mib):
    return pltpu.CompilerParams(vmem_limit_bytes=mib * MIB)


def cost(flops, moved):
    return pl.CostEstimate(flops=flops, bytes_accessed=moved, transcendentals=0)


def whole(shape):
    return pl.BlockSpec(shape, lambda *_: (0,) * len(shape))


HBM = pl.BlockSpec(memory_space=pltpu.HBM)
VMEM = pl.BlockSpec(memory_space=pltpu.VMEM)


def copies(sems, *pairs):
    started = []
    for i, (source, target) in enumerate(pairs):
        copy = pltpu.make_async_copy(source, target, sems.at[i])
        copy.start()
        started.append(copy)
    return started


def one_hot(mask):
    return jnp.where(mask, 1.0, 0.0).astype(BF16)


def matmul(a, b, dims):
    return lax.dot_general(a, b, dims, preferred_element_type=F32)


def pair_lanes(ref, pair):
    return jnp.concatenate([ref[2 * pair : 2 * pair + 1, :], ref[2 * pair + 1 : 2 * pair + 2, :]], axis=1)


def gather_kernel(x_hbm, send_hbm, hub_hbm, out_ref, x_ref, send_ref, hub_ref, sems):
    for copy in copies(sems, (x_hbm, x_ref), (send_hbm, send_ref), (hub_hbm, hub_ref)):
        copy.wait()
    x = x_ref[...]
    node = lax.broadcasted_iota(jnp.int32, (NODES, 2 * SLOTS), 0)
    hub_node = lax.broadcasted_iota(jnp.int32, (NODES, HUBS_OWN), 0)
    hub_feats = matmul(x, one_hot(hub_node == hub_ref[...]), NN)
    hub_rows = hub_feats.T
    hub_block = jnp.concatenate([hub_rows, jnp.zeros_like(hub_rows)], axis=1).astype(BF16)
    for pair in range(PEERS // 2):
        picked = matmul(x, one_hot(node == pair_lanes(send_ref, pair)), NN).astype(BF16)
        out_ref[2 * pair, :FEATS, :] = picked[:, :SLOTS]
        out_ref[2 * pair + 1, :FEATS, :] = picked[:, SLOTS:]
        out_ref[2 * pair, FEATS:, :] = hub_block
        out_ref[2 * pair + 1, FEATS:, :] = hub_block


def gather_slots(feats, send_lanes, hub_own):
    return pl.pallas_call(
        gather_kernel,
        in_specs=[HBM, HBM, HBM],
        out_shape=jax.ShapeDtypeStruct((PEERS, ROWS, SLOTS), BF16),
        scratch_shapes=[
            pltpu.VMEM((FEATS, NODES), BF16),
            pltpu.VMEM((PEERS, SLOTS), jnp.int32),
            pltpu.VMEM((1, HUBS_OWN), jnp.int32),
            pltpu.SemaphoreType.DMA((3,)),
        ],
        compiler_params=params(60),
        cost_estimate=cost(2 * 256 * 4096 * 1024, 1 << 20),
        name="gather_slots",
    )(feats, send_lanes, hub_own)


BUILD = 256
KEPT = 512


def counts_of(nbr_ref, rows):
    first = lax.broadcasted_iota(jnp.int32, (rows, nbr_ref.shape[1]), 0)
    counts = jnp.zeros(first.shape, F32)
    for k in range(nbr_ref.shape[0]):
        counts = counts + jnp.where(first == nbr_ref[k : k + 1, :], 1.0, 0.0)
    return counts.astype(BF16)


def build_kernel(x_ref, loc_ref, hub_ref, local_ref, hubs_ref, sum_ref):
    counts = counts_of(loc_ref, NODES)
    local_ref[...] = counts
    hubs_ref[...] = counts_of(hub_ref, HUBS)
    sum_ref[...] = matmul(x_ref[...], counts, NN)


def build_counts(feats, loc_lanes, hub_lanes):
    return pl.pallas_call(
        build_kernel,
        grid=(NODES // BUILD,),
        in_specs=[
            whole((FEATS, NODES)),
            pl.BlockSpec((loc_lanes.shape[0], BUILD), lambda i: (0, i)),
            pl.BlockSpec((hub_lanes.shape[0], BUILD), lambda i: (0, i)),
        ],
        out_specs=[
            pl.BlockSpec((NODES, BUILD), lambda i: (0, i)),
            pl.BlockSpec((HUBS, BUILD), lambda i: (0, i)),
            pl.BlockSpec((FEATS, BUILD), lambda i: (0, i)),
        ],
        out_shape=[
            jax.ShapeDtypeStruct((NODES, NODES), BF16),
            jax.ShapeDtypeStruct((HUBS, NODES), BF16),
            jax.ShapeDtypeStruct((KEPT, NODES), F32),
        ],
        compiler_params=params(60),
        cost_estimate=cost(1 << 30, 4 << 20),
        name="build_counts",
    )(feats, loc_lanes, hub_lanes)


AGG = 256


def fold_halves(block):
    return jnp.concatenate([block[: OWN // 2, :], block[OWN // 2 :, :]], axis=1)


NEIGHBOURS = 10.0


def aggregate_kernel(
    x_hbm, inc_ref, recv_hbm, sum_hbm, hub_hbm, cot_hbm, out_ref, degree_ref,
    slots, table, recv_ref, hub_ref, x_ref, cot_ref, sum_ref, sems,
):
    staged = copies(
        sems,
        (recv_hbm, recv_ref),
        (hub_hbm, hub_ref),
        (x_hbm, x_ref),
        (cot_hbm, cot_ref),
        (sum_hbm.at[:FEATS], sum_ref),
    )
    for peer in range(PEERS):
        slots[:FEATS, SLOTS * peer : SLOTS * (peer + 1)] = inc_ref[peer, :FEATS, :]
    slots[FEATS:, :] = jnp.ones((16, PEERS * SLOTS), BF16)
    rows = inc_ref[:, FEATS:, :].astype(F32).reshape(HUBS, SLOTS)
    table[...] = rows.T[:FEATS, :].astype(BF16)
    staged[0].wait()
    for tile in range(NODES // AGG):
        lanes = slice(AGG * tile, AGG * (tile + 1))
        node = lax.broadcasted_iota(jnp.int32, (AGG, 2 * SLOTS), 0) + AGG * tile
        remote = jnp.zeros((ROWS, AGG), F32)
        for pair in range(PEERS // 2):
            remote = remote + matmul(
                slots[:, 2 * SLOTS * pair : 2 * SLOTS * (pair + 1)],
                one_hot(node == pair_lanes(recv_ref, pair)),
                NT,
            )
        if tile == 0:
            for copy in staged[1:]:
                copy.wait()
        hubs = counts_of(hub_ref[:, lanes], HUBS)
        total = remote[:FEATS, :] + sum_ref[:, lanes] + matmul(table[...], hubs, NN)
        degree = remote[FEATS : FEATS + 8, :] + NEIGHBOURS
        degree_ref[:, lanes] = degree
        mean = (total / degree[0:1, :]).T
        nodes = jnp.concatenate([x_ref[:, lanes].astype(F32).T, mean], axis=1).astype(BF16)
        slopes = cot_ref[:, lanes].astype(F32).T
        for part in range(AGG // OWN):
            layer = AGG // OWN * tile + part
            out_ref[layer, :OWN, :] = nodes[OWN * part : OWN * (part + 1), :]
            out_ref[layer, OWN:, :] = fold_halves(slopes[OWN * part : OWN * (part + 1), :]).astype(BF16)


def aggregate(feats, incoming, recv_lanes, local_sum, hub_lanes, cotangent):
    return pl.pallas_call(
        aggregate_kernel,
        out_shape=[
            jax.ShapeDtypeStruct((LAYERS, 96, SLOTS), BF16),
            jax.ShapeDtypeStruct((8, NODES), F32),
        ],
        in_specs=[HBM, VMEM, HBM, HBM, HBM, HBM],
        scratch_shapes=[
            pltpu.VMEM((ROWS, PEERS * SLOTS), BF16),
            pltpu.VMEM((FEATS, HUBS), BF16),
            pltpu.VMEM((PEERS, SLOTS), jnp.int32),
            pltpu.VMEM((2, NODES), jnp.int32),
            pltpu.VMEM((FEATS, NODES), BF16),
            pltpu.VMEM((FEATS, NODES), BF16),
            pltpu.VMEM((FEATS, NODES), F32),
            pltpu.SemaphoreType.DMA((5,)),
        ],
        compiler_params=params(52),
        cost_estimate=cost(2 * 256 * 5632 * 1024, 3 << 20),
        name="aggregate",
    )(feats, incoming, recv_lanes, local_sum, hub_lanes, cotangent)


PIECE = 32
TILE = 256
CHIPS = PEERS // 2
SLICE = LAYERS * PIECE


def regroup_kernel(inc_ref, out_ref):
    group = lax.broadcasted_iota(jnp.int32, (OWN, SLOTS), 1) // PIECE
    for part in range(4):
        blocks = [inc_ref[4 * part + i, :OWN, :].astype(F32) for i in range(4)]
        for slice_of in range(4):
            tile = jnp.zeros((OWN, SLOTS), F32)
            for i in range(4):
                moved = blocks[i]
                if i != slice_of:
                    moved = pltpu.roll(moved, (PIECE * (i - slice_of)) % SLOTS, 1)
                tile = jnp.where(group == i, moved, tile)
            tile = tile.astype(BF16)
            for outs in range(4):
                out_ref[4 * slice_of + outs, :, SLOTS * part : SLOTS * (part + 1)] = tile


def regroup(node_block):
    return pl.pallas_call(
        regroup_kernel,
        out_shape=jax.ShapeDtypeStruct((CHIPS, OWN, SLICE), BF16),
        compiler_params=params(16),
        cost_estimate=cost(1 << 24, 2 << 20),
        name="regroup",
    )(node_block)


HALF = OUTS // 2
STEPS = 4


def prepare_kernel(own_block, other_block, joined_ref, cot_ref):
    core = lax.axis_index("row") % 2
    for layer in range(LAYERS):
        lanes = slice(SLOTS * layer, SLOTS * (layer + 1))
        joined_ref[0, :, lanes] = own_block[layer, :OWN, :]
        joined_ref[1, :, lanes] = other_block[layer, :OWN, :]
    for side, block in enumerate((own_block, other_block)):
        for pair in range(LAYERS // 4):
            even = block[8 * core + 2 * pair, OWN:, :].astype(F32)
            odd = block[8 * core + 2 * pair + 1, OWN:, :].astype(F32)
            top = jnp.concatenate([even[:, :FEATS], odd[:, :FEATS]], axis=1)
            bottom = jnp.concatenate([even[:, FEATS:], odd[:, FEATS:]], axis=1)
            cot_ref[side, :, SLOTS * pair : SLOTS * (pair + 1)] = jnp.concatenate(
                [top, bottom], axis=0
            ).astype(BF16)


def prepare(own_block, other_block):
    return pl.pallas_call(
        prepare_kernel,
        out_shape=[
            jax.ShapeDtypeStruct((2, OWN, 2 * OUTS), BF16),
            jax.ShapeDtypeStruct((2, OWN, HALF), BF16),
        ],
        compiler_params=params(16),
        cost_estimate=cost(1 << 20, 2 << 20),
        name="prepare",
    )(own_block, other_block)


def forward_kernel(
    joined_hbm, cot_hbm, weights_hbm, slopes_hbm, flat_hbm, hidden_hbm,
    joined, cots, weights, out_tile, flat, hidden, in_sems, out_sems,
):
    depth = 2 * OUTS // STEPS
    bands = [slice(depth * step, depth * (step + 1)) for step in range(STEPS)]
    staged = copies(
        in_sems,
        (joined_hbm, joined),
        *[(weights_hbm.at[band, :], weights.at[band, :]) for band in bands],
        (cot_hbm, cots),
    )
    staged[0].wait()
    preact = jnp.zeros((2 * OWN, HALF), F32)
    for step, band in enumerate(bands):
        staged[step + 1].wait()
        rows = joined[:, :, band].reshape(2 * OWN, depth)
        preact = preact + matmul(rows, weights[band, :], NN)
    staged[STEPS + 1].wait()
    sigmoid_part = jax.nn.sigmoid(preact)
    silu = preact * sigmoid_part
    slope = sigmoid_part * (1.0 + preact * (1.0 - sigmoid_part))
    slopes = (cots[...].reshape(2 * OWN, HALF).astype(F32) * slope).astype(BF16)
    for outs in range(4):
        out_tile[outs] = slopes[:, SLOTS * outs : SLOTS * (outs + 1)]
    sent = []
    for chip in range(CHIPS):
        copy = pltpu.make_async_copy(out_tile.at[chip % 4], slopes_hbm.at[chip], out_sems.at[chip])
        copy.start()
        sent.append(copy)
    flat[...] = slopes
    for block in range(2):
        for layer in range(LAYERS // 2):
            tile = silu[OWN * block : OWN * (block + 1), FEATS * layer : FEATS * (layer + 1)]
            hidden[block, layer] = fold_halves(tile).astype(BF16)
    for i, (source, target) in enumerate(((flat, flat_hbm), (hidden, hidden_hbm))):
        copy = pltpu.make_async_copy(source, target, out_sems.at[CHIPS + i])
        copy.start()
        sent.append(copy)
    for copy in sent:
        copy.wait()


def forward(joined, cots, weights):
    return pl.pallas_call(
        forward_kernel,
        in_specs=[HBM, HBM, HBM],
        out_specs=[HBM, HBM, HBM],
        out_shape=[
            jax.ShapeDtypeStruct((CHIPS, 2 * OWN, SLOTS), BF16),
            jax.ShapeDtypeStruct((2 * OWN, HALF), BF16),
            jax.ShapeDtypeStruct((2, LAYERS // 2, OWN // 2, SLOTS), BF16),
        ],
        scratch_shapes=[
            pltpu.VMEM((2, OWN, 2 * OUTS), BF16),
            pltpu.VMEM((2, OWN, HALF), BF16),
            pltpu.VMEM((2 * OUTS, HALF), BF16),
            pltpu.VMEM((4, 2 * OWN, SLOTS), BF16),
            pltpu.VMEM((2 * OWN, HALF), BF16),
            pltpu.VMEM((2, LAYERS // 2, OWN // 2, SLOTS), BF16),
            pltpu.SemaphoreType.DMA((STEPS + 2,)),
            pltpu.SemaphoreType.DMA((CHIPS + 2,)),
        ],
        compiler_params=params(60),
        cost_estimate=cost(2 * 256 * 2048 * 512, 4 << 20),
        name="forward",
    )(joined, cots, weights)


SWAP = LAYERS + 4


def backward_kernel(slopes_ref, hidden_ref, weights_ref, keep_ref, send_ref):
    back = matmul(slopes_ref[...], weights_ref[...], NT)
    keep_ref[...] = back[:OWN, :]
    for layer in range(LAYERS):
        send_ref[layer] = back[OWN:, SLOTS * layer : SLOTS * (layer + 1)].astype(BF16)
    for pair in range(LAYERS // 4):
        send_ref[LAYERS + pair] = hidden_ref[1, 2 * pair : 2 * pair + 2].reshape(OWN, SLOTS)


def backward(slopes, hidden, weights):
    return pl.pallas_call(
        backward_kernel,
        out_shape=[
            jax.ShapeDtypeStruct((OWN, 2 * OUTS), F32),
            jax.ShapeDtypeStruct((SWAP, OWN, SLOTS), BF16),
        ],
        compiler_params=params(16),
        cost_estimate=cost(2 * 256 * 2048 * 512, 4 << 20),
        name="backward",
    )(slopes, hidden, weights)


def weight_kernel(
    mine_hbm, theirs_hbm, slopes_ref, keep_hbm, swapped_hbm, hidden_hbm, degree_hbm, out_ref,
    mine, theirs, keep, swapped, hidden, degree, sems,
):
    core = lax.axis_index("row") % 2
    staged = copies(
        sems,
        (degree_hbm, degree),
        (keep_hbm, keep),
        (swapped_hbm, swapped),
        (hidden_hbm.at[0], hidden),
        (mine_hbm, mine),
        (theirs_hbm, theirs),
    )
    slopes = [
        slopes_ref[:, OWN * side : OWN * (side + 1), :].astype(F32).reshape(CHIPS * OWN, SLOTS)
        for side in range(2)
    ]
    columns = [rows.T.astype(BF16) for rows in slopes]
    for copy in staged[:4]:
        copy.wait()
    direct = lax.broadcasted_iota(jnp.int32, (OWN, SLOTS), 1) < FEATS
    divisor = jnp.where(direct, 1.0, degree[...])
    for layer in range(LAYERS):
        back = keep[:, SLOTS * layer : SLOTS * (layer + 1)] + swapped[layer].astype(F32)
        out_ref[layer, :OWN, :] = (back / divisor).astype(BF16)
    for pair in range(LAYERS // 4):
        for side in range(2):
            layer = 2 * pair + side
            out_ref[8 * core + layer, OWN:96, :] = hidden[layer]
            out_ref[8 * (1 - core) + layer, OWN:96, :] = swapped[
                LAYERS + pair, OWN // 2 * side : OWN // 2 * (side + 1), :
            ]
    part = jnp.zeros((SLOTS, SLICE), F32)
    for side, rows in enumerate((mine, theirs)):
        staged[4 + side].wait()
        part = part + matmul(columns[side], rows[...].reshape(CHIPS * OWN, SLICE), NN)
    part = part.T.astype(BF16)
    for layer in range(LAYERS):
        out_ref[layer, 96:, :] = part[PIECE * layer : PIECE * (layer + 1), :]


def weight_parts(mine, theirs, slopes_rows, keep, swapped, hidden, own_degree):
    return pl.pallas_call(
        weight_kernel,
        in_specs=[HBM, HBM, VMEM, HBM, HBM, HBM, HBM],
        out_shape=jax.ShapeDtypeStruct((LAYERS, SLOTS, SLOTS), BF16),
        scratch_shapes=[
            pltpu.VMEM((CHIPS, OWN, SLICE), BF16),
            pltpu.VMEM((CHIPS, OWN, SLICE), BF16),
            pltpu.VMEM((OWN, 2 * OUTS), F32),
            pltpu.VMEM((SWAP, OWN, SLOTS), BF16),
            pltpu.VMEM((LAYERS // 2, OWN // 2, SLOTS), BF16),
            pltpu.VMEM((OWN, 1), F32),
            pltpu.SemaphoreType.DMA((6,)),
        ],
        compiler_params=params(52),
        cost_estimate=cost(2 * 256 * 2048 * 256, 4 << 20),
        name="weight_parts",
    )(mine, theirs, slopes_rows, keep, swapped, hidden, own_degree)


RETURN_ROWS = 112


def return_kernel(
    back_hbm, recv_hbm, hubs_hbm, out_hbm,
    back_ref, part_ref, recv_ref, hubs_ref, out_ref, in_sems, out_sems,
):
    staged = copies(
        in_sems,
        (recv_hbm, recv_ref),
        (hubs_hbm, hubs_ref),
        (back_hbm.at[:, :OWN, :], back_ref),
        (back_hbm.at[:, 96:, :], part_ref),
    )
    node = lax.broadcasted_iota(jnp.int32, (NODES, 2 * SLOTS), 0)
    staged[2].wait()
    share = back_ref[...].astype(F32).reshape(NODES, SLOTS).T[FEATS:, :].astype(BF16)
    staged[0].wait()
    staged[3].wait()
    sums = jnp.sum(part_ref[...].astype(F32), axis=0).astype(BF16)
    sent = []
    for pair in range(PEERS // 2):
        values = matmul(share, one_hot(node == pair_lanes(recv_ref, pair)), NN).astype(BF16)
        for side in range(2):
            peer = 2 * pair + side
            out_ref[peer, :FEATS, :] = values[:, SLOTS * side : SLOTS * (side + 1)]
            out_ref[peer, ROWS:, :] = sums
        if pair == 3:
            staged[1].wait()
            terms = matmul(share, hubs_ref[...], NT).T
            high = terms.astype(BF16).astype(F32)
            both = jnp.concatenate([high, terms - high], axis=1)
            out_ref[:, FEATS:ROWS, :] = both.reshape(PEERS, HUBS_OWN, SLOTS).astype(BF16)
        if pair % 4 == 3:
            part = pl.ds(2 * pair - 6, 8)
            copy = pltpu.make_async_copy(out_ref.at[part], out_hbm.at[part], out_sems.at[pair // 4])
            copy.start()
            sent.append(copy)
    for copy in sent:
        copy.wait()


def return_slots(back_block, recv_lanes, hubs):
    return pl.pallas_call(
        return_kernel,
        in_specs=[HBM, HBM, HBM],
        out_specs=HBM,
        out_shape=jax.ShapeDtypeStruct((PEERS, RETURN_ROWS, SLOTS), BF16),
        scratch_shapes=[
            pltpu.VMEM((LAYERS, OWN, SLOTS), BF16),
            pltpu.VMEM((LAYERS, 32, SLOTS), BF16),
            pltpu.VMEM((PEERS, SLOTS), jnp.int32),
            pltpu.VMEM((HUBS, NODES), BF16),
            pltpu.VMEM((PEERS, RETURN_ROWS, SLOTS), BF16),
            pltpu.SemaphoreType.DMA((4,)),
            pltpu.SemaphoreType.DMA((4,)),
        ],
        compiler_params=params(53),
        cost_estimate=cost(2 * 256 * 4608 * 1024, 3 << 20),
        name="return_slots",
    )(back_block, recv_lanes, hubs)


def local_kernel(back_ref, local_ref, base_hbm, hidden_ref, base_ref, sems):
    columns = back_ref[:, :OWN, :].astype(F32).reshape(NODES, SLOTS).T
    share = columns[FEATS:, :].astype(BF16)
    base_ref[...] = columns[:FEATS, :] + matmul(share, local_ref[...], NT)
    (sent,) = copies(sems, (base_ref, base_hbm.at[:FEATS]))
    folded = back_ref[:, OWN:96, :].astype(F32)
    rows = jnp.concatenate([folded[:, :, :FEATS], folded[:, :, FEATS:]], axis=1)
    hidden_ref[...] = rows.reshape(NODES, FEATS).T.astype(BF16)
    sent.wait()


def local_grads(back_block, local):
    return pl.pallas_call(
        local_kernel,
        out_specs=[HBM, VMEM],
        out_shape=[
            jax.ShapeDtypeStruct((KEPT, NODES), F32),
            jax.ShapeDtypeStruct((FEATS, NODES), BF16),
        ],
        scratch_shapes=[pltpu.VMEM((FEATS, NODES), F32), pltpu.SemaphoreType.DMA((1,))],
        compiler_params=params(60),
        cost_estimate=cost(2 * 256 * 1024 * 1024, 3 << 20),
        name="local_grads",
    )(back_block, local)


SPREAD = 256


def spread_kernel(
    back_ref, send_hbm, hub_hbm, base_hbm, out_ref, self_hbm, neigh_hbm,
    send_ref, hub_ref, base_ref, grads_ref, slots, in_sems, out_sems,
):
    staged = copies(in_sems, (send_hbm, send_ref), (hub_hbm, hub_ref), (base_hbm.at[:FEATS], base_ref))
    for peer in range(PEERS):
        slots[:, SLOTS * peer : SLOTS * (peer + 1)] = back_ref[peer, :FEATS, :]
        grads = back_ref[peer, ROWS:, :].astype(F32)
        slice_of, start = peer // 8, HALF * (peer % 2) + SLOTS * (peer // 2 % 4)
        grads_ref[PIECE * slice_of : PIECE * (slice_of + 1), start : start + SLOTS] = grads
    sent = copies(
        out_sems, (grads_ref.at[:FEATS], self_hbm), (grads_ref.at[FEATS:], neigh_hbm)
    )
    sums = jnp.sum(back_ref[:, FEATS:ROWS, :].astype(F32), axis=0)
    total = sums[:, :FEATS] + sums[:, FEATS:]
    high = total.astype(BF16).astype(F32)
    hub_high = high.T.astype(BF16)
    hub_low = (total - high).T.astype(BF16)
    staged[0].wait()
    staged[1].wait()
    for tile in range(NODES // SPREAD):
        lanes = slice(SPREAD * tile, SPREAD * (tile + 1))
        node = lax.broadcasted_iota(jnp.int32, (SPREAD, 2 * SLOTS), 0) + SPREAD * tile
        grad = jnp.zeros((FEATS, SPREAD), F32)
        for pair in range(PEERS // 2):
            grad = grad + matmul(
                slots[:, 2 * SLOTS * pair : 2 * SLOTS * (pair + 1)],
                one_hot(node == pair_lanes(send_ref, pair)),
                NT,
            )
        hub_node = lax.broadcasted_iota(jnp.int32, (SPREAD, HUBS_OWN), 0) + SPREAD * tile
        hub_hot = one_hot(hub_node == hub_ref[...])
        grad = grad + matmul(hub_high, hub_hot, NT) + matmul(hub_low, hub_hot, NT)
        if tile == 0:
            staged[2].wait()
        out_ref[:, lanes] = (grad + base_ref[:, lanes]).astype(BF16)
    for copy in sent:
        copy.wait()


def spread_grads(returned, send_lanes, hub_own, base):
    return pl.pallas_call(
        spread_kernel,
        in_specs=[VMEM, HBM, HBM, HBM],
        out_specs=[VMEM, HBM, HBM],
        out_shape=[
            jax.ShapeDtypeStruct((FEATS, NODES), BF16),
            jax.ShapeDtypeStruct((FEATS, OUTS), F32),
            jax.ShapeDtypeStruct((FEATS, OUTS), F32),
        ],
        scratch_shapes=[
            pltpu.VMEM((PEERS, SLOTS), jnp.int32),
            pltpu.VMEM((1, HUBS_OWN), jnp.int32),
            pltpu.VMEM((FEATS, NODES), F32),
            pltpu.VMEM((2 * FEATS, OUTS), F32),
            pltpu.VMEM((FEATS, PEERS * SLOTS), BF16),
            pltpu.SemaphoreType.DMA((3,)),
            pltpu.SemaphoreType.DMA((2,)),
        ],
        compiler_params=params(52),
        cost_estimate=cost(2 * 256 * 4224 * 1024, 2 << 20),
        name="spread_grads",
    )(returned, send_lanes, hub_own, base)


SAME_CORE = [list(range(core, PEERS, 2)) for core in range(2)]


def exchange(blocks, axis, groups=None):
    return lax.all_to_all(blocks, axis, 0, 0, axis_index_groups=groups, tiled=True)


def other_core(block):
    return lax.ppermute(block, "row", [(i, i ^ 1) for i in range(PEERS)])


def per_device(feats, w_self, w_neigh, cotangent, loc_nbr, send_rows, recv_node, hub_rows, hub_nbr):
    send_lanes = send_rows.reshape(PEERS, SLOTS)
    recv_lanes = recv_node.reshape(PEERS, SLOTS)
    hub_own = hub_rows[None, :]
    half = HALF * (lax.axis_index("row") % 2)
    weights = lax.all_gather(
        lax.dynamic_slice_in_dim(jnp.concatenate([w_self, w_neigh], axis=0), half, HALF, 1),
        "col",
        axis=0,
        tiled=True,
    )
    incoming = exchange(gather_slots(feats, send_lanes, hub_own), "row")
    hub_lanes = hub_nbr.T
    local, hubs, local_sum = build_counts(feats, loc_nbr.T, hub_lanes)
    outgoing, degree = aggregate(feats, incoming, recv_lanes, local_sum, hub_lanes, cotangent)
    node_block = exchange(outgoing, "col")
    own_degree = lax.dynamic_slice_in_dim(degree[0], OWN * lax.axis_index("col"), OWN)[:, None]
    joined_mine = exchange(regroup(node_block), "row", SAME_CORE)
    joined, cots = prepare(node_block, other_core(node_block))
    slopes_out, slopes, hidden = forward(joined, cots, weights)
    slopes_rows = exchange(slopes_out, "row", SAME_CORE)
    joined_mine, slopes = lax.optimization_barrier((joined_mine, slopes))
    joined_theirs = other_core(joined_mine)
    keep, sent = backward(slopes, hidden, weights)
    parts = weight_parts(
        joined_mine, joined_theirs, slopes_rows, keep, other_core(sent), hidden, own_degree
    )
    back_block = exchange(parts, "col")
    returned = exchange(return_slots(back_block, recv_lanes, hubs), "row")
    base, hidden_out = local_grads(back_block, local)
    grad_feats, grad_self, grad_neigh = spread_grads(returned, send_lanes, hub_own, base)
    return (hidden_out, grad_feats, grad_self, grad_neigh)


def solution(mesh):
    return jax.shard_map(
        per_device,
        mesh=mesh,
        in_specs=(
            P("col", "row"),
            P("col", None),
            P("col", None),
            P("col", "row"),
            P("row", None),
            P("row", None, None),
            P("row", None, None),
            P("row"),
            P("row", None),
        ),
        out_specs=(P("col", "row"), P("col", "row"), P("col", None), P("col", None)),
        check_vma=False,
    )
```

```python
import jax
import jax.numpy as jnp
from jax import lax
from jax.experimental import pallas as pl
from jax.experimental.pallas import tpu as pltpu
from jax.sharding import PartitionSpec as P

NODES = 1024
FEATS = 64
PEERS = 32
SLOTS = 128
HUBS_OWN = 16
HUBS = 512
ROWS = 80
LAYERS = 16
OWN = 64
OUTS = 1024
BF16 = jnp.bfloat16
F32 = jnp.float32
NT = (((1,), (1,)), ((), ()))
NN = (((1,), (0,)), ((), ()))
MIB = 1 << 20


def params(mib):
    return pltpu.CompilerParams(vmem_limit_bytes=mib * MIB)


def cost(flops, moved):
    return pl.CostEstimate(flops=flops, bytes_accessed=moved, transcendentals=0)


def whole(shape):
    return pl.BlockSpec(shape, lambda *_: (0,) * len(shape))


HBM = pl.BlockSpec(memory_space=pltpu.HBM)
VMEM = pl.BlockSpec(memory_space=pltpu.VMEM)


def copies(sems, *pairs):
    started = []
    for i, (source, target) in enumerate(pairs):
        copy = pltpu.make_async_copy(source, target, sems.at[i])
        copy.start()
        started.append(copy)
    return started


def one_hot(mask):
    return jnp.where(mask, 1.0, 0.0).astype(BF16)


def matmul(a, b, dims):
    return lax.dot_general(a, b, dims, preferred_element_type=F32)


def pair_lanes(ref, pair):
    return jnp.concatenate([ref[2 * pair : 2 * pair + 1, :], ref[2 * pair + 1 : 2 * pair + 2, :]], axis=1)


def gather_kernel(x_hbm, send_hbm, hub_hbm, out_ref, x_ref, send_ref, hub_ref, sems):
    for copy in copies(sems, (x_hbm, x_ref), (send_hbm, send_ref), (hub_hbm, hub_ref)):
        copy.wait()
    x = x_ref[...]
    node = lax.broadcasted_iota(jnp.int32, (NODES, 2 * SLOTS), 0)
    hub_node = lax.broadcasted_iota(jnp.int32, (NODES, HUBS_OWN), 0)
    hub_feats = matmul(x, one_hot(hub_node == hub_ref[...]), NN)
    hub_rows = hub_feats.T
    hub_block = jnp.concatenate([hub_rows, jnp.zeros_like(hub_rows)], axis=1).astype(BF16)
    for pair in range(PEERS // 2):
        picked = matmul(x, one_hot(node == pair_lanes(send_ref, pair)), NN).astype(BF16)
        out_ref[2 * pair, :FEATS, :] = picked[:, :SLOTS]
        out_ref[2 * pair + 1, :FEATS, :] = picked[:, SLOTS:]
        out_ref[2 * pair, FEATS:, :] = hub_block
        out_ref[2 * pair + 1, FEATS:, :] = hub_block


def gather_slots(feats, send_lanes, hub_own):
    return pl.pallas_call(
        gather_kernel,
        in_specs=[HBM, HBM, HBM],
        out_shape=jax.ShapeDtypeStruct((PEERS, ROWS, SLOTS), BF16),
        scratch_shapes=[
            pltpu.VMEM((FEATS, NODES), BF16),
            pltpu.VMEM((PEERS, SLOTS), jnp.int32),
            pltpu.VMEM((1, HUBS_OWN), jnp.int32),
            pltpu.SemaphoreType.DMA((3,)),
        ],
        compiler_params=params(60),
        cost_estimate=cost(2 * 256 * 4096 * 1024, 1 << 20),
        name="gather_slots",
    )(feats, send_lanes, hub_own)


BUILD = 256
KEPT = 512


def counts_of(nbr_ref, rows):
    first = lax.broadcasted_iota(jnp.int32, (rows, nbr_ref.shape[1]), 0)
    counts = jnp.zeros(first.shape, F32)
    for k in range(nbr_ref.shape[0]):
        counts = counts + jnp.where(first == nbr_ref[k : k + 1, :], 1.0, 0.0)
    return counts.astype(BF16)


def build_kernel(x_ref, loc_ref, hub_ref, local_ref, hubs_ref, sum_ref):
    counts = counts_of(loc_ref, NODES)
    local_ref[...] = counts
    hubs_ref[...] = counts_of(hub_ref, HUBS)
    sum_ref[...] = matmul(x_ref[...], counts, NN)


def build_counts(feats, loc_lanes, hub_lanes):
    return pl.pallas_call(
        build_kernel,
        grid=(NODES // BUILD,),
        in_specs=[
            whole((FEATS, NODES)),
            pl.BlockSpec((loc_lanes.shape[0], BUILD), lambda i: (0, i)),
            pl.BlockSpec((hub_lanes.shape[0], BUILD), lambda i: (0, i)),
        ],
        out_specs=[
            pl.BlockSpec((NODES, BUILD), lambda i: (0, i)),
            pl.BlockSpec((HUBS, BUILD), lambda i: (0, i)),
            pl.BlockSpec((FEATS, BUILD), lambda i: (0, i)),
        ],
        out_shape=[
            jax.ShapeDtypeStruct((NODES, NODES), BF16),
            jax.ShapeDtypeStruct((HUBS, NODES), BF16),
            jax.ShapeDtypeStruct((KEPT, NODES), F32),
        ],
        compiler_params=params(60),
        cost_estimate=cost(1 << 30, 4 << 20),
        name="build_counts",
    )(feats, loc_lanes, hub_lanes)


AGG = 256


def fold_halves(block):
    return jnp.concatenate([block[: OWN // 2, :], block[OWN // 2 :, :]], axis=1)


NEIGHBOURS = 10.0


def aggregate_kernel(
    x_hbm, inc_ref, recv_hbm, sum_hbm, hub_hbm, cot_hbm, out_ref, degree_ref,
    slots, table, recv_ref, hub_ref, x_ref, cot_ref, sum_ref, sems,
):
    staged = copies(
        sems,
        (recv_hbm, recv_ref),
        (hub_hbm, hub_ref),
        (x_hbm, x_ref),
        (cot_hbm, cot_ref),
        (sum_hbm.at[:FEATS], sum_ref),
    )
    for peer in range(PEERS):
        slots[:FEATS, SLOTS * peer : SLOTS * (peer + 1)] = inc_ref[peer, :FEATS, :]
    slots[FEATS:, :] = jnp.ones((16, PEERS * SLOTS), BF16)
    rows = inc_ref[:, FEATS:, :].astype(F32).reshape(HUBS, SLOTS)
    table[...] = rows.T[:FEATS, :].astype(BF16)
    staged[0].wait()
    for tile in range(NODES // AGG):
        lanes = slice(AGG * tile, AGG * (tile + 1))
        node = lax.broadcasted_iota(jnp.int32, (AGG, 2 * SLOTS), 0) + AGG * tile
        remote = jnp.zeros((ROWS, AGG), F32)
        for pair in range(PEERS // 2):
            remote = remote + matmul(
                slots[:, 2 * SLOTS * pair : 2 * SLOTS * (pair + 1)],
                one_hot(node == pair_lanes(recv_ref, pair)),
                NT,
            )
        if tile == 0:
            for copy in staged[1:]:
                copy.wait()
        hubs = counts_of(hub_ref[:, lanes], HUBS)
        total = remote[:FEATS, :] + sum_ref[:, lanes] + matmul(table[...], hubs, NN)
        degree = remote[FEATS : FEATS + 8, :] + NEIGHBOURS
        degree_ref[:, lanes] = degree
        mean = (total / degree[0:1, :]).T
        nodes = jnp.concatenate([x_ref[:, lanes].astype(F32).T, mean], axis=1).astype(BF16)
        slopes = cot_ref[:, lanes].astype(F32).T
        for part in range(AGG // OWN):
            layer = AGG // OWN * tile + part
            out_ref[layer, :OWN, :] = nodes[OWN * part : OWN * (part + 1), :]
            out_ref[layer, OWN:, :] = fold_halves(slopes[OWN * part : OWN * (part + 1), :]).astype(BF16)


def aggregate(feats, incoming, recv_lanes, local_sum, hub_lanes, cotangent):
    return pl.pallas_call(
        aggregate_kernel,
        out_shape=[
            jax.ShapeDtypeStruct((LAYERS, 96, SLOTS), BF16),
            jax.ShapeDtypeStruct((8, NODES), F32),
        ],
        in_specs=[HBM, VMEM, HBM, HBM, HBM, HBM],
        scratch_shapes=[
            pltpu.VMEM((ROWS, PEERS * SLOTS), BF16),
            pltpu.VMEM((FEATS, HUBS), BF16),
            pltpu.VMEM((PEERS, SLOTS), jnp.int32),
            pltpu.VMEM((2, NODES), jnp.int32),
            pltpu.VMEM((FEATS, NODES), BF16),
            pltpu.VMEM((FEATS, NODES), BF16),
            pltpu.VMEM((FEATS, NODES), F32),
            pltpu.SemaphoreType.DMA((5,)),
        ],
        compiler_params=params(52),
        cost_estimate=cost(2 * 256 * 5632 * 1024, 3 << 20),
        name="aggregate",
    )(feats, incoming, recv_lanes, local_sum, hub_lanes, cotangent)


PIECE = 32
TILE = 256
CHIPS = PEERS // 2
SLICE = LAYERS * PIECE


def regroup_kernel(inc_ref, out_ref):
    group = lax.broadcasted_iota(jnp.int32, (OWN, SLOTS), 1) // PIECE
    for part in range(4):
        blocks = [inc_ref[4 * part + i, :OWN, :].astype(F32) for i in range(4)]
        for slice_of in range(4):
            tile = jnp.zeros((OWN, SLOTS), F32)
            for i in range(4):
                moved = blocks[i]
                if i != slice_of:
                    moved = pltpu.roll(moved, (PIECE * (i - slice_of)) % SLOTS, 1)
                tile = jnp.where(group == i, moved, tile)
            tile = tile.astype(BF16)
            for outs in range(4):
                out_ref[4 * slice_of + outs, :, SLOTS * part : SLOTS * (part + 1)] = tile


def regroup(node_block):
    return pl.pallas_call(
        regroup_kernel,
        out_shape=jax.ShapeDtypeStruct((CHIPS, OWN, SLICE), BF16),
        compiler_params=params(16),
        cost_estimate=cost(1 << 24, 2 << 20),
        name="regroup",
    )(node_block)


HALF = OUTS // 2
STEPS = 4


def prepare_kernel(own_block, other_block, joined_ref, cot_ref):
    core = lax.axis_index("row") % 2
    for layer in range(LAYERS):
        lanes = slice(SLOTS * layer, SLOTS * (layer + 1))
        joined_ref[0, :, lanes] = own_block[layer, :OWN, :]
        joined_ref[1, :, lanes] = other_block[layer, :OWN, :]
    for side, block in enumerate((own_block, other_block)):
        for pair in range(LAYERS // 4):
            even = block[8 * core + 2 * pair, OWN:, :].astype(F32)
            odd = block[8 * core + 2 * pair + 1, OWN:, :].astype(F32)
            top = jnp.concatenate([even[:, :FEATS], odd[:, :FEATS]], axis=1)
            bottom = jnp.concatenate([even[:, FEATS:], odd[:, FEATS:]], axis=1)
            cot_ref[side, :, SLOTS * pair : SLOTS * (pair + 1)] = jnp.concatenate(
                [top, bottom], axis=0
            ).astype(BF16)


def prepare(own_block, other_block):
    return pl.pallas_call(
        prepare_kernel,
        out_shape=[
            jax.ShapeDtypeStruct((2, OWN, 2 * OUTS), BF16),
            jax.ShapeDtypeStruct((2, OWN, HALF), BF16),
        ],
        compiler_params=params(16),
        cost_estimate=cost(1 << 20, 2 << 20),
        name="prepare",
    )(own_block, other_block)


def forward_kernel(
    joined_hbm, cot_hbm, weights_hbm, slopes_hbm, flat_hbm, hidden_hbm,
    joined, cots, weights, out_tile, flat, hidden, in_sems, out_sems,
):
    depth = 2 * OUTS // STEPS
    bands = [slice(depth * step, depth * (step + 1)) for step in range(STEPS)]
    staged = copies(
        in_sems,
        (joined_hbm, joined),
        *[(weights_hbm.at[band, :], weights.at[band, :]) for band in bands],
        (cot_hbm, cots),
    )
    staged[0].wait()
    preact = jnp.zeros((2 * OWN, HALF), F32)
    for step, band in enumerate(bands):
        staged[step + 1].wait()
        rows = joined[:, :, band].reshape(2 * OWN, depth)
        preact = preact + matmul(rows, weights[band, :], NN)
    staged[STEPS + 1].wait()
    sigmoid_part = jax.nn.sigmoid(preact)
    silu = preact * sigmoid_part
    slope = sigmoid_part * (1.0 + preact * (1.0 - sigmoid_part))
    slopes = (cots[...].reshape(2 * OWN, HALF).astype(F32) * slope).astype(BF16)
    for outs in range(4):
        out_tile[outs] = slopes[:, SLOTS * outs : SLOTS * (outs + 1)]
    sent = []
    for chip in range(CHIPS):
        copy = pltpu.make_async_copy(out_tile.at[chip % 4], slopes_hbm.at[chip], out_sems.at[chip])
        copy.start()
        sent.append(copy)
    flat[...] = slopes
    for block in range(2):
        for layer in range(LAYERS // 2):
            tile = silu[OWN * block : OWN * (block + 1), FEATS * layer : FEATS * (layer + 1)]
            hidden[block, layer] = fold_halves(tile).astype(BF16)
    for i, (source, target) in enumerate(((flat, flat_hbm), (hidden, hidden_hbm))):
        copy = pltpu.make_async_copy(source, target, out_sems.at[CHIPS + i])
        copy.start()
        sent.append(copy)
    for copy in sent:
        copy.wait()


def forward(joined, cots, weights):
    return pl.pallas_call(
        forward_kernel,
        in_specs=[HBM, HBM, HBM],
        out_specs=[HBM, HBM, HBM],
        out_shape=[
            jax.ShapeDtypeStruct((CHIPS, 2 * OWN, SLOTS), BF16),
            jax.ShapeDtypeStruct((2 * OWN, HALF), BF16),
            jax.ShapeDtypeStruct((2, LAYERS // 2, OWN // 2, SLOTS), BF16),
        ],
        scratch_shapes=[
            pltpu.VMEM((2, OWN, 2 * OUTS), BF16),
            pltpu.VMEM((2, OWN, HALF), BF16),
            pltpu.VMEM((2 * OUTS, HALF), BF16),
            pltpu.VMEM((4, 2 * OWN, SLOTS), BF16),
            pltpu.VMEM((2 * OWN, HALF), BF16),
            pltpu.VMEM((2, LAYERS // 2, OWN // 2, SLOTS), BF16),
            pltpu.SemaphoreType.DMA((STEPS + 2,)),
            pltpu.SemaphoreType.DMA((CHIPS + 2,)),
        ],
        compiler_params=params(60),
        cost_estimate=cost(2 * 256 * 2048 * 512, 4 << 20),
        name="forward",
    )(joined, cots, weights)


SWAP = LAYERS + 4


def backward_kernel(slopes_ref, hidden_ref, weights_ref, keep_ref, send_ref):
    back = matmul(slopes_ref[...], weights_ref[...], NT)
    keep_ref[...] = back[:OWN, :]
    for layer in range(LAYERS):
        send_ref[layer] = back[OWN:, SLOTS * layer : SLOTS * (layer + 1)].astype(BF16)
    for pair in range(LAYERS // 4):
        send_ref[LAYERS + pair] = hidden_ref[1, 2 * pair : 2 * pair + 2].reshape(OWN, SLOTS)


def backward(slopes, hidden, weights):
    return pl.pallas_call(
        backward_kernel,
        out_shape=[
            jax.ShapeDtypeStruct((OWN, 2 * OUTS), F32),
            jax.ShapeDtypeStruct((SWAP, OWN, SLOTS), BF16),
        ],
        compiler_params=params(16),
        cost_estimate=cost(2 * 256 * 2048 * 512, 4 << 20),
        name="backward",
    )(slopes, hidden, weights)


def weight_kernel(
    mine_hbm, theirs_hbm, slopes_ref, keep_hbm, swapped_hbm, hidden_hbm, degree_hbm, out_ref,
    mine, theirs, keep, swapped, hidden, degree, sems,
):
    core = lax.axis_index("row") % 2
    staged = copies(
        sems,
        (degree_hbm, degree),
        (keep_hbm, keep),
        (swapped_hbm, swapped),
        (hidden_hbm.at[0], hidden),
        (mine_hbm, mine),
        (theirs_hbm, theirs),
    )
    slopes = [
        slopes_ref[:, OWN * side : OWN * (side + 1), :].astype(F32).reshape(CHIPS * OWN, SLOTS)
        for side in range(2)
    ]
    columns = [rows.T.astype(BF16) for rows in slopes]
    for copy in staged[:4]:
        copy.wait()
    direct = lax.broadcasted_iota(jnp.int32, (OWN, SLOTS), 1) < FEATS
    divisor = jnp.where(direct, 1.0, degree[...])
    for layer in range(LAYERS):
        back = keep[:, SLOTS * layer : SLOTS * (layer + 1)] + swapped[layer].astype(F32)
        out_ref[layer, :OWN, :] = (back / divisor).astype(BF16)
    for pair in range(LAYERS // 4):
        for side in range(2):
            layer = 2 * pair + side
            out_ref[8 * core + layer, OWN:96, :] = hidden[layer]
            out_ref[8 * (1 - core) + layer, OWN:96, :] = swapped[
                LAYERS + pair, OWN // 2 * side : OWN // 2 * (side + 1), :
            ]
    part = jnp.zeros((SLOTS, SLICE), F32)
    for side, rows in enumerate((mine, theirs)):
        staged[4 + side].wait()
        part = part + matmul(columns[side], rows[...].reshape(CHIPS * OWN, SLICE), NN)
    part = part.T.astype(BF16)
    for layer in range(LAYERS):
        out_ref[layer, 96:, :] = part[PIECE * layer : PIECE * (layer + 1), :]


def weight_parts(mine, theirs, slopes_rows, keep, swapped, hidden, own_degree):
    return pl.pallas_call(
        weight_kernel,
        in_specs=[HBM, HBM, VMEM, HBM, HBM, HBM, HBM],
        out_shape=jax.ShapeDtypeStruct((LAYERS, SLOTS, SLOTS), BF16),
        scratch_shapes=[
            pltpu.VMEM((CHIPS, OWN, SLICE), BF16),
            pltpu.VMEM((CHIPS, OWN, SLICE), BF16),
            pltpu.VMEM((OWN, 2 * OUTS), F32),
            pltpu.VMEM((SWAP, OWN, SLOTS), BF16),
            pltpu.VMEM((LAYERS // 2, OWN // 2, SLOTS), BF16),
            pltpu.VMEM((OWN, 1), F32),
            pltpu.SemaphoreType.DMA((6,)),
        ],
        compiler_params=params(52),
        cost_estimate=cost(2 * 256 * 2048 * 256, 4 << 20),
        name="weight_parts",
    )(mine, theirs, slopes_rows, keep, swapped, hidden, own_degree)


RETURN_ROWS = 112


def return_kernel(
    back_ref, recv_hbm, hubs_hbm, out_hbm, recv_ref, hubs_ref, out_ref, in_sems, out_sems
):
    staged = copies(in_sems, (recv_hbm, recv_ref), (hubs_hbm, hubs_ref))
    node = lax.broadcasted_iota(jnp.int32, (NODES, 2 * SLOTS), 0)
    share = back_ref[:, :OWN, :].astype(F32).reshape(NODES, SLOTS).T[FEATS:, :].astype(BF16)
    staged[0].wait()
    sums = jnp.sum(back_ref[:, 96:, :].astype(F32), axis=0).astype(BF16)
    sent = []
    for pair in range(PEERS // 2):
        values = matmul(share, one_hot(node == pair_lanes(recv_ref, pair)), NN).astype(BF16)
        for side in range(2):
            peer = 2 * pair + side
            out_ref[peer, :FEATS, :] = values[:, SLOTS * side : SLOTS * (side + 1)]
            out_ref[peer, ROWS:, :] = sums
        if pair == 3:
            staged[1].wait()
            terms = matmul(share, hubs_ref[...], NT).T
            high = terms.astype(BF16).astype(F32)
            both = jnp.concatenate([high, terms - high], axis=1)
            out_ref[:, FEATS:ROWS, :] = both.reshape(PEERS, HUBS_OWN, SLOTS).astype(BF16)
        if pair % 4 == 3:
            part = pl.ds(2 * pair - 6, 8)
            copy = pltpu.make_async_copy(out_ref.at[part], out_hbm.at[part], out_sems.at[pair // 4])
            copy.start()
            sent.append(copy)
    for copy in sent:
        copy.wait()


def return_slots(back_block, recv_lanes, hubs):
    return pl.pallas_call(
        return_kernel,
        in_specs=[VMEM, HBM, HBM],
        out_specs=HBM,
        out_shape=jax.ShapeDtypeStruct((PEERS, RETURN_ROWS, SLOTS), BF16),
        scratch_shapes=[
            pltpu.VMEM((PEERS, SLOTS), jnp.int32),
            pltpu.VMEM((HUBS, NODES), BF16),
            pltpu.VMEM((PEERS, RETURN_ROWS, SLOTS), BF16),
            pltpu.SemaphoreType.DMA((2,)),
            pltpu.SemaphoreType.DMA((4,)),
        ],
        compiler_params=params(53),
        cost_estimate=cost(2 * 256 * 4608 * 1024, 3 << 20),
        name="return_slots",
    )(back_block, recv_lanes, hubs)


def local_kernel(back_ref, local_ref, base_hbm, hidden_ref, base_ref, sems):
    columns = back_ref[:, :OWN, :].astype(F32).reshape(NODES, SLOTS).T
    share = columns[FEATS:, :].astype(BF16)
    base_ref[...] = columns[:FEATS, :] + matmul(share, local_ref[...], NT)
    (sent,) = copies(sems, (base_ref, base_hbm.at[:FEATS]))
    folded = back_ref[:, OWN:96, :].astype(F32)
    rows = jnp.concatenate([folded[:, :, :FEATS], folded[:, :, FEATS:]], axis=1)
    hidden_ref[...] = rows.reshape(NODES, FEATS).T.astype(BF16)
    sent.wait()


def local_grads(back_block, local):
    return pl.pallas_call(
        local_kernel,
        out_specs=[HBM, VMEM],
        out_shape=[
            jax.ShapeDtypeStruct((KEPT, NODES), F32),
            jax.ShapeDtypeStruct((FEATS, NODES), BF16),
        ],
        scratch_shapes=[pltpu.VMEM((FEATS, NODES), F32), pltpu.SemaphoreType.DMA((1,))],
        compiler_params=params(60),
        cost_estimate=cost(2 * 256 * 1024 * 1024, 3 << 20),
        name="local_grads",
    )(back_block, local)


SPREAD = 256


def spread_kernel(
    back_ref, send_hbm, hub_hbm, base_hbm, out_ref, self_hbm, neigh_hbm,
    send_ref, hub_ref, base_ref, grads_ref, slots, in_sems, out_sems,
):
    staged = copies(in_sems, (send_hbm, send_ref), (hub_hbm, hub_ref), (base_hbm.at[:FEATS], base_ref))
    for peer in range(PEERS):
        slots[:, SLOTS * peer : SLOTS * (peer + 1)] = back_ref[peer, :FEATS, :]
        grads = back_ref[peer, ROWS:, :].astype(F32)
        slice_of, start = peer // 8, HALF * (peer % 2) + SLOTS * (peer // 2 % 4)
        grads_ref[PIECE * slice_of : PIECE * (slice_of + 1), start : start + SLOTS] = grads
    sent = copies(
        out_sems, (grads_ref.at[:FEATS], self_hbm), (grads_ref.at[FEATS:], neigh_hbm)
    )
    sums = jnp.sum(back_ref[:, FEATS:ROWS, :].astype(F32), axis=0)
    total = sums[:, :FEATS] + sums[:, FEATS:]
    high = total.astype(BF16).astype(F32)
    hub_high = high.T.astype(BF16)
    hub_low = (total - high).T.astype(BF16)
    staged[0].wait()
    staged[1].wait()
    for tile in range(NODES // SPREAD):
        lanes = slice(SPREAD * tile, SPREAD * (tile + 1))
        node = lax.broadcasted_iota(jnp.int32, (SPREAD, 2 * SLOTS), 0) + SPREAD * tile
        grad = jnp.zeros((FEATS, SPREAD), F32)
        for pair in range(PEERS // 2):
            grad = grad + matmul(
                slots[:, 2 * SLOTS * pair : 2 * SLOTS * (pair + 1)],
                one_hot(node == pair_lanes(send_ref, pair)),
                NT,
            )
        hub_node = lax.broadcasted_iota(jnp.int32, (SPREAD, HUBS_OWN), 0) + SPREAD * tile
        hub_hot = one_hot(hub_node == hub_ref[...])
        grad = grad + matmul(hub_high, hub_hot, NT) + matmul(hub_low, hub_hot, NT)
        if tile == 0:
            staged[2].wait()
        out_ref[:, lanes] = (grad + base_ref[:, lanes]).astype(BF16)
    for copy in sent:
        copy.wait()


def spread_grads(returned, send_lanes, hub_own, base):
    return pl.pallas_call(
        spread_kernel,
        in_specs=[VMEM, HBM, HBM, HBM],
        out_specs=[VMEM, HBM, HBM],
        out_shape=[
            jax.ShapeDtypeStruct((FEATS, NODES), BF16),
            jax.ShapeDtypeStruct((FEATS, OUTS), F32),
            jax.ShapeDtypeStruct((FEATS, OUTS), F32),
        ],
        scratch_shapes=[
            pltpu.VMEM((PEERS, SLOTS), jnp.int32),
            pltpu.VMEM((1, HUBS_OWN), jnp.int32),
            pltpu.VMEM((FEATS, NODES), F32),
            pltpu.VMEM((2 * FEATS, OUTS), F32),
            pltpu.VMEM((FEATS, PEERS * SLOTS), BF16),
            pltpu.SemaphoreType.DMA((3,)),
            pltpu.SemaphoreType.DMA((2,)),
        ],
        compiler_params=params(52),
        cost_estimate=cost(2 * 256 * 4224 * 1024, 2 << 20),
        name="spread_grads",
    )(returned, send_lanes, hub_own, base)


SAME_CORE = [list(range(core, PEERS, 2)) for core in range(2)]


def exchange(blocks, axis, groups=None):
    return lax.all_to_all(blocks, axis, 0, 0, axis_index_groups=groups, tiled=True)


def other_core(block):
    return lax.ppermute(block, "row", [(i, i ^ 1) for i in range(PEERS)])


def per_device(feats, w_self, w_neigh, cotangent, loc_nbr, send_rows, recv_node, hub_rows, hub_nbr):
    send_lanes = send_rows.reshape(PEERS, SLOTS)
    recv_lanes = recv_node.reshape(PEERS, SLOTS)
    hub_own = hub_rows[None, :]
    half = HALF * (lax.axis_index("row") % 2)
    weights = lax.all_gather(
        lax.dynamic_slice_in_dim(jnp.concatenate([w_self, w_neigh], axis=0), half, HALF, 1),
        "col",
        axis=0,
        tiled=True,
    )
    incoming = exchange(gather_slots(feats, send_lanes, hub_own), "row")
    hub_lanes = hub_nbr.T
    local, hubs, local_sum = build_counts(feats, loc_nbr.T, hub_lanes)
    outgoing, degree = aggregate(feats, incoming, recv_lanes, local_sum, hub_lanes, cotangent)
    node_block = exchange(outgoing, "col")
    own_degree = lax.dynamic_slice_in_dim(degree[0], OWN * lax.axis_index("col"), OWN)[:, None]
    joined_mine = exchange(regroup(node_block), "row", SAME_CORE)
    joined, cots = prepare(node_block, other_core(node_block))
    slopes_out, slopes, hidden = forward(joined, cots, weights)
    slopes_rows = exchange(slopes_out, "row", SAME_CORE)
    joined_mine, slopes = lax.optimization_barrier((joined_mine, slopes))
    joined_theirs = other_core(joined_mine)
    keep, sent = backward(slopes, hidden, weights)
    parts = weight_parts(
        joined_mine, joined_theirs, slopes_rows, keep, other_core(sent), hidden, own_degree
    )
    back_block = exchange(parts, "col")
    returned = exchange(return_slots(back_block, recv_lanes, hubs), "row")
    base, hidden_out = local_grads(back_block, local)
    grad_feats, grad_self, grad_neigh = spread_grads(returned, send_lanes, hub_own, base)
    return (hidden_out, grad_feats, grad_self, grad_neigh)


def solution(mesh):
    return jax.shard_map(
        per_device,
        mesh=mesh,
        in_specs=(
            P("col", "row"),
            P("col", None),
            P("col", None),
            P("col", "row"),
            P("row", None),
            P("row", None, None),
            P("row", None, None),
            P("row"),
            P("row", None),
        ),
        out_specs=(P("col", "row"), P("col", "row"), P("col", None), P("col", None)),
        check_vma=False,
    )
```

```python
import jax
import jax.numpy as jnp
from jax import lax
from jax.experimental import pallas as pl
from jax.experimental.pallas import tpu as pltpu
from jax.sharding import PartitionSpec as P

NODES = 1024
FEATS = 64
PEERS = 32
SLOTS = 128
HUBS_OWN = 16
HUBS = 512
ROWS = 80
LAYERS = 16
OWN = 64
OUTS = 1024
BF16 = jnp.bfloat16
F32 = jnp.float32
NT = (((1,), (1,)), ((), ()))
NN = (((1,), (0,)), ((), ()))
MIB = 1 << 20


def params(mib):
    return pltpu.CompilerParams(vmem_limit_bytes=mib * MIB)


def cost(flops, moved):
    return pl.CostEstimate(flops=flops, bytes_accessed=moved, transcendentals=0)


def whole(shape):
    return pl.BlockSpec(shape, lambda *_: (0,) * len(shape))


HBM = pl.BlockSpec(memory_space=pltpu.HBM)
VMEM = pl.BlockSpec(memory_space=pltpu.VMEM)


def copies(sems, *pairs):
    started = []
    for i, (source, target) in enumerate(pairs):
        copy = pltpu.make_async_copy(source, target, sems.at[i])
        copy.start()
        started.append(copy)
    return started


def one_hot(mask):
    return jnp.where(mask, 1.0, 0.0).astype(BF16)


def matmul(a, b, dims):
    return lax.dot_general(a, b, dims, preferred_element_type=F32)


def pair_lanes(ref, pair):
    return jnp.concatenate([ref[2 * pair : 2 * pair + 1, :], ref[2 * pair + 1 : 2 * pair + 2, :]], axis=1)


def gather_kernel(x_hbm, send_hbm, hub_hbm, out_ref, x_ref, send_ref, hub_ref, sems):
    for copy in copies(sems, (x_hbm, x_ref), (send_hbm, send_ref), (hub_hbm, hub_ref)):
        copy.wait()
    x = x_ref[...]
    node = lax.broadcasted_iota(jnp.int32, (NODES, 2 * SLOTS), 0)
    hub_node = lax.broadcasted_iota(jnp.int32, (NODES, HUBS_OWN), 0)
    hub_feats = matmul(x, one_hot(hub_node == hub_ref[...]), NN)
    hub_rows = hub_feats.T
    hub_block = jnp.concatenate([hub_rows, jnp.zeros_like(hub_rows)], axis=1).astype(BF16)
    for pair in range(PEERS // 2):
        picked = matmul(x, one_hot(node == pair_lanes(send_ref, pair)), NN).astype(BF16)
        out_ref[2 * pair, :FEATS, :] = picked[:, :SLOTS]
        out_ref[2 * pair + 1, :FEATS, :] = picked[:, SLOTS:]
        out_ref[2 * pair, FEATS:, :] = hub_block
        out_ref[2 * pair + 1, FEATS:, :] = hub_block


def gather_slots(feats, send_lanes, hub_own):
    return pl.pallas_call(
        gather_kernel,
        in_specs=[HBM, HBM, HBM],
        out_shape=jax.ShapeDtypeStruct((PEERS, ROWS, SLOTS), BF16),
        scratch_shapes=[
            pltpu.VMEM((FEATS, NODES), BF16),
            pltpu.VMEM((PEERS, SLOTS), jnp.int32),
            pltpu.VMEM((1, HUBS_OWN), jnp.int32),
            pltpu.SemaphoreType.DMA((3,)),
        ],
        compiler_params=params(60),
        cost_estimate=cost(2 * 256 * 4096 * 1024, 1 << 20),
        name="gather_slots",
    )(feats, send_lanes, hub_own)


BUILD = 256
KEPT = 512


def counts_of(nbr_ref, rows):
    first = lax.broadcasted_iota(jnp.int32, (rows, nbr_ref.shape[1]), 0)
    counts = jnp.zeros(first.shape, F32)
    for k in range(nbr_ref.shape[0]):
        counts = counts + jnp.where(first == nbr_ref[k : k + 1, :], 1.0, 0.0)
    return counts.astype(BF16)


def build_kernel(x_ref, loc_ref, hub_ref, local_ref, hubs_ref, sum_ref):
    counts = counts_of(loc_ref, NODES)
    local_ref[...] = counts
    hubs_ref[...] = counts_of(hub_ref, HUBS)
    sum_ref[...] = matmul(x_ref[...], counts, NN)


def build_counts(feats, loc_lanes, hub_lanes):
    return pl.pallas_call(
        build_kernel,
        grid=(NODES // BUILD,),
        in_specs=[
            whole((FEATS, NODES)),
            pl.BlockSpec((loc_lanes.shape[0], BUILD), lambda i: (0, i)),
            pl.BlockSpec((hub_lanes.shape[0], BUILD), lambda i: (0, i)),
        ],
        out_specs=[
            pl.BlockSpec((NODES, BUILD), lambda i: (0, i)),
            pl.BlockSpec((HUBS, BUILD), lambda i: (0, i)),
            pl.BlockSpec((FEATS, BUILD), lambda i: (0, i)),
        ],
        out_shape=[
            jax.ShapeDtypeStruct((NODES, NODES), BF16),
            jax.ShapeDtypeStruct((HUBS, NODES), BF16),
            jax.ShapeDtypeStruct((KEPT, NODES), F32),
        ],
        compiler_params=params(60),
        cost_estimate=cost(1 << 30, 4 << 20),
        name="build_counts",
    )(feats, loc_lanes, hub_lanes)


AGG = 256


def fold_halves(block):
    return jnp.concatenate([block[: OWN // 2, :], block[OWN // 2 :, :]], axis=1)


NEIGHBOURS = 10.0


def aggregate_kernel(
    x_hbm, inc_ref, recv_hbm, sum_hbm, hub_hbm, cot_hbm, out_ref, degree_ref,
    slots, table, recv_ref, hub_ref, x_ref, cot_ref, sum_ref, sems,
):
    staged = copies(
        sems,
        (recv_hbm, recv_ref),
        (hub_hbm, hub_ref),
        (x_hbm, x_ref),
        (cot_hbm, cot_ref),
        (sum_hbm.at[:FEATS], sum_ref),
    )
    for peer in range(PEERS):
        slots[:FEATS, SLOTS * peer : SLOTS * (peer + 1)] = inc_ref[peer, :FEATS, :]
    slots[FEATS:, :] = jnp.ones((16, PEERS * SLOTS), BF16)
    rows = inc_ref[:, FEATS:, :].astype(F32).reshape(HUBS, SLOTS)
    table[...] = rows.T[:FEATS, :].astype(BF16)
    staged[0].wait()
    for tile in range(NODES // AGG):
        lanes = slice(AGG * tile, AGG * (tile + 1))
        node = lax.broadcasted_iota(jnp.int32, (AGG, 2 * SLOTS), 0) + AGG * tile
        remote = jnp.zeros((ROWS, AGG), F32)
        for pair in range(PEERS // 2):
            remote = remote + matmul(
                slots[:, 2 * SLOTS * pair : 2 * SLOTS * (pair + 1)],
                one_hot(node == pair_lanes(recv_ref, pair)),
                NT,
            )
        if tile == 0:
            for copy in staged[1:]:
                copy.wait()
        hubs = counts_of(hub_ref[:, lanes], HUBS)
        total = remote[:FEATS, :] + sum_ref[:, lanes] + matmul(table[...], hubs, NN)
        degree = remote[FEATS : FEATS + 8, :] + NEIGHBOURS
        degree_ref[:, lanes] = degree
        mean = (total / degree[0:1, :]).T
        nodes = jnp.concatenate([x_ref[:, lanes].astype(F32).T, mean], axis=1).astype(BF16)
        slopes = cot_ref[:, lanes].astype(F32).T
        for part in range(AGG // OWN):
            layer = AGG // OWN * tile + part
            out_ref[layer, :OWN, :] = nodes[OWN * part : OWN * (part + 1), :]
            out_ref[layer, OWN:, :] = fold_halves(slopes[OWN * part : OWN * (part + 1), :]).astype(BF16)


def aggregate(feats, incoming, recv_lanes, local_sum, hub_lanes, cotangent):
    return pl.pallas_call(
        aggregate_kernel,
        out_shape=[
            jax.ShapeDtypeStruct((LAYERS, 96, SLOTS), BF16),
            jax.ShapeDtypeStruct((8, NODES), F32),
        ],
        in_specs=[HBM, VMEM, HBM, HBM, HBM, HBM],
        scratch_shapes=[
            pltpu.VMEM((ROWS, PEERS * SLOTS), BF16),
            pltpu.VMEM((FEATS, HUBS), BF16),
            pltpu.VMEM((PEERS, SLOTS), jnp.int32),
            pltpu.VMEM((2, NODES), jnp.int32),
            pltpu.VMEM((FEATS, NODES), BF16),
            pltpu.VMEM((FEATS, NODES), BF16),
            pltpu.VMEM((FEATS, NODES), F32),
            pltpu.SemaphoreType.DMA((5,)),
        ],
        compiler_params=params(52),
        cost_estimate=cost(2 * 256 * 5632 * 1024, 3 << 20),
        name="aggregate",
    )(feats, incoming, recv_lanes, local_sum, hub_lanes, cotangent)


PIECE = 32
TILE = 256
CHIPS = PEERS // 2
SLICE = LAYERS * PIECE


def regroup_kernel(inc_ref, out_ref):
    group = lax.broadcasted_iota(jnp.int32, (OWN, SLOTS), 1) // PIECE
    for part in range(4):
        blocks = [inc_ref[4 * part + i, :OWN, :].astype(F32) for i in range(4)]
        for slice_of in range(4):
            tile = jnp.zeros((OWN, SLOTS), F32)
            for i in range(4):
                moved = blocks[i]
                if i != slice_of:
                    moved = pltpu.roll(moved, (PIECE * (i - slice_of)) % SLOTS, 1)
                tile = jnp.where(group == i, moved, tile)
            tile = tile.astype(BF16)
            for outs in range(4):
                out_ref[4 * slice_of + outs, :, SLOTS * part : SLOTS * (part + 1)] = tile


def regroup(node_block):
    return pl.pallas_call(
        regroup_kernel,
        out_shape=jax.ShapeDtypeStruct((CHIPS, OWN, SLICE), BF16),
        compiler_params=params(16),
        cost_estimate=cost(1 << 24, 2 << 20),
        name="regroup",
    )(node_block)


HALF = OUTS // 2
STEPS = 4


def prepare_kernel(own_block, other_block, joined_ref, cot_ref):
    core = lax.axis_index("row") % 2
    for layer in range(LAYERS):
        lanes = slice(SLOTS * layer, SLOTS * (layer + 1))
        joined_ref[0, :, lanes] = own_block[layer, :OWN, :]
        joined_ref[1, :, lanes] = other_block[layer, :OWN, :]
    for side, block in enumerate((own_block, other_block)):
        for pair in range(LAYERS // 4):
            even = block[8 * core + 2 * pair, OWN:, :].astype(F32)
            odd = block[8 * core + 2 * pair + 1, OWN:, :].astype(F32)
            top = jnp.concatenate([even[:, :FEATS], odd[:, :FEATS]], axis=1)
            bottom = jnp.concatenate([even[:, FEATS:], odd[:, FEATS:]], axis=1)
            cot_ref[side, :, SLOTS * pair : SLOTS * (pair + 1)] = jnp.concatenate(
                [top, bottom], axis=0
            ).astype(BF16)


def prepare(own_block, other_block):
    return pl.pallas_call(
        prepare_kernel,
        out_shape=[
            jax.ShapeDtypeStruct((2, OWN, 2 * OUTS), BF16),
            jax.ShapeDtypeStruct((2, OWN, HALF), BF16),
        ],
        compiler_params=params(16),
        cost_estimate=cost(1 << 20, 2 << 20),
        name="prepare",
    )(own_block, other_block)


def forward_kernel(
    joined_hbm, cot_hbm, weights_hbm, slopes_hbm, flat_hbm, hidden_hbm,
    joined, cots, weights, out_tile, flat, hidden, in_sems, out_sems,
):
    depth = 2 * OUTS // STEPS
    bands = [slice(depth * step, depth * (step + 1)) for step in range(STEPS)]
    staged = copies(
        in_sems,
        (joined_hbm, joined),
        *[(weights_hbm.at[band, :], weights.at[band, :]) for band in bands],
        (cot_hbm, cots),
    )
    staged[0].wait()
    preact = jnp.zeros((2 * OWN, HALF), F32)
    for step, band in enumerate(bands):
        staged[step + 1].wait()
        rows = joined[:, :, band].reshape(2 * OWN, depth)
        preact = preact + matmul(rows, weights[band, :], NN)
    staged[STEPS + 1].wait()
    sigmoid_part = jax.nn.sigmoid(preact)
    silu = preact * sigmoid_part
    slope = sigmoid_part * (1.0 + preact * (1.0 - sigmoid_part))
    slopes = (cots[...].reshape(2 * OWN, HALF).astype(F32) * slope).astype(BF16)
    for outs in range(4):
        out_tile[outs] = slopes[:, SLOTS * outs : SLOTS * (outs + 1)]
    sent = []
    for chip in range(CHIPS):
        copy = pltpu.make_async_copy(out_tile.at[chip % 4], slopes_hbm.at[chip], out_sems.at[chip])
        copy.start()
        sent.append(copy)
    flat[...] = slopes
    for block in range(2):
        for layer in range(LAYERS // 2):
            tile = silu[OWN * block : OWN * (block + 1), FEATS * layer : FEATS * (layer + 1)]
            hidden[block, layer] = fold_halves(tile).astype(BF16)
    for i, (source, target) in enumerate(((flat, flat_hbm), (hidden, hidden_hbm))):
        copy = pltpu.make_async_copy(source, target, out_sems.at[CHIPS + i])
        copy.start()
        sent.append(copy)
    for copy in sent:
        copy.wait()


def forward(joined, cots, weights):
    return pl.pallas_call(
        forward_kernel,
        in_specs=[HBM, HBM, HBM],
        out_specs=[HBM, HBM, HBM],
        out_shape=[
            jax.ShapeDtypeStruct((CHIPS, 2 * OWN, SLOTS), BF16),
            jax.ShapeDtypeStruct((2 * OWN, HALF), BF16),
            jax.ShapeDtypeStruct((2, LAYERS // 2, OWN // 2, SLOTS), BF16),
        ],
        scratch_shapes=[
            pltpu.VMEM((2, OWN, 2 * OUTS), BF16),
            pltpu.VMEM((2, OWN, HALF), BF16),
            pltpu.VMEM((2 * OUTS, HALF), BF16),
            pltpu.VMEM((4, 2 * OWN, SLOTS), BF16),
            pltpu.VMEM((2 * OWN, HALF), BF16),
            pltpu.VMEM((2, LAYERS // 2, OWN // 2, SLOTS), BF16),
            pltpu.SemaphoreType.DMA((STEPS + 2,)),
            pltpu.SemaphoreType.DMA((CHIPS + 2,)),
        ],
        compiler_params=params(60),
        cost_estimate=cost(2 * 256 * 2048 * 512, 4 << 20),
        name="forward",
    )(joined, cots, weights)


SWAP = LAYERS + 4


def backward_kernel(slopes_ref, hidden_ref, weights_ref, keep_ref, send_ref):
    back = matmul(slopes_ref[...], weights_ref[...], NT)
    keep_ref[...] = back[:OWN, :]
    for layer in range(LAYERS):
        send_ref[layer] = back[OWN:, SLOTS * layer : SLOTS * (layer + 1)].astype(BF16)
    for pair in range(LAYERS // 4):
        send_ref[LAYERS + pair] = hidden_ref[1, 2 * pair : 2 * pair + 2].reshape(OWN, SLOTS)


def backward(slopes, hidden, weights):
    return pl.pallas_call(
        backward_kernel,
        out_shape=[
            jax.ShapeDtypeStruct((OWN, 2 * OUTS), F32),
            jax.ShapeDtypeStruct((SWAP, OWN, SLOTS), BF16),
        ],
        compiler_params=params(16),
        cost_estimate=cost(2 * 256 * 2048 * 512, 4 << 20),
        name="backward",
    )(slopes, hidden, weights)


def weight_kernel(
    mine_hbm, theirs_hbm, slopes_ref, keep_hbm, swapped_hbm, hidden_hbm, degree_hbm, out_ref,
    mine, theirs, keep, swapped, hidden, degree, sems,
):
    core = lax.axis_index("row") % 2
    staged = copies(
        sems,
        (degree_hbm, degree),
        (keep_hbm, keep),
        (swapped_hbm, swapped),
        (hidden_hbm.at[0], hidden),
        (mine_hbm, mine),
        (theirs_hbm, theirs),
    )
    slopes = [
        slopes_ref[:, OWN * side : OWN * (side + 1), :].astype(F32).reshape(CHIPS * OWN, SLOTS)
        for side in range(2)
    ]
    columns = [rows.T.astype(BF16) for rows in slopes]
    for copy in staged[:4]:
        copy.wait()
    direct = lax.broadcasted_iota(jnp.int32, (OWN, SLOTS), 1) < FEATS
    divisor = jnp.where(direct, 1.0, degree[...])
    for layer in range(LAYERS):
        back = keep[:, SLOTS * layer : SLOTS * (layer + 1)] + swapped[layer].astype(F32)
        out_ref[layer, :OWN, :] = (back / divisor).astype(BF16)
    for pair in range(LAYERS // 4):
        for side in range(2):
            layer = 2 * pair + side
            out_ref[8 * core + layer, OWN:96, :] = hidden[layer]
            out_ref[8 * (1 - core) + layer, OWN:96, :] = swapped[
                LAYERS + pair, OWN // 2 * side : OWN // 2 * (side + 1), :
            ]
    part = jnp.zeros((SLOTS, SLICE), F32)
    for side, rows in enumerate((mine, theirs)):
        staged[4 + side].wait()
        part = part + matmul(columns[side], rows[...].reshape(CHIPS * OWN, SLICE), NN)
    part = part.T.astype(BF16)
    for layer in range(LAYERS):
        out_ref[layer, 96:, :] = part[PIECE * layer : PIECE * (layer + 1), :]


def weight_parts(mine, theirs, slopes_rows, keep, swapped, hidden, own_degree):
    return pl.pallas_call(
        weight_kernel,
        in_specs=[HBM, HBM, VMEM, HBM, HBM, HBM, HBM],
        out_shape=jax.ShapeDtypeStruct((LAYERS, SLOTS, SLOTS), BF16),
        scratch_shapes=[
            pltpu.VMEM((CHIPS, OWN, SLICE), BF16),
            pltpu.VMEM((CHIPS, OWN, SLICE), BF16),
            pltpu.VMEM((OWN, 2 * OUTS), F32),
            pltpu.VMEM((SWAP, OWN, SLOTS), BF16),
            pltpu.VMEM((LAYERS // 2, OWN // 2, SLOTS), BF16),
            pltpu.VMEM((OWN, 1), F32),
            pltpu.SemaphoreType.DMA((6,)),
        ],
        compiler_params=params(52),
        cost_estimate=cost(2 * 256 * 2048 * 256, 4 << 20),
        name="weight_parts",
    )(mine, theirs, slopes_rows, keep, swapped, hidden, own_degree)


RETURN_ROWS = 112


def return_kernel(
    back_hbm, recv_hbm, hubs_hbm, out_hbm,
    back_ref, part_ref, recv_ref, hubs_ref, out_ref, in_sems, out_sems,
):
    staged = copies(
        in_sems,
        (recv_hbm, recv_ref),
        (hubs_hbm, hubs_ref),
        (back_hbm.at[:, :OWN, :], back_ref),
        (back_hbm.at[:, 96:, :], part_ref),
    )
    node = lax.broadcasted_iota(jnp.int32, (NODES, 2 * SLOTS), 0)
    staged[2].wait()
    share = back_ref[...].astype(F32).reshape(NODES, SLOTS).T[FEATS:, :].astype(BF16)
    staged[0].wait()
    staged[3].wait()
    sums = jnp.sum(part_ref[...].astype(F32), axis=0).astype(BF16)
    sent = []
    for pair in range(PEERS // 2):
        values = matmul(share, one_hot(node == pair_lanes(recv_ref, pair)), NN).astype(BF16)
        for side in range(2):
            peer = 2 * pair + side
            out_ref[peer, :FEATS, :] = values[:, SLOTS * side : SLOTS * (side + 1)]
            out_ref[peer, ROWS:, :] = sums
        if pair == 3:
            staged[1].wait()
            terms = matmul(share, hubs_ref[...], NT).T
            high = terms.astype(BF16).astype(F32)
            both = jnp.concatenate([high, terms - high], axis=1)
            out_ref[:, FEATS:ROWS, :] = both.reshape(PEERS, HUBS_OWN, SLOTS).astype(BF16)
        if pair % 4 == 3:
            part = pl.ds(2 * pair - 6, 8)
            copy = pltpu.make_async_copy(out_ref.at[part], out_hbm.at[part], out_sems.at[pair // 4])
            copy.start()
            sent.append(copy)
    for copy in sent:
        copy.wait()


def return_slots(back_block, recv_lanes, hubs):
    return pl.pallas_call(
        return_kernel,
        in_specs=[HBM, HBM, HBM],
        out_specs=HBM,
        out_shape=jax.ShapeDtypeStruct((PEERS, RETURN_ROWS, SLOTS), BF16),
        scratch_shapes=[
            pltpu.VMEM((LAYERS, OWN, SLOTS), BF16),
            pltpu.VMEM((LAYERS, 32, SLOTS), BF16),
            pltpu.VMEM((PEERS, SLOTS), jnp.int32),
            pltpu.VMEM((HUBS, NODES), BF16),
            pltpu.VMEM((PEERS, RETURN_ROWS, SLOTS), BF16),
            pltpu.SemaphoreType.DMA((4,)),
            pltpu.SemaphoreType.DMA((4,)),
        ],
        compiler_params=params(53),
        cost_estimate=cost(2 * 256 * 4608 * 1024, 3 << 20),
        name="return_slots",
    )(back_block, recv_lanes, hubs)


def local_kernel(back_ref, local_ref, base_hbm, hidden_ref, base_ref, sems):
    columns = back_ref[:, :OWN, :].astype(F32).reshape(NODES, SLOTS).T
    share = columns[FEATS:, :].astype(BF16)
    base_ref[...] = columns[:FEATS, :] + matmul(share, local_ref[...], NT)
    (sent,) = copies(sems, (base_ref, base_hbm.at[:FEATS]))
    folded = back_ref[:, OWN:96, :].astype(F32)
    rows = jnp.concatenate([folded[:, :, :FEATS], folded[:, :, FEATS:]], axis=1)
    hidden_ref[...] = rows.reshape(NODES, FEATS).T.astype(BF16)
    sent.wait()


def local_grads(back_block, local):
    return pl.pallas_call(
        local_kernel,
        out_specs=[HBM, VMEM],
        out_shape=[
            jax.ShapeDtypeStruct((KEPT, NODES), F32),
            jax.ShapeDtypeStruct((FEATS, NODES), BF16),
        ],
        scratch_shapes=[pltpu.VMEM((FEATS, NODES), F32), pltpu.SemaphoreType.DMA((1,))],
        compiler_params=params(60),
        cost_estimate=cost(2 * 256 * 1024 * 1024, 3 << 20),
        name="local_grads",
    )(back_block, local)


SPREAD = 256


def spread_kernel(
    back_ref, send_hbm, hub_hbm, base_hbm, out_ref, self_hbm, neigh_hbm,
    send_ref, hub_ref, base_ref, grads_ref, slots, in_sems, out_sems,
):
    staged = copies(in_sems, (send_hbm, send_ref), (hub_hbm, hub_ref), (base_hbm.at[:FEATS], base_ref))
    for peer in range(PEERS):
        slots[:, SLOTS * peer : SLOTS * (peer + 1)] = back_ref[peer, :FEATS, :]
    sums = jnp.sum(back_ref[:, FEATS:ROWS, :].astype(F32), axis=0)
    total = sums[:, :FEATS] + sums[:, FEATS:]
    high = total.astype(BF16).astype(F32)
    hub_high = high.T.astype(BF16)
    hub_low = (total - high).T.astype(BF16)
    staged[0].wait()
    staged[1].wait()
    for tile in range(NODES // SPREAD):
        lanes = slice(SPREAD * tile, SPREAD * (tile + 1))
        node = lax.broadcasted_iota(jnp.int32, (SPREAD, 2 * SLOTS), 0) + SPREAD * tile
        grad = jnp.zeros((FEATS, SPREAD), F32)
        for pair in range(PEERS // 2):
            grad = grad + matmul(
                slots[:, 2 * SLOTS * pair : 2 * SLOTS * (pair + 1)],
                one_hot(node == pair_lanes(send_ref, pair)),
                NT,
            )
        hub_node = lax.broadcasted_iota(jnp.int32, (SPREAD, HUBS_OWN), 0) + SPREAD * tile
        hub_hot = one_hot(hub_node == hub_ref[...])
        grad = grad + matmul(hub_high, hub_hot, NT) + matmul(hub_low, hub_hot, NT)
        if tile == 0:
            for peer in range(PEERS):
                slice_of, start = peer // 8, HALF * (peer % 2) + SLOTS * (peer // 2 % 4)
                grads_ref[
                    PIECE * slice_of : PIECE * (slice_of + 1), start : start + SLOTS
                ] = back_ref[peer, ROWS:, :].astype(F32)
            sent = copies(
                out_sems, (grads_ref.at[:FEATS], self_hbm), (grads_ref.at[FEATS:], neigh_hbm)
            )
            staged[2].wait()
        out_ref[:, lanes] = (grad + base_ref[:, lanes]).astype(BF16)
    for copy in sent:
        copy.wait()


def spread_grads(returned, send_lanes, hub_own, base):
    return pl.pallas_call(
        spread_kernel,
        in_specs=[VMEM, HBM, HBM, HBM],
        out_specs=[VMEM, HBM, HBM],
        out_shape=[
            jax.ShapeDtypeStruct((FEATS, NODES), BF16),
            jax.ShapeDtypeStruct((FEATS, OUTS), F32),
            jax.ShapeDtypeStruct((FEATS, OUTS), F32),
        ],
        scratch_shapes=[
            pltpu.VMEM((PEERS, SLOTS), jnp.int32),
            pltpu.VMEM((1, HUBS_OWN), jnp.int32),
            pltpu.VMEM((FEATS, NODES), F32),
            pltpu.VMEM((2 * FEATS, OUTS), F32),
            pltpu.VMEM((FEATS, PEERS * SLOTS), BF16),
            pltpu.SemaphoreType.DMA((3,)),
            pltpu.SemaphoreType.DMA((2,)),
        ],
        compiler_params=params(52),
        cost_estimate=cost(2 * 256 * 4224 * 1024, 2 << 20),
        name="spread_grads",
    )(returned, send_lanes, hub_own, base)


SAME_CORE = [list(range(core, PEERS, 2)) for core in range(2)]


def exchange(blocks, axis, groups=None):
    return lax.all_to_all(blocks, axis, 0, 0, axis_index_groups=groups, tiled=True)


def other_core(block):
    return lax.ppermute(block, "row", [(i, i ^ 1) for i in range(PEERS)])


def per_device(feats, w_self, w_neigh, cotangent, loc_nbr, send_rows, recv_node, hub_rows, hub_nbr):
    send_lanes = send_rows.reshape(PEERS, SLOTS)
    recv_lanes = recv_node.reshape(PEERS, SLOTS)
    hub_own = hub_rows[None, :]
    half = HALF * (lax.axis_index("row") % 2)
    weights = lax.all_gather(
        lax.dynamic_slice_in_dim(jnp.concatenate([w_self, w_neigh], axis=0), half, HALF, 1),
        "col",
        axis=0,
        tiled=True,
    )
    incoming = exchange(gather_slots(feats, send_lanes, hub_own), "row")
    hub_lanes = hub_nbr.T
    local, hubs, local_sum = build_counts(feats, loc_nbr.T, hub_lanes)
    outgoing, degree = aggregate(feats, incoming, recv_lanes, local_sum, hub_lanes, cotangent)
    node_block = exchange(outgoing, "col")
    own_degree = lax.dynamic_slice_in_dim(degree[0], OWN * lax.axis_index("col"), OWN)[:, None]
    joined_mine = exchange(regroup(node_block), "row", SAME_CORE)
    joined, cots = prepare(node_block, other_core(node_block))
    slopes_out, slopes, hidden = forward(joined, cots, weights)
    slopes_rows = exchange(slopes_out, "row", SAME_CORE)
    joined_mine, slopes = lax.optimization_barrier((joined_mine, slopes))
    joined_theirs = other_core(joined_mine)
    keep, sent = backward(slopes, hidden, weights)
    parts = weight_parts(
        joined_mine, joined_theirs, slopes_rows, keep, other_core(sent), hidden, own_degree
    )
    back_block = exchange(parts, "col")
    returned = exchange(return_slots(back_block, recv_lanes, hubs), "row")
    base, hidden_out = local_grads(back_block, local)
    grad_feats, grad_self, grad_neigh = spread_grads(returned, send_lanes, hub_own, base)
    return (hidden_out, grad_feats, grad_self, grad_neigh)


def solution(mesh):
    return jax.shard_map(
        per_device,
        mesh=mesh,
        in_specs=(
            P("col", "row"),
            P("col", None),
            P("col", None),
            P("col", "row"),
            P("row", None),
            P("row", None, None),
            P("row", None, None),
            P("row"),
            P("row", None),
        ),
        out_specs=(P("col", "row"), P("col", "row"), P("col", None), P("col", None)),
        check_vma=False,
    )
```
